128 devices in a mesh: ctx: 32 (over x_lo, y, z), tp: 4 (over x_hi, core).
Axes of the slice: x: 4 (x_hi: 2, x_lo: 2; x = x_hi * 2 + x_lo), y: 4, z: 4, core: 2. Of those that a mesh axis runs over, the one named last changes fastest.
Arguments:
- queries: bfloat16 [32768, 2048], P('ctx', 'tp'), may hold values from -24 to 24
- keys: bfloat16 [32768, 2048], P('ctx', 'tp'), may hold values from -4 to 4
- values: bfloat16 [32768, 2048], P('ctx', 'tp'), may hold values from -6 to 6
- out_weight: bfloat16 [2048, 4096], P('tp'), may hold values from -0.125 to 0.125
- out_grad: bfloat16 [32768, 4096], P('ctx', 'tp'), may hold values from -6 to 6
- spans: int32 [64, 2], replicated, may hold values from 0 to 64, as said below
- pairs: int32 [192, 2], replicated, may hold values from 0 to 63, as said below
Outputs:
- mixed: bfloat16 [32768, 4096], P('ctx', 'tp')
- query_grad: bfloat16 [32768, 2048], P('ctx', 'tp')
- key_grad: bfloat16 [32768, 2048], P('ctx', 'tp')
- value_grad: bfloat16 [32768, 2048], P('ctx', 'tp')
- weight_grad: float32 [2048, 4096], P('tp', 'ctx')
The draws below stay inside these ranges and needn't reach their ends.
Inputs may be any that keep to these rules, and one draw needn't show every extreme that they name: `spans`: recordings do not intersect and lie in order; an empty slot has 0 blocks; some recording has exactly 8 blocks, none more; unused slots start at 64. `pairs`: every listed pair (a, b) has 0 <= a - b < 4; each block a appears in exactly three rows as query block, one of them (a, a); rows may repeat and come in any order.
All inputs are finite; a program needn't handle non-finite values.
Results may differ from the reference program's by a relative error of at most 0.017.
Values may be sent and summed in bfloat16 or wider, within the bound.
No kernel may reach another device: no remote copies, remote signals or barrier semaphores. Data moves between devices by JAX's collectives and lax.ppermute only.
A program may use at most 256 MiB of HBM per device.

```python
import math
import jax
import jax.numpy as jnp
from jax import lax

D = 4096
HEADS = 16
HDIM = 128
BLK = 512
WIN = 4
SPAN_MAX = 8
NB = 64
FRAMES = 32768
FEAT = 2048
REC = 64
NPAIR = 192


def shared_rows(key):
    drawn = jnp.clip(jax.random.normal(key, (FRAMES, FEAT), jnp.float32), -4.0, 4.0)
    return drawn


def draw_keys(key, part):
    drawn = shared_rows(key)
    return drawn.astype(jnp.bfloat16)


def draw_queries(key, part):
    key = jax.random.fold_in(key, 2)
    return jnp.clip(jax.random.normal(key, (FRAMES, FEAT), jnp.float32), -4.0, 4.0).astype(jnp.bfloat16)


def draw_spans(key, part):
    key = jax.random.fold_in(key, 3)
    first_key, second_key = jax.random.split(key)
    lengths = jax.random.randint(first_key, (REC,), 1, SPAN_MAX + 1)
    lengths = lengths.at[0].set(SPAN_MAX)
    gap_sizes = jax.random.randint(second_key, (REC,), 0, 2)
    ends = jnp.cumsum(lengths + gap_sizes)
    starts = jnp.minimum(ends - lengths, NB)
    lengths = jnp.maximum(jnp.minimum(lengths, NB - starts), 0)
    return jnp.stack([starts, lengths], axis=1).astype(jnp.int32)


def draw_pairs(key, part):
    key = jax.random.fold_in(key, 5)
    first_key, second_key = jax.random.split(key)
    query_block = jnp.arange(NB, dtype=jnp.int32)
    offsets = jax.random.randint(first_key, (NB, 2), 1, WIN)
    key_block = jnp.maximum(query_block[:, None] - offsets, 0)
    diagonal = jnp.stack([query_block, query_block], axis=1)
    first_off = jnp.stack([query_block, key_block[:, 0]], axis=1)
    second_off = jnp.stack([query_block, key_block[:, 1]], axis=1)
    listing = jnp.concatenate([diagonal, first_off, second_off], axis=0)
    order = jax.random.permutation(second_key, NPAIR)
    return listing[order].astype(jnp.int32)


def raised(result, rng, source, target, parts, factor):
    def block_of(dim):
        return (jnp.arange(result.shape[dim]) // (result.shape[dim] // parts)).reshape((-1,) + (1,) * (result.ndim - 1 - dim))

    first = jax.random.permutation(rng, parts)[block_of(target)]
    second = (block_of(target) + parts // 2) % parts
    return jnp.where((block_of(source) == first) | (block_of(source) == second), factor * result, result)


def block_levels(key, extent, shards, low, top_value):
    gain, own = 1.0, jax.random.fold_in(key, 6)
    for dim, parts in shards:
        draws = jnp.exp(jax.random.uniform(jax.random.fold_in(own, dim), (parts,), jnp.float32, low / len(shards), top_value / len(shards)))
        gain = gain * jnp.repeat(draws, extent[dim] // parts).reshape([-1 if axis == dim else 1 for axis in range(len(extent))])
    return gain


def gaussian(stream_key, shape, spread, limit, shards=(), kind=jnp.bfloat16):
    factor_of = block_levels(stream_key, shape, shards, -0.22, 0.18) if shards else 1.0
    result = jax.random.normal(stream_key, shape, jnp.float32) * spread * factor_of
    return jnp.minimum(jnp.maximum(result, -limit), limit).astype(kind)


def heavy_noise(key, dims, deviation, most, shards, heavy, kind=jnp.bfloat16):
    entries = deviation * jax.random.normal(key, dims, jnp.float32)
    if shards:
        entries = entries * block_levels(key, dims, shards, -0.22, 0.18)
    return jnp.clip(raised(entries, jax.random.fold_in(key, 3), *heavy), -most, most).astype(kind)


def setup_inputs(seed: int = 0) -> dict:
    streams_of = jax.random.split(jax.random.key(seed), 8)
    return {
        "queries": draw_queries(jax.random.fold_in(streams_of[7], 71), 0),
        "keys": draw_keys(jax.random.fold_in(streams_of[7], 71), 0),
        "values": gaussian(streams_of[2], (FRAMES, FEAT), 1.0, 6.0, ((0, 32), (1, 4))),
        "out_weight": gaussian(streams_of[3], (FEAT, D), FEAT ** -0.5, 0.125, ((0, 4),)),
        "out_grad": heavy_noise(streams_of[4], (FRAMES, D), 1.0, 6.0, ((0, 32), (1, 4)), (0, 1, 32, 2.75)),
        "spans": draw_spans(jax.random.fold_in(streams_of[7], 71), 0),
        "pairs": draw_pairs(jax.random.fold_in(streams_of[7], 71), 0),
    }


def block_rule(spans, pairs, query_block, key_block):
    listed = jnp.any((pairs[:, 0] == query_block[..., None]) & (pairs[:, 1] == key_block[..., None]), axis=-1)
    span_lower = spans[:, 0]
    span_upper = spans[:, 0] + spans[:, 1]
    query_inside = (span_lower <= query_block[..., None]) & (query_block[..., None] < span_upper)
    key_inside = (span_lower <= key_block[..., None]) & (key_block[..., None] < span_upper)
    same = jnp.any(query_inside & key_inside, axis=-1)
    reach = (query_block - key_block >= 0) & (query_block - key_block < WIN)
    return listed & same & reach

def block_weights(queries, keys_pad, values_pad, spans, pairs, group):
    scale = 1.0 / math.sqrt(HDIM)
    query_rows = lax.dynamic_slice_in_dim(queries, group * BLK, BLK, 0).astype(jnp.float32).reshape(BLK, HEADS, HDIM)
    key_rows = lax.dynamic_slice_in_dim(keys_pad, group * BLK, WIN * BLK, 0).astype(jnp.float32).reshape(WIN * BLK, HEADS, HDIM)
    value_rows = lax.dynamic_slice_in_dim(values_pad, group * BLK, WIN * BLK, 0).astype(jnp.float32).reshape(WIN * BLK, HEADS, HDIM)
    scores = jnp.einsum('thd,shd->hts', query_rows, key_rows) * scale
    columns = jnp.arange(WIN * BLK, dtype=jnp.int32)
    key_block = group - (WIN - 1) + columns // BLK
    block_fine = block_rule(spans, pairs, jnp.zeros_like(key_block) + group, key_block)
    key_pos = (group - (WIN - 1)) * BLK + columns
    query_pos = group * BLK + jnp.arange(BLK, dtype=jnp.int32)
    allowed = block_fine[None, :] & (key_pos[None, :] <= query_pos[:, None])
    masked = jnp.where(allowed[None], scores, -jnp.inf)
    row_max = lax.optimization_barrier(jnp.max(masked, axis=-1))
    has_any = jnp.any(allowed, axis=-1)
    row_max = jnp.where(has_any[None], row_max, 0.0)
    expo = jnp.where(allowed[None], jnp.exp(scores - row_max[..., None]), 0.0)
    total = lax.optimization_barrier(jnp.sum(expo, axis=-1))
    weights = expo / jnp.where(total > 0, total, 1.0)[..., None]
    return (weights, query_rows, key_rows, value_rows)

def reference(queries, keys, values, out_weight, out_grad, spans, pairs):
    scale = 1.0 / math.sqrt(HDIM)
    front = jnp.zeros(((WIN - 1) * BLK, FEAT), jnp.bfloat16)
    keys_pad = jnp.concatenate([front, keys], axis=0)
    values_pad = jnp.concatenate([front, values], axis=0)
    groups = jnp.arange(NB, dtype=jnp.int32)

    def forward(group):
        weights, query_rows, key_rows, value_rows = block_weights(queries, keys_pad, values_pad, spans, pairs, group)
        weights_low = lax.optimization_barrier(weights.astype(jnp.bfloat16)).astype(jnp.float32)
        out_rows = jnp.einsum('hts,shd->thd', weights_low, value_rows)
        return out_rows.reshape(BLK, FEAT).astype(jnp.bfloat16)
    attention = lax.map(forward, groups).reshape(FRAMES, FEAT)
    mixed = jnp.dot(attention, out_weight, preferred_element_type=jnp.float32).astype(jnp.bfloat16)
    attn_grad = jnp.dot(out_grad, out_weight.T, preferred_element_type=jnp.float32).astype(jnp.bfloat16)
    weight_grad = jnp.dot(attention.T, out_grad, preferred_element_type=jnp.float32)

    def backward(carry, group):
        key_acc, value_acc = carry
        weights, query_rows, key_rows, value_rows = block_weights(queries, keys_pad, values_pad, spans, pairs, group)
        weights_low = lax.optimization_barrier(weights.astype(jnp.bfloat16)).astype(jnp.float32)
        grad_rows = lax.dynamic_slice_in_dim(attn_grad, group * BLK, BLK, 0).astype(jnp.float32).reshape(BLK, HEADS, HDIM)
        attn_rows = lax.dynamic_slice_in_dim(attention, group * BLK, BLK, 0).astype(jnp.float32).reshape(BLK, HEADS, HDIM)
        delta = jnp.einsum('thd,thd->ht', grad_rows, attn_rows)
        weights_grad = jnp.einsum('thd,shd->hts', grad_rows, value_rows)
        score_grad = weights * (weights_grad - delta[..., None])
        score_grad = lax.optimization_barrier(score_grad.astype(jnp.bfloat16)).astype(jnp.float32)
        query_part = (jnp.einsum('hts,shd->thd', score_grad, key_rows) * scale).reshape(BLK, FEAT).astype(jnp.bfloat16)
        key_part = (jnp.einsum('hts,thd->shd', score_grad, query_rows) * scale).reshape(WIN * BLK, FEAT)
        value_part = jnp.einsum('hts,thd->shd', weights_low, grad_rows).reshape(WIN * BLK, FEAT)
        start = group * BLK
        key_acc = lax.dynamic_update_slice_in_dim(key_acc, lax.dynamic_slice_in_dim(key_acc, start, WIN * BLK, 0) + key_part, start, 0)
        value_acc = lax.dynamic_update_slice_in_dim(value_acc, lax.dynamic_slice_in_dim(value_acc, start, WIN * BLK, 0) + value_part, start, 0)
        return ((key_acc, value_acc), query_part)
    empty = jnp.zeros(((NB + WIN - 1) * BLK, FEAT), jnp.float32)
    (key_acc, value_acc), query_parts = lax.scan(backward, (empty, empty), groups)
    query_grad = query_parts.reshape(FRAMES, FEAT)
    key_grad = key_acc[(WIN - 1) * BLK:].astype(jnp.bfloat16)
    value_grad = value_acc[(WIN - 1) * BLK:].astype(jnp.bfloat16)
    return (mixed, query_grad, key_grad, value_grad, weight_grad)
```

```python
import functools
import math

import jax
import jax.numpy as jnp
from jax import lax
from jax.experimental import pallas as pl
from jax.experimental.pallas import tpu as pltpu
from jax.sharding import PartitionSpec as P

HDIM = 128
BLK = 512
WIN = 4
SCALE = 1.0 / math.sqrt(HDIM)
SCALE2 = SCALE * math.log2(math.e)
AXES = ("ctx", "tp")
NT = (((1,), (1,)), ((), ()))
NN = (((1,), (0,)), ((), ()))
f32 = jnp.float32
bf16 = jnp.bfloat16


def places():
    for x_lo in range(2):
        for y in range(4):
            for z in range(4):
                for x_hi in range(2):
                    for core in range(2):
                        yield x_lo, y, z, x_hi, core


def number(x_lo, y, z, x_hi, core):
    return ((x_lo * 4 + y) * 4 + z) * 4 + x_hi * 2 + core


def move(value, target):
    pairs = [(number(*place), number(*target(*place))) for place in places()]
    return lax.ppermute(value, AXES, pairs)


def to_core(value):
    return move(value, lambda x_lo, y, z, x_hi, core: (x_lo, y, z, x_hi, 1 - core))


def to_x_hi(value):
    return move(value, lambda x_lo, y, z, x_hi, core: (x_lo, y, z, 1 - x_hi, core))


def to_x_lo(value):
    return move(value, lambda x_lo, y, z, x_hi, core: (1 - x_lo, y, z, x_hi, core))


def to_y(value, steps):
    return move(value, lambda x_lo, y, z, x_hi, core: (x_lo, (y + steps) % 4, z, x_hi, core))


def to_z(value, steps):
    return move(value, lambda x_lo, y, z, x_hi, core: (x_lo, y, (z + steps) % 4, x_hi, core))


def along_ctx(value, steps):
    pairs = [(s, s + steps) for s in range(32) if 0 <= s + steps < 32]
    return lax.ppermute(value, "ctx", pairs)


def two_along_ctx(value, sign):
    value = to_z(value, -sign)
    pairs = []
    for source in range(32):
        if 0 <= source + 2 * sign < 32:
            middle = source // 4 * 4 + (source % 4 - sign) % 4
            pairs.append((middle, source + 2 * sign))
    return lax.ppermute(value, "ctx", pairs)


def block_rule(spans, pairs, query_block, key_block):
    listed = jnp.any(
        (pairs[:, 0] == query_block[..., None]) & (pairs[:, 1] == key_block[..., None]), axis=-1
    )
    span_lower = spans[:, 0]
    span_upper = spans[:, 0] + spans[:, 1]
    query_inside = (span_lower <= query_block[..., None]) & (query_block[..., None] < span_upper)
    key_inside = (span_lower <= key_block[..., None]) & (key_block[..., None] < span_upper)
    same = jnp.any(query_inside & key_inside, axis=-1)
    reach = (query_block - key_block >= 0) & (query_block - key_block < WIN)
    return listed & same & reach


def dot(a, b, dims):
    return lax.dot_general(a, b, dims, preferred_element_type=f32)


def key_tile(index, far, near, own):
    if index == 0:
        return far[...]
    if index < 3:
        return near[pl.ds((index - 1) * BLK, BLK), :]
    return own[pl.ds((index - 3) * BLK, BLK), :]


def causal():
    key_row = lax.broadcasted_iota(jnp.int32, (BLK, BLK), 0)
    query_column = lax.broadcasted_iota(jnp.int32, (BLK, BLK), 1)
    return key_row <= query_column


def forward_kernel(
    flags, q_ref, k_ref, v_ref, k1_ref, v1_ref, k2_ref, v2_ref,
    out_ref, turned_ref, log_ref, top, total, acc,
):
    for qb in range(2):
        rows = pl.ds(qb * BLK, BLK)
        diagonal = flags[qb * WIN] == 1

        @pl.when(jnp.logical_not(diagonal))
        def _():
            out_ref[rows, :] = jnp.zeros((BLK, HDIM), bf16)
            turned_ref[:, rows] = jnp.zeros((HDIM, BLK), bf16)
            log_ref[0, qb : qb + 1, :] = jnp.zeros((1, BLK), f32)

        @pl.when(diagonal)
        def _():
            for o in range(WIN):

                def tile(o=o):
                    keys = key_tile(3 + qb - o, k2_ref, k1_ref, k_ref)
                    vals = key_tile(3 + qb - o, v2_ref, v1_ref, v_ref)
                    s = dot(keys, q_ref[rows, :], NT)
                    if o == 0:
                        s = jnp.where(causal(), s, -jnp.inf)
                        m = jnp.max(s, axis=0, keepdims=True)
                    else:
                        m = jnp.maximum(top[...], jnp.max(s, axis=0, keepdims=True))
                    p = jnp.exp2(s * SCALE2 - m * SCALE2)
                    row_sum = jnp.sum(p, axis=0, keepdims=True)
                    part = dot(vals.T, p.astype(bf16), NN)
                    if o == 0:
                        total[...] = row_sum
                        acc[...] = part
                    else:
                        fix = jnp.exp2((top[...] - m) * SCALE2)
                        total[...] = total[...] * fix + row_sum
                        acc[...] = acc[...] * fix + part
                    top[...] = m

                if o == 0:
                    tile()
                else:
                    pl.when(flags[qb * WIN + o] == 1)(tile)
            result = acc[...] * (1.0 / total[...])
            turned_ref[:, rows] = result.astype(bf16)
            out_ref[rows, :] = result.T.astype(bf16)
            log_ref[0, qb : qb + 1, :] = top[...] * SCALE2 + jnp.log2(total[...])


def backward_kernel(
    flags, q_ref, k_ref, v_ref, k1_ref, v1_ref, k2_ref, v2_ref, out_ref, grad_ref, log_ref,
    dq_ref, own_ref, near_ref, far_ref, dk, dv, dq,
):
    dk[...] = jnp.zeros_like(dk)
    dv[...] = jnp.zeros_like(dv)
    for qb in range(2):
        rows = pl.ds(qb * BLK, BLK)
        diagonal = flags[qb * WIN] == 1

        @pl.when(jnp.logical_not(diagonal))
        def _():
            dq_ref[rows, :] = jnp.zeros((BLK, HDIM), bf16)

        @pl.when(diagonal)
        def _():
            grad = grad_ref[rows, :]
            product = grad.astype(f32) * out_ref[rows, :].astype(f32)
            delta = jnp.sum(product.T, axis=0, keepdims=True)
            log_sum = log_ref[0, qb : qb + 1, :]
            for o in range(WIN):

                def tile(o=o):
                    index = 3 + qb - o
                    keys = key_tile(index, k2_ref, k1_ref, k_ref)
                    vals = key_tile(index, v2_ref, v1_ref, v_ref)
                    s = dot(keys, q_ref[rows, :], NT)
                    p = jnp.exp2(s * SCALE2 - log_sum)
                    if o == 0:
                        p = jnp.where(causal(), p, 0.0)
                    key_rows = pl.ds(index * BLK, BLK)
                    dv[key_rows, :] += dot(p.astype(bf16), grad, NN)
                    dp = dot(vals, grad, NT)
                    ds = (p * (dp - delta)).astype(bf16)
                    dk[key_rows, :] += dot(ds, q_ref[rows, :], NN)
                    part = dot(keys.T, ds, NN)
                    if o == 0:
                        dq[...] = part
                    else:
                        dq[...] += part

                if o == 0:
                    tile()
                else:
                    pl.when(flags[qb * WIN + o] == 1)(tile)
            dq_ref[rows, :] = (dq[...] * SCALE).T.astype(bf16)
    far_ref[0] = (dk[pl.ds(0, BLK), :] * SCALE).astype(bf16)
    far_ref[1] = dv[pl.ds(0, BLK), :].astype(bf16)
    near_ref[0] = (dk[pl.ds(BLK, 2 * BLK), :] * SCALE).astype(bf16)
    near_ref[1] = dv[pl.ds(BLK, 2 * BLK), :].astype(bf16)
    own_ref[0] = dk[pl.ds(3 * BLK, 2 * BLK), :] * SCALE
    own_ref[1] = dv[pl.ds(3 * BLK, 2 * BLK), :]


def head(rows):
    return pl.BlockSpec((rows, HDIM), lambda h, *_: (0, h))


def head_pair(rows):
    return pl.BlockSpec((2, rows, HDIM), lambda h, *_: (0, 0, h))


HEAD_LOG = pl.BlockSpec((1, 2, BLK), lambda h, *_: (h, 0, 0))


def shape(dims, dtype):
    return jax.ShapeDtypeStruct(dims, dtype)


def call(kernel, name, grid, ins, outs, out_shape, scratch, flops, args):
    return pl.pallas_call(
        kernel,
        grid_spec=pltpu.PrefetchScalarGridSpec(
            num_scalar_prefetch=1,
            grid=grid,
            in_specs=ins,
            out_specs=outs,
            scratch_shapes=scratch,
        ),
        out_shape=out_shape,
        compiler_params=pltpu.CompilerParams(vmem_limit_bytes=40 << 20),
        cost_estimate=pl.CostEstimate(flops=flops, bytes_accessed=16 << 20, transcendentals=0),
        name=name,
    )(*args)


def forward(flags, q, k, v, k1, v1, k2, v2):
    width = q.shape[1]
    heads = width // HDIM
    return call(
        forward_kernel, "attention_forward", (heads,),
        [head(1024)] * 5 + [head(512)] * 2,
        [head(1024), pl.BlockSpec((HDIM, 1024), lambda h, *_: (h, 0)), HEAD_LOG],
        [shape((1024, width), bf16), shape((width, 1024), bf16), shape((heads, 2, BLK), f32)],
        [pltpu.VMEM((1, BLK), f32), pltpu.VMEM((1, BLK), f32), pltpu.VMEM((HDIM, BLK), f32)],
        10**10, (flags, q, k, v, k1, v1, k2, v2),
    )


def backward(flags, q, k, v, k1, v1, k2, v2, out, grad, log_sum):
    width = q.shape[1]
    held = pltpu.VMEM((5 * BLK, HDIM), f32)
    return call(
        backward_kernel, "attention_backward", (width // HDIM,),
        [head(1024)] * 5 + [head(512)] * 2 + [head(1024)] * 2 + [HEAD_LOG],
        [head(1024), head_pair(1024), head_pair(1024), head_pair(512)],
        [
            shape((1024, width), bf16),
            shape((2, 1024, width), f32),
            shape((2, 1024, width), bf16),
            shape((2, 512, width), bf16),
        ],
        [held, held, pltpu.VMEM((HDIM, BLK), f32)],
        15 * 10**9, (flags, q, k, v, k1, v1, k2, v2, out, grad, log_sum),
    )


def grad_kernel(place, a_ref, b_ref, wa_ref, wb_ref, *rest):
    total = dot(a_ref[...], wa_ref[...], NT) + dot(b_ref[...], wb_ref[...], NT)
    if len(rest) == 2:
        total += rest[0][...]
    rest[-1][...] = total.astype(rest[-1].dtype)


def grad_terms(place, first, a, b, weight, before=None):
    tile = 256
    row = pl.BlockSpec((tile, 1024), lambda i, place: (i, 0))
    result = pl.BlockSpec((tile, 512), lambda i, place: (i, 0))

    def columns(flip):
        return pl.BlockSpec((512, 1024), lambda i, place: (0, place[0] ^ flip))

    ins = [row, row, columns(first), columns(first + 1)] + ([result] if before is not None else [])
    args = (place, a, b, weight, weight) + ((before,) if before is not None else ())
    dtype = bf16 if before is not None else f32
    return call(
        grad_kernel, "projection_backward", (1024 // tile,), ins, result,
        shape((1024, 512), dtype), [], 2 * 10**9, args,
    )


def weight_kernel(place, turned_ref, *refs):
    out_ref = refs[-1]
    for part in range(4):

        @pl.when(pl.program_id(0) == part)
        def _():
            out_ref[0, 0] = dot(turned_ref[...], refs[part][...], NN).astype(bf16)


def weight_terms(place, turned, cotangents):
    def piece(part):
        return pl.BlockSpec(
            (1024, 512),
            lambda i, half, place: (
                0, jnp.where(i == part, half, jnp.where(i < part, 0, 1)),
            ),
        )

    def target(i, half, place):
        owner = place[0] ^ i
        y = (owner % 2) * 2 + half
        return ((y - place[1] + 4) % 4, owner // 2, 0, 0)

    return call(
        weight_kernel, "weight_gradient", (4, 2),
        [pl.BlockSpec((512, 1024), lambda i, half, place: (0, 0))] + [piece(p) for p in range(4)],
        pl.BlockSpec((1, 1, 512, 512), target),
        shape((4, 2, 512, 512), bf16), [], 4 * 10**9, (place, turned, *cotangents),
    )


def mix_kernel(place, a_ref, w_ref, out_ref):
    out_ref[0] = dot(a_ref[...], w_ref[...], NN).astype(bf16)


def mix_terms(place, attention, weight, flip):
    return call(
        mix_kernel, "projection", (2, 2),
        [
            pl.BlockSpec((512, 512), lambda s, i, place: (i, 0)),
            pl.BlockSpec((512, 1024), lambda s, i, place: (0, place[0] ^ (2 - 2 * s + flip))),
        ],
        pl.BlockSpec((1, 512, 1024), lambda s, i, place: (s, i, 0)),
        shape((2, 1024, 1024), bf16), [], 2 * 10**9, (place, attention, weight),
    )


def per_device(queries, keys, values, out_weight, out_grad, spans, pairs):
    ctx = lax.axis_index("ctx")
    tp = lax.axis_index("tp")
    x_lo, y, z = ctx // 16, ctx // 4 % 4, ctx % 4
    place = jnp.stack([tp, y]).astype(jnp.int32)

    far_grad = to_x_hi(out_grad)
    near_keys = along_ctx(keys, 1)
    near_values = along_ctx(values, 1)
    far_keys = two_along_ctx(keys[BLK:], 1)
    far_values = two_along_ctx(values[BLK:], 1)
    core_grad = to_core(out_grad)

    query_block = ctx * 2 + jnp.arange(2, dtype=jnp.int32)[:, None] + jnp.zeros((1, WIN), jnp.int32)
    key_block = query_block - jnp.arange(WIN, dtype=jnp.int32)[None, :]
    flags = block_rule(spans, pairs, query_block, key_block).astype(jnp.int32).reshape(-1)

    terms = grad_terms(place, 0, out_grad, core_grad, out_weight)
    tiles = (flags, queries, keys, values, near_keys, near_values, far_keys, far_values)
    attention, turned, log_sum = forward(*tiles)
    far_core_grad = to_core(far_grad)
    attn_grad = grad_terms(place, 2, far_grad, far_core_grad, out_weight, terms)

    weight_parts = weight_terms(place, turned, (out_grad, core_grad, far_grad, far_core_grad))
    weight_one = to_y(weight_parts[1], 1)
    weight_three = to_y(weight_parts[3], 3)
    weight_two = to_y(weight_parts[2], 2)

    mix_core = to_core(mix_terms(place, attention, out_weight, 1))
    mix_own = mix_terms(place, attention, out_weight, 0)
    mix_far = to_x_hi((mix_own[0].astype(f32) + mix_core[0].astype(f32)).astype(bf16))

    query_grad, own, near, far = backward(*tiles, attention, attn_grad, log_sum)
    far_back = two_along_ctx(far, -1)
    near_back = along_ctx(near, -1)

    mixed = (
        mix_own[1].astype(f32) + mix_core[1].astype(f32) + mix_far.astype(f32)
    ).astype(bf16)

    weight_sum = (
        weight_parts[0].astype(f32)
        + weight_one.astype(f32)
        + weight_two.astype(f32)
        + weight_three.astype(f32)
    ).astype(bf16)

    def z_piece(steps):
        return lax.dynamic_slice_in_dim(weight_sum, (z + steps) % 4 * 128, 128, 2)

    z_sum = z_piece(0).astype(f32)
    for steps in (1, 3, 2):
        z_sum = z_sum + to_z(z_piece(steps), steps).astype(f32)
    z_sum = z_sum.astype(bf16)
    kept = lax.dynamic_index_in_dim(z_sum, x_lo, 0, keepdims=False)
    sent = lax.dynamic_index_in_dim(z_sum, 1 - x_lo, 0, keepdims=False)
    weight_grad = kept.astype(f32) + to_x_lo(sent).astype(f32)

    summed = own + near_back.astype(f32)
    summed = summed.at[:, BLK:].add(far_back.astype(f32))
    key_grad = summed[0].astype(bf16)
    value_grad = summed[1].astype(bf16)
    return (mixed, query_grad, key_grad, value_grad, weight_grad)


def solution(mesh):
    placed = (
        P("ctx", "tp"),
        P("ctx", "tp"),
        P("ctx", "tp"),
        P("tp", None),
        P("ctx", "tp"),
        P(),
        P(),
    )
    return jax.shard_map(
        per_device,
        mesh=mesh,
        in_specs=placed,
        out_specs=(P("ctx", "tp"), P("ctx", "tp"), P("ctx", "tp"), P("ctx", "tp"), P("tp", "ctx")),
        check_vma=False,
    )
```

```python
import functools
import math

import jax
import jax.numpy as jnp
from jax import lax
from jax.experimental import pallas as pl
from jax.experimental.pallas import tpu as pltpu
from jax.sharding import PartitionSpec as P

HDIM = 128
BLK = 512
WIN = 4
SCALE = 1.0 / math.sqrt(HDIM)
SCALE2 = SCALE * math.log2(math.e)
AXES = ("ctx", "tp")
NT = (((1,), (1,)), ((), ()))
NN = (((1,), (0,)), ((), ()))
f32 = jnp.float32
bf16 = jnp.bfloat16


def places():
    for x_lo in range(2):
        for y in range(4):
            for z in range(4):
                for x_hi in range(2):
                    for core in range(2):
                        yield x_lo, y, z, x_hi, core


def number(x_lo, y, z, x_hi, core):
    return ((x_lo * 4 + y) * 4 + z) * 4 + x_hi * 2 + core


def move(value, target):
    pairs = [(number(*place), number(*target(*place))) for place in places()]
    return lax.ppermute(value, AXES, pairs)


def to_core(value):
    return move(value, lambda x_lo, y, z, x_hi, core: (x_lo, y, z, x_hi, 1 - core))


def to_x_hi(value):
    return move(value, lambda x_lo, y, z, x_hi, core: (x_lo, y, z, 1 - x_hi, core))


def to_x_lo(value):
    return move(value, lambda x_lo, y, z, x_hi, core: (1 - x_lo, y, z, x_hi, core))


def to_z(value, steps):
    return move(value, lambda x_lo, y, z, x_hi, core: (x_lo, y, (z + steps) % 4, x_hi, core))


EDGE = 15


def along_ctx(value, steps, without=()):
    pairs = [(s, s + steps) for s in range(32) if 0 <= s + steps < 32 and s not in without]
    return lax.ppermute(value, "ctx", pairs)


def from_next_z(value, sign, without):
    pairs = []
    for source in range(32):
        if 0 <= source + 2 * sign < 32 and source != without:
            middle = source // 4 * 4 + (source % 4 - sign) % 4
            pairs.append((middle, source + 2 * sign))
    return lax.ppermute(value, "ctx", pairs)


def across(value, sources):
    return lax.ppermute(value, "ctx", [(s, (s + 16) % 32) for s in sources])


def gathered(value, sources, target):
    return [lax.ppermute(value, "ctx", [((s + 16) % 32, target)]) for s in sources]


def block_rule(spans, pairs, query_block, key_block):
    listed = jnp.any(
        (pairs[:, 0] == query_block[..., None]) & (pairs[:, 1] == key_block[..., None]), axis=-1
    )
    span_lower = spans[:, 0]
    span_upper = spans[:, 0] + spans[:, 1]
    query_inside = (span_lower <= query_block[..., None]) & (query_block[..., None] < span_upper)
    key_inside = (span_lower <= key_block[..., None]) & (key_block[..., None] < span_upper)
    same = jnp.any(query_inside & key_inside, axis=-1)
    reach = (query_block - key_block >= 0) & (query_block - key_block < WIN)
    return listed & same & reach


def dot(a, b, dims):
    return lax.dot_general(a, b, dims, preferred_element_type=f32)


def causal():
    key_row = lax.broadcasted_iota(jnp.int32, (BLK, BLK), 0)
    query_column = lax.broadcasted_iota(jnp.int32, (BLK, BLK), 1)
    return key_row <= query_column


def block_rows(index):
    return pl.ds(index * BLK, BLK)


OWN_TILES = ((0, 0, 0), (1, 0, 1), (1, 1, 0))
BEHIND_TILES = ((0, 3, 0), (0, 2, 1), (0, 1, 2), (1, 3, 1), (1, 2, 2))


def key_value(index, near_k, near_v, far, edge_v, edge_far):
    if index == 0:
        return far[0] + edge_far[0], far[1] + edge_far[1]
    rows = block_rows(index - 1)
    return near_k[rows, :], near_v[rows, :] + edge_v[index - 1]


def absorb(keys, vals, query, top, total, acc, rows):
    s = dot(keys, query, NT)
    old = top
    m = jnp.maximum(old, jnp.max(s, axis=0, keepdims=True))
    p = jnp.exp2(s * SCALE2 - m * SCALE2)
    fix = jnp.exp2((old - m) * SCALE2)
    part = dot(vals.T, p.astype(bf16), NN)
    acc[:, rows] = acc[:, rows] * fix + part
    return m, total * fix + jnp.sum(p, axis=0, keepdims=True)


def forward_own_kernel(flags, q_ref, k_ref, v_ref, after, acc, top, total):
    for qb, o, index in OWN_TILES:
        rows = block_rows(qb)
        line = slice(qb, qb + 1)

        def diagonal(rows=rows, line=line):
            s = jnp.where(causal(), dot(k_ref[rows, :], q_ref[rows, :], NT), -jnp.inf)
            m = jnp.max(s, axis=0, keepdims=True)
            p = jnp.exp2(s * SCALE2 - m * SCALE2)
            acc[:, rows] = dot(v_ref[rows, :].T, p.astype(bf16), NN)
            top[0, line, :] = m
            total[0, line, :] = jnp.sum(p, axis=0, keepdims=True)

        def nothing(rows=rows, line=line):
            acc[:, rows] = jnp.zeros((HDIM, BLK), f32)
            top[0, line, :] = jnp.zeros((1, BLK), f32)
            total[0, line, :] = jnp.ones((1, BLK), f32)

        def tile(rows=rows, line=line, index=index):
            held = block_rows(index)
            top[0, line, :], total[0, line, :] = absorb(
                k_ref[held, :], v_ref[held, :], q_ref[rows, :],
                top[0, line, :], total[0, line, :], acc, rows,
            )

        listed = flags[qb * WIN + o] == 1
        if o == 0:
            pl.when(listed)(diagonal)
            pl.when(jnp.logical_not(listed))(nothing)
        else:
            pl.when(listed)(tile)


def forward_behind_kernel(
    flags, q_ref, k1_ref, v1_ref, far_ref, e0, e1, acc_in, top_in, total_in,
    after, out_ref, turned_ref, log_ref, acc, top, total,
):
    acc[...] = acc_in[...]
    top[...] = top_in[0]
    total[...] = total_in[0]
    for qb, o, index in BEHIND_TILES:
        rows = block_rows(qb)
        line = slice(qb, qb + 1)

        @pl.when(flags[qb * WIN + o] == 1)
        def _(rows=rows, line=line, index=index):
            keys, vals = key_value(index, k1_ref, v1_ref, far_ref, e0, e1)
            top[line, :], total[line, :] = absorb(
                keys, vals, q_ref[rows, :], top[line, :], total[line, :], acc, rows
            )

    for qb in range(2):
        rows = block_rows(qb)
        result = acc[:, rows] * (1.0 / total[qb : qb + 1, :])
        turned_ref[:, rows] = result.astype(bf16)
        out_ref[rows, :] = result.T.astype(bf16)
    log_ref[0] = top[...] * SCALE2 + jnp.log2(total[...])


def tile_grads(keys, vals, query, grad, log_sum, delta, diagonal):
    p = jnp.exp2(dot(keys, query, NT) * SCALE2 - log_sum)
    if diagonal:
        p = jnp.where(causal(), p, 0.0)
    value_part = dot(p.astype(bf16), grad, NN)
    dp = dot(vals, grad, NT)
    ds = (p * (dp - delta)).astype(bf16)
    return dot(ds, query, NN), value_part, dot(keys.T, ds, NN)


def backward_behind_kernel(
    flags, q_ref, k1_ref, v1_ref, far_ref, e0, e1, out_ref, grad_ref, log_ref,
    after, near_back, far_back, dq, delta_ref, dk, dv,
):
    dk[...] = jnp.zeros_like(dk)
    dv[...] = jnp.zeros_like(dv)
    dq[...] = jnp.zeros_like(dq)
    product = grad_ref[...].astype(f32) * out_ref[...].astype(f32)
    delta = jnp.sum(product.T, axis=0, keepdims=True)
    for qb in range(2):
        delta_ref[0, qb : qb + 1, :] = delta[:, qb * BLK : (qb + 1) * BLK]
    for qb, o, index in BEHIND_TILES:
        rows = block_rows(qb)
        line = slice(qb, qb + 1)

        @pl.when(flags[qb * WIN + o] == 1)
        def _(rows=rows, line=line, index=index):
            keys, vals = key_value(index, k1_ref, v1_ref, far_ref, e0, e1)
            key_part, value_part, query_part = tile_grads(
                keys, vals, q_ref[rows, :], grad_ref[rows, :],
                log_ref[0, line, :], delta_ref[0, line, :], False,
            )
            dk[block_rows(index), :] += key_part
            dv[block_rows(index), :] += value_part
            dq[:, rows] += query_part

    far_back[0] = (dk[block_rows(0), :] * SCALE).astype(bf16)
    far_back[1] = dv[block_rows(0), :].astype(bf16)
    near_back[0] = (dk[pl.ds(BLK, 2 * BLK), :] * SCALE).astype(bf16)
    near_back[1] = dv[pl.ds(BLK, 2 * BLK), :].astype(bf16)


def backward_own_kernel(
    flags, q_ref, k_ref, v_ref, grad_ref, log_ref, dq_in, delta_ref, after,
    dq_ref, own_ref, dk, dv, dq,
):
    dk[...] = jnp.zeros_like(dk)
    dv[...] = jnp.zeros_like(dv)
    dq[...] = dq_in[...]
    for qb, o, index in OWN_TILES:
        rows = block_rows(qb)
        line = slice(qb, qb + 1)

        @pl.when(flags[qb * WIN + o] == 1)
        def _(rows=rows, line=line, index=index, o=o):
            held = block_rows(index)
            key_part, value_part, query_part = tile_grads(
                k_ref[held, :], v_ref[held, :], q_ref[rows, :], grad_ref[rows, :],
                log_ref[0, line, :], delta_ref[0, line, :], o == 0,
            )
            dk[held, :] += key_part
            dv[held, :] += value_part
            dq[:, rows] += query_part

    own_ref[0] = dk[...] * SCALE
    own_ref[1] = dv[...]
    dq_ref[...] = (dq[...] * SCALE).T.astype(bf16)


def finish_kernel(place, own_ref, near_ref, far_ref, after, key_ref, value_ref):
    for part, result in enumerate((key_ref, value_ref)):
        for block in range(2):
            rows = block_rows(block)
            total = own_ref[part, rows, :] + near_ref[part, rows, :].astype(f32)
            if block == 1:
                total += far_ref[part].astype(f32)
            result[rows, :] = total.astype(bf16)


def head(rows):
    return pl.BlockSpec((rows, HDIM), lambda h, *_: (0, h))


def head_pair(rows):
    return pl.BlockSpec((2, rows, HDIM), lambda h, *_: (0, 0, h))


HEAD_LINES = pl.BlockSpec((1, 2, BLK), lambda h, *_: (h, 0, 0))
ANY = pl.BlockSpec(memory_space=pl.ANY)
HEAD_TURNED = pl.BlockSpec((HDIM, 1024), lambda h, *_: (h, 0))


def shape(dims, dtype):
    return jax.ShapeDtypeStruct(dims, dtype)


WIDTH = 512
HEADS = WIDTH // HDIM
LINES = shape((HEADS, 2, BLK), f32)
TURNED = shape((WIDTH, 1024), f32)


def call(kernel, name, grid, ins, outs, out_shape, scratch, args):
    return pl.pallas_call(
        kernel,
        grid_spec=pltpu.PrefetchScalarGridSpec(
            num_scalar_prefetch=1,
            grid=grid,
            in_specs=ins,
            out_specs=outs,
            scratch_shapes=scratch,
        ),
        out_shape=out_shape,
        compiler_params=pltpu.CompilerParams(vmem_limit_bytes=64 << 20),
        cost_estimate=pl.CostEstimate(flops=1, bytes_accessed=1, transcendentals=0),
        name=name,
    )(*args)


def forward_own(flags, q, k, v, after):
    return call(
        forward_own_kernel, "forward_own", (HEADS,),
        [head(1024)] * 3 + [ANY],
        [HEAD_TURNED, HEAD_LINES, HEAD_LINES],
        [TURNED, LINES, LINES],
        [], (flags, q, k, v, after),
    )


def forward_behind(flags, q, near_k, near_v, far, edge, state, after):
    lines = pltpu.VMEM((2, BLK), f32)
    return call(
        forward_behind_kernel, "forward_behind", (HEADS,),
        [head(1024)] * 3 + [head_pair(512)] * 3
        + [HEAD_TURNED, HEAD_LINES, HEAD_LINES, ANY],
        [head(1024), HEAD_TURNED, HEAD_LINES],
        [shape((1024, WIDTH), bf16), shape((WIDTH, 1024), bf16), LINES],
        [pltpu.VMEM((HDIM, 1024), f32), lines, lines],
        (flags, q, near_k, near_v, far, *edge, *state, after),
    )


def backward_behind(flags, q, near_k, near_v, far, edge, out, grad, log_sum, after):
    held = pltpu.VMEM((3 * BLK, HDIM), f32)
    return call(
        backward_behind_kernel, "backward_behind", (HEADS,),
        [head(1024)] * 3 + [head_pair(512)] * 3
        + [head(1024), head(1024), HEAD_LINES, ANY],
        [head_pair(1024), head_pair(512), HEAD_TURNED, HEAD_LINES],
        [shape((2, 1024, WIDTH), bf16), shape((2, 512, WIDTH), bf16), TURNED, LINES],
        [held, held], (flags, q, near_k, near_v, far, *edge, out, grad, log_sum, after),
    )


def backward_own(flags, q, k, v, grad, log_sum, dq, delta, after):
    held = pltpu.VMEM((2 * BLK, HDIM), f32)
    return call(
        backward_own_kernel, "backward_own", (HEADS,),
        [head(1024)] * 4 + [HEAD_LINES, HEAD_TURNED, HEAD_LINES, ANY],
        [head(1024), head_pair(1024)],
        [shape((1024, WIDTH), bf16), shape((2, 1024, WIDTH), f32)],
        [held, held, pltpu.VMEM((HDIM, 1024), f32)],
        (flags, q, k, v, grad, log_sum, dq, delta, after),
    )


def finish(place, own, near, far, after):
    return call(
        finish_kernel, "key_value_sum", (HEADS,),
        [head_pair(1024)] * 2 + [head_pair(512), ANY],
        [head(1024), head(1024)],
        [shape((1024, WIDTH), bf16)] * 2,
        [], (place, own, near, far, after),
    )


def pack_kernel(flags, k_ref, v_ref, second_ref, crossing_ref):
    second_ref[0] = k_ref[block_rows(1), :]
    second_ref[1] = v_ref[block_rows(1), :]
    first = flags[0] == EDGE - 1
    for part in range(2):
        crossing_ref[part] = jnp.where(first, second_ref[part], v_ref[block_rows(part), :])


def pack(ctx, k, v):
    return call(
        pack_kernel, "halo_pack", (HEADS,), [head(1024)] * 2, [head_pair(512)] * 2,
        [shape((2, 512, WIDTH), bf16)] * 2, [], (ctx, k, v),
    )


def nothing_kernel(*refs):
    pass


def behind(value, *after):
    return pl.pallas_call(
        nothing_kernel,
        in_specs=[ANY] * (1 + len(after)),
        out_specs=ANY,
        out_shape=shape(value.shape, value.dtype),
        input_output_aliases={0: 0},
        compiler_params=pltpu.CompilerParams(vmem_limit_bytes=64 << 20),
        name="order",
    )(value, *after)


def grad_kernel(place, a_ref, b_ref, wa_ref, wb_ref, *rest):
    total = dot(a_ref[...], wa_ref[...], NT) + dot(b_ref[...], wb_ref[...], NT)
    if len(rest) == 3:
        total += rest[0][...]
    rest[-1][...] = total.astype(rest[-1].dtype)


def grad_terms(place, first, a, b, weight, before, after):
    tile = 256
    row = pl.BlockSpec((tile, 1024), lambda i, place: (i, 0))
    result = pl.BlockSpec((tile, 512), lambda i, place: (i, 0))

    def columns(flip):
        return pl.BlockSpec((512, 1024), lambda i, place: (0, place[0] ^ flip))

    more = [] if before is None else [before]
    return call(
        grad_kernel, "projection_backward", (1024 // tile,),
        [row, row, columns(first), columns(first + 1)] + [result] * len(more) + [ANY], result,
        shape((1024, 512), bf16 if more else f32), [], (place, a, b, weight, weight, *more, after),
    )


def weight_kernel(place, turned_ref, *refs):
    out_ref = refs[-1]
    for part in range(4):

        @pl.when(pl.program_id(0) == part)
        def _(part=part):
            out_ref[0, 0] = dot(turned_ref[...], refs[part][...], NN).astype(bf16)


def weight_terms(place, turned, cotangents):
    def piece(part):
        return pl.BlockSpec(
            (1024, 512),
            lambda i, half, place: (
                0, jnp.where(i == part, half, jnp.where(i < part, 0, 1)),
            ),
        )

    def target(i, half, place):
        owner = place[0] ^ i
        return (owner % 2 * 2 + half, owner // 2, 0, 0)

    return call(
        weight_kernel, "weight_gradient", (4, 2),
        [pl.BlockSpec((512, 1024), lambda i, half, place: (0, 0))] + [piece(p) for p in range(4)],
        pl.BlockSpec((1, 1, 512, 512), target),
        shape((4, 2, 512, 512), bf16), [], (place, turned, *cotangents),
    )


def groups_along(axis):
    groups = {}
    for ctx in range(32):
        spot = [ctx // 16, ctx // 4 % 4, ctx % 4]
        spot[axis] = None
        groups.setdefault(tuple(spot), []).append(ctx)
    return list(groups.values())


def pieces_kernel(place, in_ref, after, *outs):
    for slot, out_ref in enumerate(outs):

        @pl.when(pl.program_id(0) == slot)
        def _(out_ref=out_ref):
            out_ref[...] = in_ref[...]


def pieces_by_z(place, total, after):
    return call(
        pieces_kernel, "weight_by_z", (4,),
        [pl.BlockSpec((2, 512, 128), lambda i, place: (0, 0, (place[2] + i + 1) % 4)), ANY],
        [pl.BlockSpec((2, 512, 128), lambda i, place: (0, 0, 0))] * 4,
        [shape((2, 512, 128), bf16)] * 4, [], (place, total, after),
    )


def weight_z_kernel(place, a_ref, b_ref, c_ref, d_ref, kept_ref, sent_ref):
    def total(index):
        return sum(ref[index].astype(f32) for ref in (a_ref, b_ref, c_ref, d_ref))

    kept_ref[...] = total(place[3])
    sent_ref[...] = total(1 - place[3]).astype(bf16)


def weight_z_sum(place, terms):
    whole = pl.BlockSpec((2, 512, 128), lambda i, place: (0, 0, 0))
    result = pl.BlockSpec((512, 128), lambda i, place: (0, 0))
    return call(
        weight_z_kernel, "weight_z_sum", (1,), [whole] * 4, [result] * 2,
        [shape((512, 128), f32), shape((512, 128), bf16)], [], (place, *terms),
    )


def copy_kernel(place, in_ref, *refs):
    refs[-1][...] = in_ref[...]


def far_columns(place, weight):
    return call(
        copy_kernel, "projection_quarter", (1,),
        [pl.BlockSpec((128, 2048), lambda i, place: (place[1], 1 - place[0] // 2))],
        pl.BlockSpec((128, 2048), lambda i, place: (0, 0)),
        shape((128, 2048), bf16), [], (place, weight),
    )


def two_kernel(place, a_ref, b_ref, after, a_out, b_out):
    a_out[...] = a_ref[...]
    b_out[...] = b_ref[...]


def late_copies(a, b, after):
    def rows(value):
        return pl.BlockSpec((256, value.shape[1]), lambda i, place: (i, 0))

    return call(
        two_kernel, "late_copies", (4,), [rows(a), rows(b), ANY], [rows(a), rows(b)],
        [shape(a.shape, a.dtype), shape(b.shape, b.dtype)],
        [], (jnp.zeros(1, jnp.int32), a, b, after),
    )


def core_kernel(place, own_ref, far_ref, after, out_ref):
    out_ref[0] = own_ref[...]
    out_ref[1] = far_ref[...]


def core_columns(place, weight, far_weight, after):
    return call(
        core_kernel, "projection_core", (1,),
        [
            pl.BlockSpec((512, 1024), lambda i, place: (0, place[0] ^ 1)),
            pl.BlockSpec((512, 1024), lambda i, place: (0, 1 - place[0] % 2)),
            ANY,
        ],
        pl.BlockSpec((2, 512, 1024), lambda i, place: (0, 0, 0)),
        shape((2, 512, 1024), bf16), [], (place, weight, far_weight, after),
    )


def mix_kernel(place, own, core, far, far_core, w_own, w_far, w_core, after, out_ref):
    total = dot(own[...], w_own[...], NN) + dot(core[...], w_core[0], NN)
    total += dot(far[...], w_far[...], NN) + dot(far_core[...], w_core[1], NN)
    out_ref[...] = total.astype(bf16)


def mix(place, attentions, weight, far_weight, core_weight, after):
    rows = pl.BlockSpec((256, 512), lambda i, place: (i, 0))
    return call(
        mix_kernel, "projection", (4,),
        [rows] * 4 + [
            pl.BlockSpec((512, 1024), lambda i, place: (0, place[0])),
            pl.BlockSpec((512, 1024), lambda i, place: (0, place[0] % 2)),
            pl.BlockSpec((2, 512, 1024), lambda i, place: (0, 0, 0)),
            ANY,
        ],
        pl.BlockSpec((256, 1024), lambda i, place: (i, 0)),
        shape((1024, 1024), bf16), [],
        (place, *attentions, weight, far_weight, core_weight, after),
    )


def per_device(queries, keys, values, out_weight, out_grad, spans, pairs):
    ctx = lax.axis_index("ctx")
    tp = lax.axis_index("tp")
    place = jnp.stack([tp, ctx // 4 % 4, ctx % 4, ctx // 16]).astype(jnp.int32)

    core_grad = to_core(out_grad)
    near_keys = along_ctx(keys, 1)
    second_half, crossing = pack(ctx.astype(jnp.int32).reshape(1), keys, values)
    far_moved = to_z(second_half, -1)
    crossed = across(crossing, (EDGE - 1, EDGE))
    far_weight = to_x_hi(far_columns(place, out_weight))

    query_block = ctx * 2 + jnp.arange(2, dtype=jnp.int32)[:, None] + jnp.zeros((1, WIN), jnp.int32)
    key_block = query_block - jnp.arange(WIN, dtype=jnp.int32)[None, :]
    listed = block_rule(spans, pairs, query_block, key_block).astype(jnp.int32).reshape(-1)
    flags = jnp.concatenate([listed, ctx.astype(jnp.int32).reshape(1)])
    own_state = forward_own(flags, queries, keys, values, crossing)
    held_values, held_grad = late_copies(values, out_grad, own_state[1])

    near_keys = behind(near_keys, held_grad)
    near_values = along_ctx(behind(held_values, near_keys), 1, (EDGE,))
    far = from_next_z(behind(far_moved, near_keys), 1, EDGE - 1)
    edge_far, edge_values = gathered(behind(crossed, near_keys), (EDGE - 1, EDGE), EDGE + 1)
    far_grad = to_x_hi(behind(held_grad, near_keys))
    far_weight = behind(far_weight, near_keys)
    terms = grad_terms(place, 0, out_grad, core_grad, out_weight, None, far_weight)
    far_weight = lax.all_gather(
        far_weight, "ctx", axis=0, tiled=True, axis_index_groups=groups_along(1)
    )
    keys_values = (flags, queries, near_keys, near_values, far, (edge_values, edge_far))
    attention, turned, log_sum = forward_behind(*keys_values, own_state, terms)
    far_grad = behind(far_grad, log_sum, far_weight)
    far_core_grad = to_core(far_grad)

    core_attention = to_core(attention)
    far_attention = to_x_hi(attention)
    weight_parts = weight_terms(place, turned, (out_grad, core_grad, far_grad, far_core_grad))
    weight_y = lax.psum_scatter(
        weight_parts, "ctx", scatter_dimension=0, axis_index_groups=groups_along(1)
    )
    attn_grad = grad_terms(place, 2, far_grad, far_core_grad, out_weight, terms, weight_parts)
    near_back, far_back, dq, delta = backward_behind(
        *keys_values, attention, attn_grad, log_sum, attn_grad
    )
    near_back = along_ctx(near_back, -1)
    far_moved = to_z(far_back, 1)
    far_attention = behind(far_attention, delta)
    far_core_attention = to_core(far_attention)
    query_grad, own = backward_own(
        flags, queries, keys, values, attn_grad, log_sum, dq, delta, delta
    )
    core_weight = to_core(core_columns(place, out_weight, far_weight, delta))
    attentions = (attention, core_attention, far_attention, far_core_attention)
    mixed = mix(place, attentions, out_weight, far_weight, core_weight, own)

    far_back = from_next_z(behind(far_moved, mixed), -1, None)
    weight_pieces = pieces_by_z(place, weight_y, mixed)
    kept, sent = weight_z_sum(
        place, [weight_pieces[3]] + [to_z(weight_pieces[s], s + 1) for s in (0, 2, 1)]
    )
    weight_grad = kept + to_x_lo(sent).astype(f32)
    key_grad, value_grad = finish(place, own, near_back, far_back, kept)
    return (mixed, query_grad, key_grad, value_grad, weight_grad)


def solution(mesh):
    placed = (
        P("ctx", "tp"),
        P("ctx", "tp"),
        P("ctx", "tp"),
        P("tp", None),
        P("ctx", "tp"),
        P(),
        P(),
    )
    return jax.shard_map(
        per_device,
        mesh=mesh,
        in_specs=placed,
        out_specs=(P("ctx", "tp"), P("ctx", "tp"), P("ctx", "tp"), P("ctx", "tp"), P("tp", "ctx")),
        check_vma=False,
    )
```

```python
import functools
import math

import jax
import jax.numpy as jnp
from jax import lax
from jax.experimental import pallas as pl
from jax.experimental.pallas import tpu as pltpu
from jax.sharding import PartitionSpec as P

HDIM = 128
BLK = 512
WIN = 4
SCALE = 1.0 / math.sqrt(HDIM)
SCALE2 = SCALE * math.log2(math.e)
AXES = ("ctx", "tp")
NT = (((1,), (1,)), ((), ()))
NN = (((1,), (0,)), ((), ()))
f32 = jnp.float32
bf16 = jnp.bfloat16


def places():
    for x_lo in range(2):
        for y in range(4):
            for z in range(4):
                for x_hi in range(2):
                    for core in range(2):
                        yield x_lo, y, z, x_hi, core


def number(x_lo, y, z, x_hi, core):
    return ((x_lo * 4 + y) * 4 + z) * 4 + x_hi * 2 + core


def move(value, target):
    pairs = [(number(*place), number(*target(*place))) for place in places()]
    return lax.ppermute(value, AXES, pairs)


def to_core(value):
    return move(value, lambda x_lo, y, z, x_hi, core: (x_lo, y, z, x_hi, 1 - core))


def to_x_hi(value):
    return move(value, lambda x_lo, y, z, x_hi, core: (x_lo, y, z, 1 - x_hi, core))


def to_x_lo(value):
    return move(value, lambda x_lo, y, z, x_hi, core: (1 - x_lo, y, z, x_hi, core))


def to_z(value, steps):
    return move(value, lambda x_lo, y, z, x_hi, core: (x_lo, y, (z + steps) % 4, x_hi, core))


EDGE = 15


def along_ctx(value, steps, without=()):
    pairs = [(s, s + steps) for s in range(32) if 0 <= s + steps < 32 and s not in without]
    return lax.ppermute(value, "ctx", pairs)


def middle(source, sign):
    place = source // 4 * 4 + (source % 4 - sign) % 4
    return place if source // 16 == (source + 2 * sign) // 16 else (place + 16) % 32


def two_pairs(sign):
    sources = [s for s in range(32) if 0 <= s + 2 * sign < 32]
    return [(s, middle(s, sign), s + 2 * sign) for s in sources]


def first_hop(value, sign):
    return lax.ppermute(value, "ctx", [(s, m) for s, m, _ in two_pairs(sign)])


def second_hop(value, sign):
    return lax.ppermute(value, "ctx", [(m, t) for _, m, t in two_pairs(sign)])


def block_rule(spans, pairs, query_block, key_block):
    listed = jnp.any(
        (pairs[:, 0] == query_block[..., None]) & (pairs[:, 1] == key_block[..., None]), axis=-1
    )
    span_lower = spans[:, 0]
    span_upper = spans[:, 0] + spans[:, 1]
    query_inside = (span_lower <= query_block[..., None]) & (query_block[..., None] < span_upper)
    key_inside = (span_lower <= key_block[..., None]) & (key_block[..., None] < span_upper)
    same = jnp.any(query_inside & key_inside, axis=-1)
    reach = (query_block - key_block >= 0) & (query_block - key_block < WIN)
    return listed & same & reach


def dot(a, b, dims):
    return lax.dot_general(a, b, dims, preferred_element_type=f32)


def causal():
    key_row = lax.broadcasted_iota(jnp.int32, (BLK, BLK), 0)
    query_column = lax.broadcasted_iota(jnp.int32, (BLK, BLK), 1)
    return key_row <= query_column


def block_rows(index):
    return pl.ds(index * BLK, BLK)


OWN_TILES = ((0, 0, 0), (1, 0, 1), (1, 1, 0))
BEHIND_TILES = ((0, 3, 0), (0, 2, 1), (0, 1, 2), (1, 3, 1), (1, 2, 2))


def key_value(index, near_k, near_v, edge_v, far):
    if index == 0:
        return far[0], far[1]
    rows = block_rows(index - 1)
    return near_k[rows, :], near_v[rows, :] + edge_v[rows, :]


def absorb(keys, vals, query, top, total, acc, rows):
    s = dot(keys, query, NT)
    old = top
    m = jnp.maximum(old, jnp.max(s, axis=0, keepdims=True))
    p = jnp.exp2(s * SCALE2 - m * SCALE2)
    fix = jnp.exp2((old - m) * SCALE2)
    part = dot(vals.T, p.astype(bf16), NN)
    acc[:, rows] = acc[:, rows] * fix + part
    return m, total * fix + jnp.sum(p, axis=0, keepdims=True)


def forward_own_kernel(flags, q_ref, k_ref, v_ref, after, acc, top, total):
    for qb, o, index in OWN_TILES:
        rows = block_rows(qb)
        line = slice(qb, qb + 1)

        def diagonal(rows=rows, line=line):
            s = jnp.where(causal(), dot(k_ref[rows, :], q_ref[rows, :], NT), -jnp.inf)
            m = jnp.max(s, axis=0, keepdims=True)
            p = jnp.exp2(s * SCALE2 - m * SCALE2)
            acc[:, rows] = dot(v_ref[rows, :].T, p.astype(bf16), NN)
            top[0, line, :] = m
            total[0, line, :] = jnp.sum(p, axis=0, keepdims=True)

        def nothing(rows=rows, line=line):
            acc[:, rows] = jnp.zeros((HDIM, BLK), f32)
            top[0, line, :] = jnp.zeros((1, BLK), f32)
            total[0, line, :] = jnp.ones((1, BLK), f32)

        def tile(rows=rows, line=line, index=index):
            held = block_rows(index)
            top[0, line, :], total[0, line, :] = absorb(
                k_ref[held, :], v_ref[held, :], q_ref[rows, :],
                top[0, line, :], total[0, line, :], acc, rows,
            )

        listed = flags[qb * WIN + o] == 1
        if o == 0:
            pl.when(listed)(diagonal)
            pl.when(jnp.logical_not(listed))(nothing)
        else:
            pl.when(listed)(tile)


def forward_behind_kernel(
    flags, q_ref, k1_ref, v1_ref, edge_ref, far_ref, acc_in, top_in, total_in,
    after, out_ref, turned_ref, log_ref, acc, top, total,
):
    acc[...] = acc_in[...]
    top[...] = top_in[0]
    total[...] = total_in[0]
    for qb, o, index in BEHIND_TILES:
        rows = block_rows(qb)
        line = slice(qb, qb + 1)

        @pl.when(flags[qb * WIN + o] == 1)
        def _(rows=rows, line=line, index=index):
            keys, vals = key_value(index, k1_ref, v1_ref, edge_ref, far_ref)
            top[line, :], total[line, :] = absorb(
                keys, vals, q_ref[rows, :], top[line, :], total[line, :], acc, rows
            )

    for qb in range(2):
        rows = block_rows(qb)
        result = acc[:, rows] * (1.0 / total[qb : qb + 1, :])
        turned_ref[:, rows] = result.astype(bf16)
        out_ref[rows, :] = result.T.astype(bf16)
    log_ref[0] = top[...] * SCALE2 + jnp.log2(total[...])


def tile_grads(keys, vals, query, grad, log_sum, delta, diagonal):
    p = jnp.exp2(dot(keys, query, NT) * SCALE2 - log_sum)
    if diagonal:
        p = jnp.where(causal(), p, 0.0)
    value_part = dot(p.astype(bf16), grad, NN)
    dp = dot(vals, grad, NT)
    ds = (p * (dp - delta)).astype(bf16)
    return dot(ds, query, NN), value_part, dot(keys.T, ds, NN)


def backward_behind_kernel(
    flags, q_ref, k1_ref, v1_ref, edge_ref, far_ref, out_ref, grad_ref, log_ref,
    after, near_back, far_back, dq, delta_ref, dk, dv,
):
    dk[...] = jnp.zeros_like(dk)
    dv[...] = jnp.zeros_like(dv)
    dq[...] = jnp.zeros_like(dq)
    product = grad_ref[...].astype(f32) * out_ref[...].astype(f32)
    delta = jnp.sum(product.T, axis=0, keepdims=True)
    for qb in range(2):
        delta_ref[0, qb : qb + 1, :] = delta[:, qb * BLK : (qb + 1) * BLK]
    for qb, o, index in BEHIND_TILES:
        rows = block_rows(qb)
        line = slice(qb, qb + 1)

        @pl.when(flags[qb * WIN + o] == 1)
        def _(rows=rows, line=line, index=index):
            keys, vals = key_value(index, k1_ref, v1_ref, edge_ref, far_ref)
            key_part, value_part, query_part = tile_grads(
                keys, vals, q_ref[rows, :], grad_ref[rows, :],
                log_ref[0, line, :], delta_ref[0, line, :], False,
            )
            dk[block_rows(index), :] += key_part
            dv[block_rows(index), :] += value_part
            dq[:, rows] += query_part

    far_back[0] = (dk[block_rows(0), :] * SCALE).astype(bf16)
    far_back[1] = dv[block_rows(0), :].astype(bf16)
    near_back[0] = (dk[pl.ds(BLK, 2 * BLK), :] * SCALE).astype(bf16)
    near_back[1] = dv[pl.ds(BLK, 2 * BLK), :].astype(bf16)


def backward_own_kernel(
    flags, q_ref, k_ref, v_ref, grad_ref, log_ref, dq_in, delta_ref, after,
    dq_ref, own_ref, dk, dv, dq,
):
    dk[...] = jnp.zeros_like(dk)
    dv[...] = jnp.zeros_like(dv)
    dq[...] = dq_in[...]
    for qb, o, index in OWN_TILES:
        rows = block_rows(qb)
        line = slice(qb, qb + 1)

        @pl.when(flags[qb * WIN + o] == 1)
        def _(rows=rows, line=line, index=index, o=o):
            held = block_rows(index)
            key_part, value_part, query_part = tile_grads(
                k_ref[held, :], v_ref[held, :], q_ref[rows, :], grad_ref[rows, :],
                log_ref[0, line, :], delta_ref[0, line, :], o == 0,
            )
            dk[held, :] += key_part
            dv[held, :] += value_part
            dq[:, rows] += query_part

    own_ref[0] = dk[...] * SCALE
    own_ref[1] = dv[...]
    dq_ref[...] = (dq[...] * SCALE).T.astype(bf16)


def finish_kernel(place, own_ref, near_ref, far_ref, after, key_ref, value_ref):
    for part, result in enumerate((key_ref, value_ref)):
        for block in range(2):
            rows = block_rows(block)
            total = own_ref[part, rows, :] + near_ref[part, rows, :].astype(f32)
            if block == 1:
                total += far_ref[part].astype(f32)
            result[rows, :] = total.astype(bf16)


def head(rows):
    return pl.BlockSpec((rows, HDIM), lambda h, *_: (0, h))


def head_pair(rows):
    return pl.BlockSpec((2, rows, HDIM), lambda h, *_: (0, 0, h))


HEAD_LINES = pl.BlockSpec((1, 2, BLK), lambda h, *_: (h, 0, 0))
ANY = pl.BlockSpec(memory_space=pl.ANY)
HEAD_TURNED = pl.BlockSpec((HDIM, 1024), lambda h, *_: (h, 0))


def shape(dims, dtype):
    return jax.ShapeDtypeStruct(dims, dtype)


WIDTH = 512
HEADS = WIDTH // HDIM
LINES = shape((HEADS, 2, BLK), f32)
TURNED = shape((WIDTH, 1024), f32)


def call(kernel, name, grid, ins, outs, out_shape, scratch, args):
    return pl.pallas_call(
        kernel,
        grid_spec=pltpu.PrefetchScalarGridSpec(
            num_scalar_prefetch=1,
            grid=grid,
            in_specs=ins,
            out_specs=outs,
            scratch_shapes=scratch,
        ),
        out_shape=out_shape,
        compiler_params=pltpu.CompilerParams(vmem_limit_bytes=64 << 20),
        cost_estimate=pl.CostEstimate(flops=1, bytes_accessed=1, transcendentals=0),
        name=name,
    )(*args)


def forward_own(flags, q, k, v, after):
    return call(
        forward_own_kernel, "forward_own", (HEADS,),
        [head(1024)] * 3 + [ANY],
        [HEAD_TURNED, HEAD_LINES, HEAD_LINES],
        [TURNED, LINES, LINES],
        [], (flags, q, k, v, after),
    )


def forward_behind(flags, q, near_k, near_v, edge_v, far, state, after):
    lines = pltpu.VMEM((2, BLK), f32)
    return call(
        forward_behind_kernel, "forward_behind", (HEADS,),
        [head(1024)] * 4 + [head_pair(512)]
        + [HEAD_TURNED, HEAD_LINES, HEAD_LINES, ANY],
        [head(1024), HEAD_TURNED, HEAD_LINES],
        [shape((1024, WIDTH), bf16), shape((WIDTH, 1024), bf16), LINES],
        [pltpu.VMEM((HDIM, 1024), f32), lines, lines],
        (flags, q, near_k, near_v, edge_v, far, *state, after),
    )


def backward_behind(flags, q, near_k, near_v, edge_v, far, out, grad, log_sum, after):
    held = pltpu.VMEM((3 * BLK, HDIM), f32)
    return call(
        backward_behind_kernel, "backward_behind", (HEADS,),
        [head(1024)] * 4 + [head_pair(512)]
        + [head(1024), head(1024), HEAD_LINES, ANY],
        [head_pair(1024), head_pair(512), HEAD_TURNED, HEAD_LINES],
        [shape((2, 1024, WIDTH), bf16), shape((2, 512, WIDTH), bf16), TURNED, LINES],
        [held, held], (flags, q, near_k, near_v, edge_v, far, out, grad, log_sum, after),
    )


def backward_own(flags, q, k, v, grad, log_sum, dq, delta, after):
    held = pltpu.VMEM((2 * BLK, HDIM), f32)
    return call(
        backward_own_kernel, "backward_own", (HEADS,),
        [head(1024)] * 4 + [HEAD_LINES, HEAD_TURNED, HEAD_LINES, ANY],
        [head(1024), head_pair(1024)],
        [shape((1024, WIDTH), bf16), shape((2, 1024, WIDTH), f32)],
        [held, held, pltpu.VMEM((HDIM, 1024), f32)],
        (flags, q, k, v, grad, log_sum, dq, delta, after),
    )


def finish(place, own, near, far, after):
    return call(
        finish_kernel, "key_value_sum", (HEADS,),
        [head_pair(1024)] * 2 + [head_pair(512), ANY],
        [head(1024), head(1024)],
        [shape((1024, WIDTH), bf16)] * 2,
        [], (place, own, near, far, after),
    )


def pack_kernel(place, k_ref, v_ref, second_ref):
    second_ref[0] = k_ref[...]
    second_ref[1] = v_ref[...]


def pack(place, k, v):
    second = pl.BlockSpec((BLK, WIDTH), lambda i, place: (1, 0))
    return call(
        pack_kernel, "second_blocks", (1,), [second, second],
        pl.BlockSpec((2, BLK, WIDTH), lambda i, place: (0, 0, 0)),
        shape((2, BLK, WIDTH), bf16), [], (place, k, v),
    )


def nothing_kernel(*refs):
    pass


def together(values, after=()):
    return pl.pallas_call(
        nothing_kernel,
        in_specs=[ANY] * (len(values) + len(after)),
        out_specs=[ANY] * len(values),
        out_shape=[shape(value.shape, value.dtype) for value in values],
        input_output_aliases={index: index for index in range(len(values))},
        compiler_params=pltpu.CompilerParams(vmem_limit_bytes=64 << 20),
        name="order",
    )(*values, *after)


def grad_kernel(place, a_ref, b_ref, wa_ref, wb_ref, *rest):
    total = dot(a_ref[...], wa_ref[...], NT) + dot(b_ref[...], wb_ref[...], NT)
    if len(rest) == 3:
        total += rest[0][...]
    rest[-1][...] = total.astype(rest[-1].dtype)


def grad_terms(place, first, a, b, weight, before, after):
    tile = 512
    row = pl.BlockSpec((tile, 1024), lambda i, place: (i, 0))
    result = pl.BlockSpec((tile, 512), lambda i, place: (i, 0))

    def columns(flip):
        return pl.BlockSpec((512, 1024), lambda i, place: (0, place[0] ^ flip))

    more = [] if before is None else [before]
    return call(
        grad_kernel, "projection_backward", (1024 // tile,),
        [row, row, columns(first), columns(first + 1)] + [result] * len(more) + [ANY], result,
        shape((1024, 512), bf16 if more else f32), [], (place, a, b, weight, weight, *more, after),
    )


def weight_kernel(place, turned_ref, a_ref, b_ref, after, out_ref):
    for part, ref in enumerate((a_ref, b_ref)):

        @pl.when(pl.program_id(0) == part)
        def _(ref=ref):
            out_ref[0] = dot(turned_ref[...], ref[...], NN).astype(bf16)


def weight_terms(place, turned, a, b, after):
    return call(
        weight_kernel, "weight_gradient", (2, 2),
        [
            pl.BlockSpec((512, 1024), lambda i, half, place: (0, 0)),
            pl.BlockSpec((1024, 512), lambda i, half, place: (0, jnp.where(i == 0, half, 1))),
            pl.BlockSpec((1024, 512), lambda i, half, place: (0, jnp.where(i == 0, 0, half))),
            ANY,
        ],
        pl.BlockSpec((1, 512, 512), lambda i, half, place: ((place[0] ^ i) % 2 * 2 + half, 0, 0)),
        shape((4, 512, 512), bf16), [], (place, turned, a, b, after),
    )


def sum_over_y(parts):
    return lax.psum_scatter(
        parts, "ctx", scatter_dimension=0, axis_index_groups=groups_along(1)
    )


def groups_along(axis):
    groups = {}
    for ctx in range(32):
        spot = [ctx // 16, ctx // 4 % 4, ctx % 4]
        spot[axis] = None
        groups.setdefault(tuple(spot), []).append(ctx)
    return list(groups.values())


def pieces_kernel(place, a_ref, b_ref, after, *outs):
    for slot, out_ref in enumerate(outs):

        @pl.when(pl.program_id(0) == slot)
        def _(out_ref=out_ref):
            out_ref[0] = a_ref[...]
            out_ref[1] = b_ref[...]


def pieces_by_z(place, a, b, after):
    piece = pl.BlockSpec((512, 128), lambda i, place: (0, (place[2] + i + 1) % 4))
    return call(
        pieces_kernel, "weight_by_z", (4,), [piece, piece, ANY],
        [pl.BlockSpec((2, 512, 128), lambda i, place: (0, 0, 0))] * 4,
        [shape((2, 512, 128), bf16)] * 4, [], (place, a, b, after),
    )


def weight_z_kernel(place, a_ref, b_ref, c_ref, d_ref, after, kept_ref, sent_ref):
    def total(index):
        return sum(ref[index].astype(f32) for ref in (a_ref, b_ref, c_ref, d_ref))

    kept = place[3] ^ (place[0] // 2)
    kept_ref[...] = total(kept)
    sent_ref[...] = total(1 - kept).astype(bf16)


def weight_z_sum(place, terms, after):
    whole = pl.BlockSpec((2, 512, 128), lambda i, place: (0, 0, 0))
    result = pl.BlockSpec((512, 128), lambda i, place: (0, 0))
    return call(
        weight_z_kernel, "weight_z_sum", (1,), [whole] * 4 + [ANY], [result] * 2,
        [shape((512, 128), f32), shape((512, 128), bf16)], [], (place, *terms, after),
    )


def copy_kernel(place, in_ref, *refs):
    refs[-1][...] = in_ref[...]


def far_columns(place, weight):
    return call(
        copy_kernel, "projection_quarter", (1,),
        [pl.BlockSpec((128, 2048), lambda i, place: (place[1], 1 - place[0] // 2))],
        pl.BlockSpec((128, 2048), lambda i, place: (0, 0)),
        shape((128, 2048), bf16), [], (place, weight),
    )


def two_kernel(place, a_ref, b_ref, after, a_out, b_out):
    a_out[...] = a_ref[...]
    b_out[...] = b_ref[...]


def late_copies(a, b, after):
    def rows(value):
        return pl.BlockSpec((512, value.shape[1]), lambda i, place: (i, 0))

    return call(
        two_kernel, "late_copies", (2,), [rows(a), rows(b), ANY], [rows(a), rows(b)],
        [shape(a.shape, a.dtype), shape(b.shape, b.dtype)],
        [], (jnp.zeros(1, jnp.int32), a, b, after),
    )


def core_kernel(place, own_ref, far_ref, after, out_ref):
    out_ref[0] = own_ref[...]
    out_ref[1] = far_ref[...]


def core_columns(place, weight, far_weight, after):
    return call(
        core_kernel, "projection_core", (1,),
        [
            pl.BlockSpec((512, 1024), lambda i, place: (0, place[0] ^ 1)),
            pl.BlockSpec((512, 1024), lambda i, place: (0, 1 - place[0] % 2)),
            ANY,
        ],
        pl.BlockSpec((2, 512, 1024), lambda i, place: (0, 0, 0)),
        shape((2, 512, 1024), bf16), [], (place, weight, far_weight, after),
    )


def mix_kernel(place, own, core, far, far_core, w_own, w_far, w_core, after, out_ref):
    total = dot(own[...], w_own[...], NN) + dot(core[...], w_core[0], NN)
    total += dot(far[...], w_far[...], NN) + dot(far_core[...], w_core[1], NN)
    out_ref[...] = total.astype(bf16)


def mix(place, attentions, weight, far_weight, core_weight, after):
    rows = pl.BlockSpec((512, 512), lambda i, place: (i, 0))
    return call(
        mix_kernel, "projection", (2,),
        [rows] * 4 + [
            pl.BlockSpec((512, 1024), lambda i, place: (0, place[0])),
            pl.BlockSpec((512, 1024), lambda i, place: (0, place[0] % 2)),
            pl.BlockSpec((2, 512, 1024), lambda i, place: (0, 0, 0)),
            ANY,
        ],
        pl.BlockSpec((512, 1024), lambda i, place: (i, 0)),
        shape((1024, 1024), bf16), [],
        (place, *attentions, weight, far_weight, core_weight, after),
    )


def per_device(queries, keys, values, out_weight, out_grad, spans, pairs):
    ctx = lax.axis_index("ctx")
    tp = lax.axis_index("tp")
    place = jnp.stack([tp, ctx // 4 % 4, ctx % 4, ctx // 16]).astype(jnp.int32)

    near_keys = along_ctx(keys, 1)
    crossed = lax.ppermute(values, "ctx", [(EDGE, EDGE + 16)])
    core_grad = to_core(out_grad)
    far_moved = first_hop(pack(place, keys, values), 1)
    far_weight = to_x_hi(far_columns(place, out_weight))

    query_block = ctx * 2 + jnp.arange(2, dtype=jnp.int32)[:, None] + jnp.zeros((1, WIN), jnp.int32)
    key_block = query_block - jnp.arange(WIN, dtype=jnp.int32)[None, :]
    flags = block_rule(spans, pairs, query_block, key_block).astype(jnp.int32).reshape(-1)
    own_state = forward_own(flags, queries, keys, values, keys)
    held_values, held_grad = late_copies(values, out_grad, own_state[1])

    near_keys, crossed, core_grad, far_moved, far_weight, held_values, held_grad = together(
        [near_keys, crossed, core_grad, far_moved, far_weight, held_values, held_grad]
    )
    near_values = along_ctx(held_values, 1, (EDGE,))
    edge_values = lax.ppermute(crossed, "ctx", [(EDGE + 16, EDGE + 1)])
    far = second_hop(far_moved, 1)
    far_grad = to_x_hi(held_grad)
    far_weight = lax.all_gather(
        far_weight, "ctx", axis=0, tiled=True, axis_index_groups=groups_along(1)
    )
    terms = grad_terms(place, 0, out_grad, core_grad, out_weight, None, near_keys)
    behind = (flags, queries, near_keys, near_values, edge_values, far)
    attention, turned, log_sum = forward_behind(*behind, own_state, terms)

    core_attention = to_core(attention)
    far_attention = to_x_hi(attention)
    own_parts = weight_terms(place, turned, out_grad, core_grad, log_sum)
    own_sum = sum_over_y(own_parts)
    far_grad, far_weight = together([far_grad, far_weight], [own_parts])
    far_core_grad = to_core(far_grad)
    core_weight = core_columns(place, out_weight, far_weight, own_parts)
    far_parts = weight_terms(place, turned, far_grad, far_core_grad, core_weight)
    far_sum = sum_over_y(far_parts)
    attn_grad = grad_terms(place, 2, far_grad, far_core_grad, out_weight, terms, far_parts)
    near_back, far_back, dq, delta = backward_behind(
        *behind, attention, attn_grad, log_sum, attn_grad
    )
    near_back = along_ctx(near_back, -1)
    far_moved = first_hop(far_back, -1)
    core_weight = to_core(core_weight)
    query_grad, own = backward_own(
        flags, queries, keys, values, attn_grad, log_sum, dq, delta, delta
    )
    core_attention, far_attention, core_weight, far_moved = together(
        [core_attention, far_attention, core_weight, far_moved], [own]
    )
    far_back = second_hop(far_moved, -1)
    far_core_attention = to_core(far_attention)
    attentions = (attention, core_attention, far_attention, far_core_attention)

    weight_pieces = pieces_by_z(place, own_sum, far_sum, far_attention)
    weight_terms_z = [weight_pieces[3]] + [to_z(weight_pieces[s], s + 1) for s in (0, 2, 1)]
    mixed = mix(place, attentions, out_weight, far_weight, core_weight, weight_pieces[3])
    kept, sent = weight_z_sum(place, weight_terms_z, mixed)
    weight_grad = kept + to_x_lo(sent).astype(f32)
    key_grad, value_grad = finish(place, own, near_back, far_back, kept)
    return (mixed, query_grad, key_grad, value_grad, weight_grad)


def solution(mesh):
    placed = (
        P("ctx", "tp"),
        P("ctx", "tp"),
        P("ctx", "tp"),
        P("tp", None),
        P("ctx", "tp"),
        P(),
        P(),
    )
    return jax.shard_map(
        per_device,
        mesh=mesh,
        in_specs=placed,
        out_specs=(P("ctx", "tp"), P("ctx", "tp"), P("ctx", "tp"), P("ctx", "tp"), P("tp", "ctx")),
        check_vma=False,
    )
```

```python
import functools
import math

import jax
import jax.numpy as jnp
from jax import lax
from jax.experimental import pallas as pl
from jax.experimental.pallas import tpu as pltpu
from jax.sharding import PartitionSpec as P

HDIM = 128
BLK = 512
WIN = 4
SCALE = 1.0 / math.sqrt(HDIM)
SCALE2 = SCALE * math.log2(math.e)
AXES = ("ctx", "tp")
NT = (((1,), (1,)), ((), ()))
NN = (((1,), (0,)), ((), ()))
f32 = jnp.float32
bf16 = jnp.bfloat16


def places():
    for x_lo in range(2):
        for y in range(4):
            for z in range(4):
                for x_hi in range(2):
                    for core in range(2):
                        yield x_lo, y, z, x_hi, core


def number(x_lo, y, z, x_hi, core):
    return ((x_lo * 4 + y) * 4 + z) * 4 + x_hi * 2 + core


def move(value, target):
    pairs = [(number(*place), number(*target(*place))) for place in places()]
    return lax.ppermute(value, AXES, pairs)


def to_core(value):
    return move(value, lambda x_lo, y, z, x_hi, core: (x_lo, y, z, x_hi, 1 - core))


def to_x_hi(value):
    return move(value, lambda x_lo, y, z, x_hi, core: (x_lo, y, z, 1 - x_hi, core))


def to_x_lo(value):
    return move(value, lambda x_lo, y, z, x_hi, core: (1 - x_lo, y, z, x_hi, core))


def to_y(value, steps):
    return move(value, lambda x_lo, y, z, x_hi, core: (x_lo, (y + steps) % 4, z, x_hi, core))


def to_z(value, steps):
    return move(value, lambda x_lo, y, z, x_hi, core: (x_lo, y, (z + steps) % 4, x_hi, core))


EDGE = 15


def along_ctx(value, steps):
    pairs = [(s, s + steps) for s in range(32) if 0 <= s + steps < 32]
    return lax.ppermute(value, "ctx", pairs)


def middle(source, sign):
    if source // 16 == (source + 2 * sign) // 16:
        return source // 4 * 4 + (source % 4 - sign) % 4
    return {14: 29, 15: 13, 17: 2, 16: 18}[source]


def two_pairs(sign):
    sources = [s for s in range(32) if 0 <= s + 2 * sign < 32]
    return [(s, middle(s, sign), s + 2 * sign) for s in sources]


def first_hop(value, sign):
    return lax.ppermute(value, "ctx", [(s, m) for s, m, _ in two_pairs(sign)])


def second_hop(value, sign):
    return lax.ppermute(value, "ctx", [(m, t) for _, m, t in two_pairs(sign)])


def block_rule(spans, pairs, query_block, key_block):
    listed = jnp.any(
        (pairs[:, 0] == query_block[..., None]) & (pairs[:, 1] == key_block[..., None]), axis=-1
    )
    span_lower = spans[:, 0]
    span_upper = spans[:, 0] + spans[:, 1]
    query_inside = (span_lower <= query_block[..., None]) & (query_block[..., None] < span_upper)
    key_inside = (span_lower <= key_block[..., None]) & (key_block[..., None] < span_upper)
    same = jnp.any(query_inside & key_inside, axis=-1)
    reach = (query_block - key_block >= 0) & (query_block - key_block < WIN)
    return listed & same & reach


def dot(a, b, dims):
    return lax.dot_general(a, b, dims, preferred_element_type=f32)


def causal():
    key_row = lax.broadcasted_iota(jnp.int32, (BLK, BLK), 0)
    query_column = lax.broadcasted_iota(jnp.int32, (BLK, BLK), 1)
    return key_row <= query_column


def block_rows(index):
    return pl.ds(index * BLK, BLK)


OWN_TILES = ((0, 0, 0), (1, 0, 1), (1, 1, 0))
BEHIND_TILES = ((0, 3, 0), (0, 2, 1), (0, 1, 2), (1, 3, 1), (1, 2, 2))


def key_value(index, near_k, near_v, edge_k, edge_v, far):
    if index == 0:
        return far[0], far[1]
    rows = block_rows(index - 1)
    return near_k[rows, :] + edge_k[rows, :], near_v[rows, :] + edge_v[rows, :]


def absorb(keys, vals, query, top, total, acc, rows):
    s = dot(keys, query, NT)
    old = top
    m = jnp.maximum(old, jnp.max(s, axis=0, keepdims=True))
    p = jnp.exp2(s * SCALE2 - m * SCALE2)
    fix = jnp.exp2((old - m) * SCALE2)
    part = dot(vals.T, p.astype(bf16), NN)
    acc[:, rows] = acc[:, rows] * fix + part
    return m, total * fix + jnp.sum(p, axis=0, keepdims=True)


def forward_own_kernel(flags, q_ref, k_ref, v_ref, after, acc, top, total):
    for qb, o, index in OWN_TILES:
        rows = block_rows(qb)
        line = slice(qb, qb + 1)

        def diagonal(rows=rows, line=line):
            s = jnp.where(causal(), dot(k_ref[rows, :], q_ref[rows, :], NT), -jnp.inf)
            m = jnp.max(s, axis=0, keepdims=True)
            p = jnp.exp2(s * SCALE2 - m * SCALE2)
            acc[:, rows] = dot(v_ref[rows, :].T, p.astype(bf16), NN)
            top[0, line, :] = m
            total[0, line, :] = jnp.sum(p, axis=0, keepdims=True)

        def nothing(rows=rows, line=line):
            acc[:, rows] = jnp.zeros((HDIM, BLK), f32)
            top[0, line, :] = jnp.zeros((1, BLK), f32)
            total[0, line, :] = jnp.ones((1, BLK), f32)

        def tile(rows=rows, line=line, index=index):
            held = block_rows(index)
            top[0, line, :], total[0, line, :] = absorb(
                k_ref[held, :], v_ref[held, :], q_ref[rows, :],
                top[0, line, :], total[0, line, :], acc, rows,
            )

        listed = flags[qb * WIN + o] == 1
        if o == 0:
            pl.when(listed)(diagonal)
            pl.when(jnp.logical_not(listed))(nothing)
        else:
            pl.when(listed)(tile)


def forward_behind_kernel(
    flags, q_ref, k1_ref, v1_ref, k0_ref, v0_ref, far_ref, acc_in, top_in, total_in,
    after, out_ref, turned_ref, log_ref, acc, top, total,
):
    acc[...] = acc_in[...]
    top[...] = top_in[0]
    total[...] = total_in[0]
    for qb, o, index in BEHIND_TILES:
        rows = block_rows(qb)
        line = slice(qb, qb + 1)

        @pl.when(flags[qb * WIN + o] == 1)
        def _(rows=rows, line=line, index=index):
            keys, vals = key_value(index, k1_ref, v1_ref, k0_ref, v0_ref, far_ref)
            top[line, :], total[line, :] = absorb(
                keys, vals, q_ref[rows, :], top[line, :], total[line, :], acc, rows
            )

    for qb in range(2):
        rows = block_rows(qb)
        result = acc[:, rows] * (1.0 / total[qb : qb + 1, :])
        turned_ref[:, rows] = result.astype(bf16)
        out_ref[rows, :] = result.T.astype(bf16)
    log_ref[0] = top[...] * SCALE2 + jnp.log2(total[...])


def tile_grads(keys, vals, query, grad, log_sum, delta, diagonal):
    p = jnp.exp2(dot(keys, query, NT) * SCALE2 - log_sum)
    if diagonal:
        p = jnp.where(causal(), p, 0.0)
    value_part = dot(p.astype(bf16), grad, NN)
    dp = dot(vals, grad, NT)
    ds = (p * (dp - delta)).astype(bf16)
    return dot(ds, query, NN), value_part, dot(keys.T, ds, NN)


def backward_behind_kernel(
    flags, q_ref, k1_ref, v1_ref, k0_ref, v0_ref, far_ref, out_ref, grad_ref, log_ref,
    after, near_back, far_back, dq, delta_ref, dk, dv,
):
    dk[...] = jnp.zeros_like(dk)
    dv[...] = jnp.zeros_like(dv)
    dq[...] = jnp.zeros_like(dq)
    product = grad_ref[...].astype(f32) * out_ref[...].astype(f32)
    delta = jnp.sum(product.T, axis=0, keepdims=True)
    for qb in range(2):
        delta_ref[0, qb : qb + 1, :] = delta[:, qb * BLK : (qb + 1) * BLK]
    for qb, o, index in BEHIND_TILES:
        rows = block_rows(qb)
        line = slice(qb, qb + 1)

        @pl.when(flags[qb * WIN + o] == 1)
        def _(rows=rows, line=line, index=index):
            keys, vals = key_value(index, k1_ref, v1_ref, k0_ref, v0_ref, far_ref)
            key_part, value_part, query_part = tile_grads(
                keys, vals, q_ref[rows, :], grad_ref[rows, :],
                log_ref[0, line, :], delta_ref[0, line, :], False,
            )
            dk[block_rows(index), :] += key_part
            dv[block_rows(index), :] += value_part
            dq[:, rows] += query_part

    far_back[0] = (dk[block_rows(0), :] * SCALE).astype(bf16)
    far_back[1] = dv[block_rows(0), :].astype(bf16)
    near_back[0] = (dk[pl.ds(BLK, 2 * BLK), :] * SCALE).astype(bf16)
    near_back[1] = dv[pl.ds(BLK, 2 * BLK), :].astype(bf16)


def backward_own_kernel(
    flags, q_ref, k_ref, v_ref, grad_ref, log_ref, dq_in, delta_ref, after,
    dq_ref, own_ref, dk, dv, dq,
):
    dk[...] = jnp.zeros_like(dk)
    dv[...] = jnp.zeros_like(dv)
    dq[...] = dq_in[...]
    for qb, o, index in OWN_TILES:
        rows = block_rows(qb)
        line = slice(qb, qb + 1)

        @pl.when(flags[qb * WIN + o] == 1)
        def _(rows=rows, line=line, index=index, o=o):
            held = block_rows(index)
            key_part, value_part, query_part = tile_grads(
                k_ref[held, :], v_ref[held, :], q_ref[rows, :], grad_ref[rows, :],
                log_ref[0, line, :], delta_ref[0, line, :], o == 0,
            )
            dk[held, :] += key_part
            dv[held, :] += value_part
            dq[:, rows] += query_part

    own_ref[0] = dk[...] * SCALE
    own_ref[1] = dv[...]
    dq_ref[...] = (dq[...] * SCALE).T.astype(bf16)


def finish_kernel(place, own_ref, near_ref, far_ref, after, key_ref, value_ref):
    for part, result in enumerate((key_ref, value_ref)):
        for block in range(2):
            rows = block_rows(block)
            total = own_ref[part, rows, :] + near_ref[part, rows, :].astype(f32)
            if block == 1:
                total += far_ref[part].astype(f32)
            result[rows, :] = total.astype(bf16)


def head(rows):
    return pl.BlockSpec((rows, HDIM), lambda h, *_: (0, h))


def head_pair(rows):
    return pl.BlockSpec((2, rows, HDIM), lambda h, *_: (0, 0, h))


HEAD_LINES = pl.BlockSpec((1, 2, BLK), lambda h, *_: (h, 0, 0))
ANY = pl.BlockSpec(memory_space=pl.ANY)
HEAD_TURNED = pl.BlockSpec((HDIM, 1024), lambda h, *_: (h, 0))


def shape(dims, dtype):
    return jax.ShapeDtypeStruct(dims, dtype)


WIDTH = 512
HEADS = WIDTH // HDIM
LINES = shape((HEADS, 2, BLK), f32)
TURNED = shape((WIDTH, 1024), f32)


def call(kernel, name, grid, ins, outs, out_shape, scratch, args):
    return pl.pallas_call(
        kernel,
        grid_spec=pltpu.PrefetchScalarGridSpec(
            num_scalar_prefetch=1,
            grid=grid,
            in_specs=ins,
            out_specs=outs,
            scratch_shapes=scratch,
        ),
        out_shape=out_shape,
        compiler_params=pltpu.CompilerParams(vmem_limit_bytes=64 << 20),
        cost_estimate=pl.CostEstimate(flops=1, bytes_accessed=1, transcendentals=0),
        name=name,
    )(*args)


def forward_own(flags, q, k, v, after):
    return call(
        forward_own_kernel, "forward_own", (HEADS,),
        [head(1024)] * 3 + [ANY],
        [HEAD_TURNED, HEAD_LINES, HEAD_LINES],
        [TURNED, LINES, LINES],
        [], (flags, q, k, v, after),
    )


def forward_behind(flags, q, near_k, near_v, edge_k, edge_v, far, state, after):
    lines = pltpu.VMEM((2, BLK), f32)
    return call(
        forward_behind_kernel, "forward_behind", (HEADS,),
        [head(1024)] * 5 + [head_pair(512)]
        + [HEAD_TURNED, HEAD_LINES, HEAD_LINES, ANY],
        [head(1024), HEAD_TURNED, HEAD_LINES],
        [shape((1024, WIDTH), bf16), shape((WIDTH, 1024), bf16), LINES],
        [pltpu.VMEM((HDIM, 1024), f32), lines, lines],
        (flags, q, near_k, near_v, edge_k, edge_v, far, *state, after),
    )


def backward_behind(
    flags, q, near_k, near_v, edge_k, edge_v, far, out, grad, log_sum, after
):
    held = pltpu.VMEM((3 * BLK, HDIM), f32)
    return call(
        backward_behind_kernel, "backward_behind", (HEADS,),
        [head(1024)] * 5 + [head_pair(512)]
        + [head(1024), head(1024), HEAD_LINES, ANY],
        [head_pair(1024), head_pair(512), HEAD_TURNED, HEAD_LINES],
        [shape((2, 1024, WIDTH), bf16), shape((2, 512, WIDTH), bf16), TURNED, LINES],
        [held, held], (flags, q, near_k, near_v, edge_k, edge_v, far, out, grad, log_sum, after),
    )


def backward_own(flags, q, k, v, grad, log_sum, dq, delta, after):
    held = pltpu.VMEM((2 * BLK, HDIM), f32)
    return call(
        backward_own_kernel, "backward_own", (HEADS,),
        [head(1024)] * 4 + [HEAD_LINES, HEAD_TURNED, HEAD_LINES, ANY],
        [head(1024), head_pair(1024)],
        [shape((1024, WIDTH), bf16), shape((2, 1024, WIDTH), f32)],
        [held, held, pltpu.VMEM((HDIM, 1024), f32)],
        (flags, q, k, v, grad, log_sum, dq, delta, after),
    )


def finish(place, own, near, far, after):
    return call(
        finish_kernel, "key_value_sum", (HEADS,),
        [head_pair(1024)] * 2 + [head_pair(512), ANY],
        [head(1024), head(1024)],
        [shape((1024, WIDTH), bf16)] * 2,
        [], (place, own, near, far, after),
    )


def pack_kernel(place, k_ref, v_ref, second_ref):
    second_ref[0] = k_ref[...]
    second_ref[1] = v_ref[...]


def pack(place, k, v):
    second = pl.BlockSpec((BLK, WIDTH), lambda i, place: (1, 0))
    return call(
        pack_kernel, "second_blocks", (1,), [second, second],
        pl.BlockSpec((2, BLK, WIDTH), lambda i, place: (0, 0, 0)),
        shape((2, BLK, WIDTH), bf16), [], (place, k, v),
    )


def nothing_kernel(*refs):
    pass


def together(values, after=()):
    return pl.pallas_call(
        nothing_kernel,
        in_specs=[ANY] * (len(values) + len(after)),
        out_specs=[ANY] * len(values),
        out_shape=[shape(value.shape, value.dtype) for value in values],
        input_output_aliases={index: index for index in range(len(values))},
        compiler_params=pltpu.CompilerParams(vmem_limit_bytes=64 << 20),
        name="order",
    )(*values, *after)


def grad_kernel(place, a_ref, b_ref, wa_ref, wb_ref, *rest):
    total = dot(a_ref[...], wa_ref[...], NT) + dot(b_ref[...], wb_ref[...], NT)
    if len(rest) == 3:
        total += rest[0][...]
    rest[-1][...] = total.astype(rest[-1].dtype)


def grad_terms(place, first, a, b, weight, before, after):
    tile = 512
    row = pl.BlockSpec((tile, 1024), lambda i, place: (i, 0))
    result = pl.BlockSpec((tile, 512), lambda i, place: (i, 0))

    def columns(flip):
        return pl.BlockSpec((512, 1024), lambda i, place: (0, place[0] ^ flip))

    more = [] if before is None else [before]
    return call(
        grad_kernel, "projection_backward", (1024 // tile,),
        [row, row, columns(first), columns(first + 1)] + [result] * len(more) + [ANY], result,
        shape((1024, 512), bf16 if more else f32), [], (place, a, b, weight, weight, *more, after),
    )


def weight_kernel(place, turned_ref, a_ref, b_ref, after, *outs):
    y = (place[0] ^ pl.program_id(0)) % 2 * 2 + pl.program_id(1)
    for part, ref in enumerate((a_ref, b_ref)):
        for slot, out_ref in enumerate(outs):

            @pl.when((pl.program_id(0) == part) & ((y - place[1] + 3) % 4 == slot))
            def _(ref=ref, out_ref=out_ref):
                out_ref[...] = dot(turned_ref[...], ref[...], NN).astype(bf16)


def weight_terms(place, turned, a, b, after):
    return call(
        weight_kernel, "weight_gradient", (2, 2),
        [
            pl.BlockSpec((512, 1024), lambda i, half, place: (0, 0)),
            pl.BlockSpec((1024, 512), lambda i, half, place: (0, jnp.where(i == 0, half, 1))),
            pl.BlockSpec((1024, 512), lambda i, half, place: (0, jnp.where(i == 0, 0, half))),
            ANY,
        ],
        [pl.BlockSpec((512, 512), lambda i, half, place: (0, 0))] * 4,
        [shape((512, 512), bf16)] * 4, [], (place, turned, a, b, after),
    )


def over_y(parts):
    return [to_y(parts[s], s + 1) for s in (0, 2, 1)]


def groups_along(axis):
    groups = {}
    for ctx in range(32):
        spot = [ctx // 16, ctx // 4 % 4, ctx % 4]
        spot[axis] = None
        groups.setdefault(tuple(spot), []).append(ctx)
    return list(groups.values())


def pieces_kernel(place, a0, a1, a2, a3, b0, b1, b2, b3, after, *outs):
    def total(refs):
        return sum(ref[...].astype(f32) for ref in refs).astype(bf16)

    for slot, out_ref in enumerate(outs):

        @pl.when(pl.program_id(0) == slot)
        def _(out_ref=out_ref):
            out_ref[0] = total((a0, a1, a2, a3))
            out_ref[1] = total((b0, b1, b2, b3))


def pieces_by_z(place, a, b, after):
    piece = pl.BlockSpec((512, 128), lambda i, place: (0, (place[2] + i + 1) % 4))
    return call(
        pieces_kernel, "weight_by_z", (4,), [piece] * 8 + [ANY],
        [pl.BlockSpec((2, 512, 128), lambda i, place: (0, 0, 0))] * 4,
        [shape((2, 512, 128), bf16)] * 4, [], (place, *a, *b, after),
    )


def weight_z_kernel(place, a_ref, b_ref, c_ref, d_ref, after, kept_ref, sent_ref):
    def total(index):
        return sum(ref[index].astype(f32) for ref in (a_ref, b_ref, c_ref, d_ref))

    kept = place[3] ^ (place[0] // 2)
    kept_ref[...] = total(kept)
    sent_ref[...] = total(1 - kept).astype(bf16)


def weight_z_sum(place, terms, after):
    whole = pl.BlockSpec((2, 512, 128), lambda i, place: (0, 0, 0))
    result = pl.BlockSpec((512, 128), lambda i, place: (0, 0))
    return call(
        weight_z_kernel, "weight_z_sum", (1,), [whole] * 4 + [ANY], [result] * 2,
        [shape((512, 128), f32), shape((512, 128), bf16)], [], (place, *terms, after),
    )


def copy_kernel(place, in_ref, *refs):
    refs[-1][...] = in_ref[...]


def far_columns(place, weight):
    return call(
        copy_kernel, "projection_quarter", (1,),
        [pl.BlockSpec((128, 2048), lambda i, place: (place[1], 1 - place[0] // 2))],
        pl.BlockSpec((128, 2048), lambda i, place: (0, 0)),
        shape((128, 2048), bf16), [], (place, weight),
    )


def two_kernel(place, a_ref, b_ref, after, a_out, b_out):
    a_out[...] = a_ref[...]
    b_out[...] = b_ref[...]


def late_copies(a, b, after):
    def rows(value):
        return pl.BlockSpec((512, value.shape[1]), lambda i, place: (i, 0))

    return call(
        two_kernel, "late_copies", (2,), [rows(a), rows(b), ANY], [rows(a), rows(b)],
        [shape(a.shape, a.dtype), shape(b.shape, b.dtype)],
        [], (jnp.zeros(1, jnp.int32), a, b, after),
    )


def core_kernel(place, own_ref, far_ref, far_rows, own_rows, after, out_ref):
    out_ref[0] = own_ref[...]
    out_ref[1] = far_ref[...]
    for part, rows in ((2, far_rows), (3, own_rows)):
        for half in range(2):
            out_ref[part, :, block_rows(half)] = rows[block_rows(half), :]


def for_core(place, weight, far_weight, far_attention, attention, after):
    rows = pl.BlockSpec((1024, 512), lambda i, place: (0, 0))
    return call(
        core_kernel, "for_core", (1,),
        [
            pl.BlockSpec((512, 1024), lambda i, place: (0, place[0] ^ 1)),
            pl.BlockSpec((512, 1024), lambda i, place: (0, 1 - place[0] % 2)),
            rows, rows, ANY,
        ],
        pl.BlockSpec((4, 512, 1024), lambda i, place: (0, 0, 0)),
        shape((4, 512, 1024), bf16), [],
        (place, weight, far_weight, far_attention, attention, after),
    )


def mix_kernel(place, own, core, far, far_core, w_own, w_far, w_core, after, out_ref):
    total = dot(own[...], w_own[...], NN) + dot(core[0], w_core[0], NN)
    total += dot(far[...], w_far[...], NN) + dot(far_core[0], w_core[1], NN)
    out_ref[...] = total.astype(bf16)


def mix(place, attention, far_attention, weight, far_weight, from_core, after):
    rows = pl.BlockSpec((512, 512), lambda i, place: (i, 0))
    return call(
        mix_kernel, "projection", (2,),
        [
            rows,
            pl.BlockSpec((1, 512, 512), lambda i, place: (3, 0, i)),
            rows,
            pl.BlockSpec((1, 512, 512), lambda i, place: (2, 0, i)),
            pl.BlockSpec((512, 1024), lambda i, place: (0, place[0])),
            pl.BlockSpec((512, 1024), lambda i, place: (0, place[0] % 2)),
            pl.BlockSpec((2, 512, 1024), lambda i, place: (0, 0, 0)),
            ANY,
        ],
        pl.BlockSpec((512, 1024), lambda i, place: (i, 0)),
        shape((1024, 1024), bf16), [],
        (place, attention, from_core, far_attention, from_core, weight, far_weight, from_core, after),
    )


def per_device(queries, keys, values, out_weight, out_grad, spans, pairs):
    ctx = lax.axis_index("ctx")
    tp = lax.axis_index("tp")
    place = jnp.stack([tp, ctx // 4 % 4, ctx % 4, ctx // 16]).astype(jnp.int32)

    near_pairs = [(s, s + 1) for s in range(31) if s != EDGE]
    near_keys = lax.ppermute(keys, "ctx", near_pairs + [(EDGE, 0)])
    crossed = lax.ppermute(values, "ctx", [(EDGE, EDGE + 16)])
    core_grad = to_core(out_grad)
    far_moved = first_hop(pack(place, keys, values), 1)
    far_weight = to_x_hi(far_columns(place, out_weight))

    query_block = ctx * 2 + jnp.arange(2, dtype=jnp.int32)[:, None] + jnp.zeros((1, WIN), jnp.int32)
    key_block = query_block - jnp.arange(WIN, dtype=jnp.int32)[None, :]
    flags = block_rule(spans, pairs, query_block, key_block).astype(jnp.int32).reshape(-1)
    own_state = forward_own(flags, queries, keys, values, keys)
    held_values, held_grad = late_copies(values, out_grad, own_state[1])

    near_keys, crossed, core_grad, far_moved, far_weight, held_values, held_grad = together(
        [near_keys, crossed, core_grad, far_moved, far_weight, held_values, held_grad]
    )
    near_values = lax.ppermute(held_values, "ctx", near_pairs)
    edge_keys = lax.ppermute(near_keys, "ctx", [(0, EDGE + 1)])
    edge_values = lax.ppermute(crossed, "ctx", [(EDGE + 16, EDGE + 1)])
    far = second_hop(far_moved, 1)
    far_grad = to_x_hi(held_grad)
    far_weight = lax.all_gather(
        far_weight, "ctx", axis=0, tiled=True, axis_index_groups=groups_along(1)
    )
    terms = grad_terms(place, 0, out_grad, core_grad, out_weight, None, near_keys)
    behind = (flags, queries, near_keys, near_values, edge_keys, edge_values, far)
    attention, turned, log_sum = forward_behind(*behind, own_state, terms)

    far_attention = to_x_hi(attention)
    own_parts = weight_terms(place, turned, out_grad, core_grad, log_sum)
    far_grad, far_weight, far_attention = together(
        [far_grad, far_weight, far_attention], [own_parts[3]]
    )
    own_moved = over_y(own_parts)
    far_core_grad = to_core(far_grad)
    from_core = to_core(
        for_core(place, out_weight, far_weight, far_attention, attention, own_parts[3])
    )
    far_parts = weight_terms(place, turned, far_grad, far_core_grad, far_weight)
    attn_grad = grad_terms(place, 2, far_grad, far_core_grad, out_weight, terms, far_parts[3])

    *held, from_core, attn_grad = together([*own_moved, *far_parts, from_core, attn_grad])
    own_moved, far_parts = held[:3], held[3:]
    far_moved = over_y(far_parts)
    near_back, far_back, dq, delta = backward_behind(
        *behind, attention, attn_grad, log_sum, attn_grad
    )
    near_back = along_ctx(near_back, -1)
    back_moved = first_hop(far_back, -1)
    query_grad, own = backward_own(
        flags, queries, keys, values, attn_grad, log_sum, dq, delta, delta
    )
    [back_moved] = together([back_moved], [own])
    far_back = second_hop(back_moved, -1)

    weight_pieces = pieces_by_z(
        place, [own_parts[3], *own_moved], [far_parts[3], *far_moved], own
    )
    weight_terms_z = [weight_pieces[3]] + [to_z(weight_pieces[s], s + 1) for s in (0, 2, 1)]
    mixed = mix(
        place, attention, far_attention, out_weight, far_weight, from_core, weight_pieces[3]
    )
    kept, sent = weight_z_sum(place, weight_terms_z, mixed)
    weight_grad = kept + to_x_lo(sent).astype(f32)
    key_grad, value_grad = finish(place, own, near_back, far_back, kept)
    return (mixed, query_grad, key_grad, value_grad, weight_grad)


def solution(mesh):
    placed = (
        P("ctx", "tp"),
        P("ctx", "tp"),
        P("ctx", "tp"),
        P("tp", None),
        P("ctx", "tp"),
        P(),
        P(),
    )
    return jax.shard_map(
        per_device,
        mesh=mesh,
        in_specs=placed,
        out_specs=(P("ctx", "tp"), P("ctx", "tp"), P("ctx", "tp"), P("ctx", "tp"), P("tp", "ctx")),
        check_vma=False,
    )
```

```python
import functools
import math

import jax
import jax.numpy as jnp
from jax import lax
from jax.experimental import pallas as pl
from jax.experimental.pallas import tpu as pltpu
from jax.sharding import PartitionSpec as P

HDIM = 128
BLK = 512
WIN = 4
SCALE = 1.0 / math.sqrt(HDIM)
SCALE2 = SCALE * math.log2(math.e)
AXES = ("ctx", "tp")
NT = (((1,), (1,)), ((), ()))
NN = (((1,), (0,)), ((), ()))
f32 = jnp.float32
bf16 = jnp.bfloat16


def places():
    for x_lo in range(2):
        for y in range(4):
            for z in range(4):
                for x_hi in range(2):
                    for core in range(2):
                        yield x_lo, y, z, x_hi, core


def number(x_lo, y, z, x_hi, core):
    return ((x_lo * 4 + y) * 4 + z) * 4 + x_hi * 2 + core


def move(value, target):
    pairs = [(number(*place), number(*target(*place))) for place in places()]
    return lax.ppermute(value, AXES, pairs)


def to_core(value):
    return move(value, lambda x_lo, y, z, x_hi, core: (x_lo, y, z, x_hi, 1 - core))


def to_x_hi(value):
    return move(value, lambda x_lo, y, z, x_hi, core: (x_lo, y, z, 1 - x_hi, core))


def to_x_lo(value):
    return move(value, lambda x_lo, y, z, x_hi, core: (1 - x_lo, y, z, x_hi, core))


def to_y(value, steps):
    return move(value, lambda x_lo, y, z, x_hi, core: (x_lo, (y + steps) % 4, z, x_hi, core))


def to_z(value, steps):
    return move(value, lambda x_lo, y, z, x_hi, core: (x_lo, y, (z + steps) % 4, x_hi, core))


EDGE = 15


def along_ctx(value, steps):
    pairs = [(s, s + steps) for s in range(32) if 0 <= s + steps < 32]
    return lax.ppermute(value, "ctx", pairs)


def middle(source, sign):
    return source // 4 * 4 + (source % 4 - sign) % 4


def two_pairs(sign):
    sources = [s for s in range(32) if 0 <= s + 2 * sign < 32]
    return [(s, middle(s, sign), s + 2 * sign) for s in sources]


def first_hop(value, sign):
    return lax.ppermute(value, "ctx", [(s, m) for s, m, _ in two_pairs(sign)])


def second_hop(value, sign):
    return lax.ppermute(value, "ctx", [(m, t) for _, m, t in two_pairs(sign)])


def block_rule(spans, pairs, query_block, key_block):
    listed = jnp.any(
        (pairs[:, 0] == query_block[..., None]) & (pairs[:, 1] == key_block[..., None]), axis=-1
    )
    span_lower = spans[:, 0]
    span_upper = spans[:, 0] + spans[:, 1]
    query_inside = (span_lower <= query_block[..., None]) & (query_block[..., None] < span_upper)
    key_inside = (span_lower <= key_block[..., None]) & (key_block[..., None] < span_upper)
    same = jnp.any(query_inside & key_inside, axis=-1)
    reach = (query_block - key_block >= 0) & (query_block - key_block < WIN)
    return listed & same & reach


def dot(a, b, dims):
    return lax.dot_general(a, b, dims, preferred_element_type=f32)


def causal():
    key_row = lax.broadcasted_iota(jnp.int32, (BLK, BLK), 0)
    query_column = lax.broadcasted_iota(jnp.int32, (BLK, BLK), 1)
    return key_row <= query_column


def block_rows(index):
    return pl.ds(index * BLK, BLK)


OWN_TILES = ((0, 0, 0), (1, 0, 1), (1, 1, 0))
BEHIND_TILES = ((0, 3, 0), (0, 2, 1), (0, 1, 2), (1, 3, 1), (1, 2, 2))


def key_value(index, near_k, near_v, edge_v, far):
    if index == 0:
        return far[0], far[1]
    rows = block_rows(index - 1)
    return near_k[rows, :], near_v[rows, :] + edge_v[rows, :]


def absorb(keys, vals, query, top, total, acc, rows):
    s = dot(keys, query, NT)
    old = top
    m = jnp.maximum(old, jnp.max(s, axis=0, keepdims=True))
    p = jnp.exp2(s * SCALE2 - m * SCALE2)
    fix = jnp.exp2((old - m) * SCALE2)
    part = dot(vals.T, p.astype(bf16), NN)
    acc[:, rows] = acc[:, rows] * fix + part
    return m, total * fix + jnp.sum(p, axis=0, keepdims=True)


def forward_own_kernel(flags, q_ref, k_ref, v_ref, after, acc, top, total):
    for qb, o, index in OWN_TILES:
        rows = block_rows(qb)
        line = slice(qb, qb + 1)

        def diagonal(rows=rows, line=line):
            s = jnp.where(causal(), dot(k_ref[rows, :], q_ref[rows, :], NT), -jnp.inf)
            m = jnp.max(s, axis=0, keepdims=True)
            p = jnp.exp2(s * SCALE2 - m * SCALE2)
            acc[:, rows] = dot(v_ref[rows, :].T, p.astype(bf16), NN)
            top[0, line, :] = m
            total[0, line, :] = jnp.sum(p, axis=0, keepdims=True)

        def nothing(rows=rows, line=line):
            acc[:, rows] = jnp.zeros((HDIM, BLK), f32)
            top[0, line, :] = jnp.zeros((1, BLK), f32)
            total[0, line, :] = jnp.ones((1, BLK), f32)

        def tile(rows=rows, line=line, index=index):
            held = block_rows(index)
            top[0, line, :], total[0, line, :] = absorb(
                k_ref[held, :], v_ref[held, :], q_ref[rows, :],
                top[0, line, :], total[0, line, :], acc, rows,
            )

        listed = flags[qb * WIN + o] == 1
        if o == 0:
            pl.when(listed)(diagonal)
            pl.when(jnp.logical_not(listed))(nothing)
        else:
            pl.when(listed)(tile)


def forward_behind_kernel(
    flags, q_ref, k1_ref, v1_ref, v0_ref, far_ref, acc_in, top_in, total_in,
    after, out_ref, turned_ref, log_ref, acc, top, total,
):
    acc[...] = acc_in[...]
    top[...] = top_in[0]
    total[...] = total_in[0]
    for qb, o, index in BEHIND_TILES:
        rows = block_rows(qb)
        line = slice(qb, qb + 1)

        @pl.when(flags[qb * WIN + o] == 1)
        def _(rows=rows, line=line, index=index):
            keys, vals = key_value(index, k1_ref, v1_ref, v0_ref, far_ref)
            top[line, :], total[line, :] = absorb(
                keys, vals, q_ref[rows, :], top[line, :], total[line, :], acc, rows
            )

    for qb in range(2):
        rows = block_rows(qb)
        result = acc[:, rows] * (1.0 / total[qb : qb + 1, :])
        turned_ref[:, rows] = result.astype(bf16)
        out_ref[rows, :] = result.T.astype(bf16)
    log_ref[0] = top[...] * SCALE2 + jnp.log2(total[...])


def tile_grads(keys, vals, query, grad, log_sum, delta, diagonal):
    p = jnp.exp2(dot(keys, query, NT) * SCALE2 - log_sum)
    if diagonal:
        p = jnp.where(causal(), p, 0.0)
    value_part = dot(p.astype(bf16), grad, NN)
    dp = dot(vals, grad, NT)
    ds = (p * (dp - delta)).astype(bf16)
    return dot(ds, query, NN), value_part, dot(keys.T, ds, NN)


def backward_behind_kernel(
    flags, q_ref, k1_ref, v1_ref, v0_ref, far_ref, out_ref, grad_ref, log_ref,
    after, near_back, far_back, dq, delta_ref, dk, dv,
):
    dk[...] = jnp.zeros_like(dk)
    dv[...] = jnp.zeros_like(dv)
    dq[...] = jnp.zeros_like(dq)
    product = grad_ref[...].astype(f32) * out_ref[...].astype(f32)
    delta = jnp.sum(product.T, axis=0, keepdims=True)
    for qb in range(2):
        delta_ref[0, qb : qb + 1, :] = delta[:, qb * BLK : (qb + 1) * BLK]
    for qb, o, index in BEHIND_TILES:
        rows = block_rows(qb)
        line = slice(qb, qb + 1)

        @pl.when(flags[qb * WIN + o] == 1)
        def _(rows=rows, line=line, index=index):
            keys, vals = key_value(index, k1_ref, v1_ref, v0_ref, far_ref)
            key_part, value_part, query_part = tile_grads(
                keys, vals, q_ref[rows, :], grad_ref[rows, :],
                log_ref[0, line, :], delta_ref[0, line, :], False,
            )
            dk[block_rows(index), :] += key_part
            dv[block_rows(index), :] += value_part
            dq[:, rows] += query_part

    far_back[0] = (dk[block_rows(0), :] * SCALE).astype(bf16)
    far_back[1] = dv[block_rows(0), :].astype(bf16)
    near_back[0] = (dk[pl.ds(BLK, 2 * BLK), :] * SCALE).astype(bf16)
    near_back[1] = dv[pl.ds(BLK, 2 * BLK), :].astype(bf16)


def backward_own_kernel(
    flags, q_ref, k_ref, v_ref, grad_ref, log_ref, dq_in, delta_ref, after,
    dq_ref, own_ref, dk, dv, dq,
):
    dk[...] = jnp.zeros_like(dk)
    dv[...] = jnp.zeros_like(dv)
    dq[...] = dq_in[...]
    for qb, o, index in OWN_TILES:
        rows = block_rows(qb)
        line = slice(qb, qb + 1)

        @pl.when(flags[qb * WIN + o] == 1)
        def _(rows=rows, line=line, index=index, o=o):
            held = block_rows(index)
            key_part, value_part, query_part = tile_grads(
                k_ref[held, :], v_ref[held, :], q_ref[rows, :], grad_ref[rows, :],
                log_ref[0, line, :], delta_ref[0, line, :], o == 0,
            )
            dk[held, :] += key_part
            dv[held, :] += value_part
            dq[:, rows] += query_part

    own_ref[0] = dk[...] * SCALE
    own_ref[1] = dv[...]
    dq_ref[...] = (dq[...] * SCALE).T.astype(bf16)


def finish_kernel(place, own_ref, near_ref, far_ref, after, key_ref, value_ref):
    for part, result in enumerate((key_ref, value_ref)):
        for block in range(2):
            rows = block_rows(block)
            total = own_ref[part, rows, :] + near_ref[part, rows, :].astype(f32)
            if block == 1:
                total += far_ref[part].astype(f32)
            result[rows, :] = total.astype(bf16)


def head(rows):
    return pl.BlockSpec((rows, HDIM), lambda h, *_: (0, h))


def head_pair(rows):
    return pl.BlockSpec((2, rows, HDIM), lambda h, *_: (0, 0, h))


HEAD_LINES = pl.BlockSpec((1, 2, BLK), lambda h, *_: (h, 0, 0))
ANY = pl.BlockSpec(memory_space=pl.ANY)
HEAD_TURNED = pl.BlockSpec((HDIM, 1024), lambda h, *_: (h, 0))


def shape(dims, dtype):
    return jax.ShapeDtypeStruct(dims, dtype)


WIDTH = 512
HEADS = WIDTH // HDIM
LINES = shape((HEADS, 2, BLK), f32)
TURNED = shape((WIDTH, 1024), f32)


def call(kernel, name, grid, ins, outs, out_shape, scratch, args):
    return pl.pallas_call(
        kernel,
        grid_spec=pltpu.PrefetchScalarGridSpec(
            num_scalar_prefetch=1,
            grid=grid,
            in_specs=ins,
            out_specs=outs,
            scratch_shapes=scratch,
        ),
        out_shape=out_shape,
        compiler_params=pltpu.CompilerParams(vmem_limit_bytes=64 << 20),
        cost_estimate=pl.CostEstimate(flops=1, bytes_accessed=1, transcendentals=0),
        name=name,
    )(*args)


def forward_own(flags, q, k, v, after):
    return call(
        forward_own_kernel, "forward_own", (HEADS,),
        [head(1024)] * 3 + [ANY],
        [HEAD_TURNED, HEAD_LINES, HEAD_LINES],
        [TURNED, LINES, LINES],
        [], (flags, q, k, v, after),
    )


def forward_behind(flags, q, near_k, near_v, edge_v, far, state, after):
    lines = pltpu.VMEM((2, BLK), f32)
    return call(
        forward_behind_kernel, "forward_behind", (HEADS,),
        [head(1024)] * 4 + [head_pair(512)]
        + [HEAD_TURNED, HEAD_LINES, HEAD_LINES, ANY],
        [head(1024), HEAD_TURNED, HEAD_LINES],
        [shape((1024, WIDTH), bf16), shape((WIDTH, 1024), bf16), LINES],
        [pltpu.VMEM((HDIM, 1024), f32), lines, lines],
        (flags, q, near_k, near_v, edge_v, far, *state, after),
    )


def backward_behind(
    flags, q, near_k, near_v, edge_v, far, out, grad, log_sum, after
):
    held = pltpu.VMEM((3 * BLK, HDIM), f32)
    return call(
        backward_behind_kernel, "backward_behind", (HEADS,),
        [head(1024)] * 4 + [head_pair(512)]
        + [head(1024), head(1024), HEAD_LINES, ANY],
        [head_pair(1024), head_pair(512), HEAD_TURNED, HEAD_LINES],
        [shape((2, 1024, WIDTH), bf16), shape((2, 512, WIDTH), bf16), TURNED, LINES],
        [held, held], (flags, q, near_k, near_v, edge_v, far, out, grad, log_sum, after),
    )


def backward_own(flags, q, k, v, grad, log_sum, dq, delta, after):
    held = pltpu.VMEM((2 * BLK, HDIM), f32)
    return call(
        backward_own_kernel, "backward_own", (HEADS,),
        [head(1024)] * 4 + [HEAD_LINES, HEAD_TURNED, HEAD_LINES, ANY],
        [head(1024), head_pair(1024)],
        [shape((1024, WIDTH), bf16), shape((2, 1024, WIDTH), f32)],
        [held, held, pltpu.VMEM((HDIM, 1024), f32)],
        (flags, q, k, v, grad, log_sum, dq, delta, after),
    )


def finish(place, own, near, far, after):
    return call(
        finish_kernel, "key_value_sum", (HEADS,),
        [head_pair(1024)] * 2 + [head_pair(512), ANY],
        [head(1024), head(1024)],
        [shape((1024, WIDTH), bf16)] * 2,
        [], (place, own, near, far, after),
    )


def pack_kernel(place, k_ref, v_ref, second_ref):
    second_ref[0] = k_ref[...]
    second_ref[1] = v_ref[...]


def pack(place, k, v):
    second = pl.BlockSpec((BLK, WIDTH), lambda i, place: (1, 0))
    return call(
        pack_kernel, "second_blocks", (1,), [second, second],
        pl.BlockSpec((2, BLK, WIDTH), lambda i, place: (0, 0, 0)),
        shape((2, BLK, WIDTH), bf16), [], (place, k, v),
    )


def nothing_kernel(*refs):
    pass


def together(values, after=()):
    return pl.pallas_call(
        nothing_kernel,
        in_specs=[ANY] * (len(values) + len(after)),
        out_specs=[ANY] * len(values),
        out_shape=[shape(value.shape, value.dtype) for value in values],
        input_output_aliases={index: index for index in range(len(values))},
        compiler_params=pltpu.CompilerParams(vmem_limit_bytes=64 << 20),
        name="order",
    )(*values, *after)


def grad_kernel(place, a_ref, b_ref, wa_ref, wb_ref, *rest):
    total = dot(a_ref[...], wa_ref[...], NT) + dot(b_ref[...], wb_ref[...], NT)
    if len(rest) == 3:
        total += rest[0][...]
    rest[-1][...] = total.astype(rest[-1].dtype)


def grad_terms(place, first, a, b, weight, before, after):
    tile = 512
    row = pl.BlockSpec((tile, 1024), lambda i, place: (i, 0))
    result = pl.BlockSpec((tile, 512), lambda i, place: (i, 0))

    def columns(flip):
        return pl.BlockSpec((512, 1024), lambda i, place: (0, place[0] ^ flip))

    more = [] if before is None else [before]
    return call(
        grad_kernel, "projection_backward", (1024 // tile,),
        [row, row, columns(first), columns(first + 1)] + [result] * len(more) + [ANY], result,
        shape((1024, 512), bf16 if more else f32), [], (place, a, b, weight, weight, *more, after),
    )


def weight_kernel(place, turned_ref, g0, g1, g2, g3, *outs):
    owner = place[0] ^ pl.program_id(0)
    y = owner % 2 * 2 + pl.program_id(1)
    for part, ref in enumerate((g0, g1, g2, g3)):
        for slot, out_ref in enumerate(outs):

            @pl.when((pl.program_id(0) == part) & ((y - place[1] + 3) % 4 == slot))
            def _(ref=ref, out_ref=out_ref, part=part):
                out_ref[part // 2] = dot(turned_ref[...], ref[...], NN).astype(bf16)


def weight_terms(place, turned, cotangents):
    def piece(part):
        return pl.BlockSpec(
            (1024, 512),
            lambda i, half, place: (
                0, jnp.where(i == part, half, jnp.where(i < part, 0, 1)),
            ),
        )

    return call(
        weight_kernel, "weight_gradient", (4, 2),
        [pl.BlockSpec((512, 1024), lambda i, half, place: (0, 0))] + [piece(p) for p in range(4)],
        [pl.BlockSpec((2, 512, 512), lambda i, half, place: (0, 0, 0))] * 4,
        [shape((2, 512, 512), bf16)] * 4, [], (place, turned, *cotangents),
    )


def over_y(parts):
    return [to_y(parts[s], s + 1) for s in (0, 2, 1)]


def groups_along(axis):
    groups = {}
    for ctx in range(32):
        spot = [ctx // 16, ctx // 4 % 4, ctx % 4]
        spot[axis] = None
        groups.setdefault(tuple(spot), []).append(ctx)
    return list(groups.values())


def pieces_kernel(place, a, b, c, d, after, *outs):
    for slot, out_ref in enumerate(outs):

        @pl.when(pl.program_id(0) == slot)
        def _(out_ref=out_ref):
            out_ref[...] = sum(ref[...].astype(f32) for ref in (a, b, c, d)).astype(bf16)


def pieces_by_z(place, terms, after):
    piece = pl.BlockSpec((2, 512, 128), lambda i, place: (0, 0, (place[2] + i + 1) % 4))
    return call(
        pieces_kernel, "weight_by_z", (4,), [piece] * 4 + [ANY],
        [pl.BlockSpec((2, 512, 128), lambda i, place: (0, 0, 0))] * 4,
        [shape((2, 512, 128), bf16)] * 4, [], (place, *terms, after),
    )


def weight_z_kernel(place, a_ref, b_ref, c_ref, d_ref, after, kept_ref, sent_ref):
    def total(index):
        return sum(ref[index].astype(f32) for ref in (a_ref, b_ref, c_ref, d_ref))

    kept = place[3] ^ (place[0] // 2)
    kept_ref[...] = total(kept)
    sent_ref[...] = total(1 - kept).astype(bf16)


def weight_z_sum(place, terms, after):
    whole = pl.BlockSpec((2, 512, 128), lambda i, place: (0, 0, 0))
    result = pl.BlockSpec((512, 128), lambda i, place: (0, 0))
    return call(
        weight_z_kernel, "weight_z_sum", (1,), [whole] * 4 + [ANY], [result] * 2,
        [shape((512, 128), f32), shape((512, 128), bf16)], [], (place, *terms, after),
    )


def copy_kernel(place, in_ref, *refs):
    refs[-1][...] = in_ref[...]


def far_columns(place, weight, after):
    return call(
        copy_kernel, "projection_quarter", (1,),
        [pl.BlockSpec((128, 2048), lambda i, place: (place[1], 1 - place[0] // 2)), ANY],
        pl.BlockSpec((128, 2048), lambda i, place: (0, 0)),
        shape((128, 2048), bf16), [], (place, weight, after),
    )


def core_kernel(place, own_ref, far_ref, far_rows, own_rows, after, out_ref):
    out_ref[0] = own_ref[...]
    out_ref[1] = far_ref[...]
    for part, rows in ((2, far_rows), (3, own_rows)):
        for half in range(2):
            out_ref[part, :, block_rows(half)] = rows[block_rows(half), :]


def for_core(place, weight, far_weight, far_attention, attention, after):
    rows = pl.BlockSpec((1024, 512), lambda i, place: (0, 0))
    return call(
        core_kernel, "for_core", (1,),
        [
            pl.BlockSpec((512, 1024), lambda i, place: (0, place[0] ^ 1)),
            pl.BlockSpec((512, 1024), lambda i, place: (0, 1 - place[0] % 2)),
            rows, rows, ANY,
        ],
        pl.BlockSpec((4, 512, 1024), lambda i, place: (0, 0, 0)),
        shape((4, 512, 1024), bf16), [],
        (place, weight, far_weight, far_attention, attention, after),
    )


def mix_kernel(place, own, core, far, far_core, w_own, w_far, w_core, after, out_ref):
    total = dot(own[...], w_own[...], NN) + dot(core[0], w_core[0], NN)
    total += dot(far[...], w_far[...], NN) + dot(far_core[0], w_core[1], NN)
    out_ref[...] = total.astype(bf16)


def mix(place, attention, far_attention, weight, far_weight, from_core, after):
    rows = pl.BlockSpec((512, 512), lambda i, place: (i, 0))
    return call(
        mix_kernel, "projection", (2,),
        [
            rows,
            pl.BlockSpec((1, 512, 512), lambda i, place: (3, 0, i)),
            rows,
            pl.BlockSpec((1, 512, 512), lambda i, place: (2, 0, i)),
            pl.BlockSpec((512, 1024), lambda i, place: (0, place[0])),
            pl.BlockSpec((512, 1024), lambda i, place: (0, place[0] % 2)),
            pl.BlockSpec((2, 512, 1024), lambda i, place: (0, 0, 0)),
            ANY,
        ],
        pl.BlockSpec((512, 1024), lambda i, place: (i, 0)),
        shape((1024, 1024), bf16), [],
        (place, attention, from_core, far_attention, from_core, weight, far_weight, from_core, after),
    )


def per_device(queries, keys, values, out_weight, out_grad, spans, pairs):
    ctx = lax.axis_index("ctx")
    tp = lax.axis_index("tp")
    place = jnp.stack([tp, ctx // 4 % 4, ctx % 4, ctx // 16]).astype(jnp.int32)

    far_grad = to_x_hi(out_grad)
    near_keys = along_ctx(keys, 1)
    near_pairs = [(s, s + 1) for s in range(31) if s != EDGE]
    near_values = lax.ppermute(values, "ctx", near_pairs + [(EDGE, 0)])
    core_grad = to_core(out_grad)
    far_moved = first_hop(pack(place, keys, values), 1)

    query_block = ctx * 2 + jnp.arange(2, dtype=jnp.int32)[:, None] + jnp.zeros((1, WIN), jnp.int32)
    key_block = query_block - jnp.arange(WIN, dtype=jnp.int32)[None, :]
    flags = block_rule(spans, pairs, query_block, key_block).astype(jnp.int32).reshape(-1)
    own_state = forward_own(flags, queries, keys, values, keys)
    terms = grad_terms(place, 0, out_grad, core_grad, out_weight, None, own_state[1])

    [far_moved] = together([far_moved], [terms])
    far = second_hop(far_moved, 1)
    near_keys, near_values, far, far_grad = together(
        [near_keys, near_values, far, far_grad], [far_moved]
    )

    far_core_grad = to_core(far_grad)
    far_weight = to_x_hi(far_columns(place, out_weight, near_keys))
    edge_values = lax.ppermute(near_values, "ctx", [(0, EDGE + 1)])
    behind = (flags, queries, near_keys, near_values, edge_values, far)
    attention, turned, log_sum = forward_behind(*behind, own_state, far)
    far_weight, far_core_grad = together([far_weight, far_core_grad], [log_sum])
    far_weight = lax.all_gather(
        far_weight, "ctx", axis=0, tiled=True, axis_index_groups=groups_along(1)
    )

    far_attention = to_x_hi(attention)
    weight_parts = weight_terms(place, turned, (out_grad, core_grad, far_grad, far_core_grad))
    attn_grad = grad_terms(place, 2, far_grad, far_core_grad, out_weight, terms, weight_parts[3])
    near_back, far_back, dq, delta = backward_behind(
        *behind, attention, attn_grad, log_sum, weight_parts[3]
    )
    far_attention, far_weight, *weight_parts = together(
        [far_attention, far_weight, *weight_parts], [delta]
    )
    weight_moved = over_y(weight_parts)
    near_back = along_ctx(near_back, -1)
    back_moved = first_hop(far_back, -1)
    query_grad, own = backward_own(
        flags, queries, keys, values, attn_grad, log_sum, dq, delta, far_attention
    )
    [back_moved] = together([back_moved], [own])
    far_back = second_hop(back_moved, -1)
    from_core = for_core(place, out_weight, far_weight, far_attention, attention, back_moved)
    *weight_moved, near_back, far_back, from_core = together(
        [*weight_moved, near_back, far_back, from_core]
    )
    weight_pieces = pieces_by_z(place, [weight_parts[3], *weight_moved], near_back)
    from_core = to_core(from_core)
    weight_terms_z = [weight_pieces[3]] + [to_z(weight_pieces[s], s + 1) for s in (0, 2, 1)]
    mixed = mix(
        place, attention, far_attention, out_weight, far_weight, from_core, weight_pieces[3]
    )
    kept, sent = weight_z_sum(place, weight_terms_z, mixed)
    weight_grad = kept + to_x_lo(sent).astype(f32)
    key_grad, value_grad = finish(place, own, near_back, far_back, kept)
    return (mixed, query_grad, key_grad, value_grad, weight_grad)


def solution(mesh):
    placed = (
        P("ctx", "tp"),
        P("ctx", "tp"),
        P("ctx", "tp"),
        P("tp", None),
        P("ctx", "tp"),
        P(),
        P(),
    )
    return jax.shard_map(
        per_device,
        mesh=mesh,
        in_specs=placed,
        out_specs=(P("ctx", "tp"), P("ctx", "tp"), P("ctx", "tp"), P("ctx", "tp"), P("tp", "ctx")),
        check_vma=False,
    )
```

```python
import functools
import math

import jax
import jax.numpy as jnp
from jax import lax
from jax.experimental import pallas as pl
from jax.experimental.pallas import tpu as pltpu
from jax.sharding import PartitionSpec as P

HDIM = 128
BLK = 512
WIN = 4
SCALE = 1.0 / math.sqrt(HDIM)
SCALE2 = SCALE * math.log2(math.e)
AXES = ("ctx", "tp")
NT = (((1,), (1,)), ((), ()))
NN = (((1,), (0,)), ((), ()))
f32 = jnp.float32
bf16 = jnp.bfloat16


def places():
    for x_lo in range(2):
        for y in range(4):
            for z in range(4):
                for x_hi in range(2):
                    for core in range(2):
                        yield x_lo, y, z, x_hi, core


def number(x_lo, y, z, x_hi, core):
    return ((x_lo * 4 + y) * 4 + z) * 4 + x_hi * 2 + core


def move(value, target):
    pairs = [(number(*place), number(*target(*place))) for place in places()]
    return lax.ppermute(value, AXES, pairs)


def to_core(value):
    return move(value, lambda x_lo, y, z, x_hi, core: (x_lo, y, z, x_hi, 1 - core))


def to_x_hi(value):
    return move(value, lambda x_lo, y, z, x_hi, core: (x_lo, y, z, 1 - x_hi, core))


def to_x_lo(value):
    return move(value, lambda x_lo, y, z, x_hi, core: (1 - x_lo, y, z, x_hi, core))


def to_y(value, steps):
    return move(value, lambda x_lo, y, z, x_hi, core: (x_lo, (y + steps) % 4, z, x_hi, core))


def to_z(value, steps):
    return move(value, lambda x_lo, y, z, x_hi, core: (x_lo, y, (z + steps) % 4, x_hi, core))


EDGE = 15


def along_ctx(value, steps):
    pairs = [(s, s + steps) for s in range(32) if 0 <= s + steps < 32]
    return lax.ppermute(value, "ctx", pairs)


def middle(source, sign):
    return source // 4 * 4 + (source % 4 - sign) % 4


def two_pairs(sign):
    sources = [s for s in range(32) if 0 <= s + 2 * sign < 32]
    return [(s, middle(s, sign), s + 2 * sign) for s in sources]


def first_hop(value, sign):
    return lax.ppermute(value, "ctx", [(s, m) for s, m, _ in two_pairs(sign)])


def second_hop(value, sign):
    return lax.ppermute(value, "ctx", [(m, t) for _, m, t in two_pairs(sign)])


def block_rule(spans, pairs, query_block, key_block):
    listed = jnp.any(
        (pairs[:, 0] == query_block[..., None]) & (pairs[:, 1] == key_block[..., None]), axis=-1
    )
    span_lower = spans[:, 0]
    span_upper = spans[:, 0] + spans[:, 1]
    query_inside = (span_lower <= query_block[..., None]) & (query_block[..., None] < span_upper)
    key_inside = (span_lower <= key_block[..., None]) & (key_block[..., None] < span_upper)
    same = jnp.any(query_inside & key_inside, axis=-1)
    reach = (query_block - key_block >= 0) & (query_block - key_block < WIN)
    return listed & same & reach


def dot(a, b, dims):
    return lax.dot_general(a, b, dims, preferred_element_type=f32)


def causal():
    key_row = lax.broadcasted_iota(jnp.int32, (BLK, BLK), 0)
    query_column = lax.broadcasted_iota(jnp.int32, (BLK, BLK), 1)
    return key_row <= query_column


def block_rows(index):
    return pl.ds(index * BLK, BLK)


OWN_TILES = ((0, 0, 0), (1, 0, 1), (1, 1, 0))
BEHIND_TILES = ((0, 3, 0), (0, 2, 1), (0, 1, 2), (1, 3, 1), (1, 2, 2))


def key_value(index, near_k, near_v, edge_v, far):
    if index == 0:
        return far[0], far[1]
    rows = block_rows(index - 1)
    return near_k[rows, :], near_v[rows, :] + edge_v[rows, :]


def absorb(keys, vals, query, top, total, acc, rows):
    s = dot(keys, query, NT)
    old = top
    m = jnp.maximum(old, jnp.max(s, axis=0, keepdims=True))
    p = jnp.exp2(s * SCALE2 - m * SCALE2)
    fix = jnp.exp2((old - m) * SCALE2)
    part = dot(vals.T, p.astype(bf16), NN)
    acc[:, rows] = acc[:, rows] * fix + part
    return m, total * fix + jnp.sum(p, axis=0, keepdims=True)


def forward_own_kernel(flags, q_ref, k_ref, v_ref, after, acc, top, total):
    for qb, o, index in OWN_TILES:
        rows = block_rows(qb)
        line = slice(qb, qb + 1)

        def diagonal(rows=rows, line=line):
            s = jnp.where(causal(), dot(k_ref[rows, :], q_ref[rows, :], NT), -jnp.inf)
            m = jnp.max(s, axis=0, keepdims=True)
            p = jnp.exp2(s * SCALE2 - m * SCALE2)
            acc[:, rows] = dot(v_ref[rows, :].T, p.astype(bf16), NN)
            top[0, line, :] = m
            total[0, line, :] = jnp.sum(p, axis=0, keepdims=True)

        def nothing(rows=rows, line=line):
            acc[:, rows] = jnp.zeros((HDIM, BLK), f32)
            top[0, line, :] = jnp.zeros((1, BLK), f32)
            total[0, line, :] = jnp.ones((1, BLK), f32)

        def tile(rows=rows, line=line, index=index):
            held = block_rows(index)
            top[0, line, :], total[0, line, :] = absorb(
                k_ref[held, :], v_ref[held, :], q_ref[rows, :],
                top[0, line, :], total[0, line, :], acc, rows,
            )

        listed = flags[qb * WIN + o] == 1
        if o == 0:
            pl.when(listed)(diagonal)
            pl.when(jnp.logical_not(listed))(nothing)
        else:
            pl.when(listed)(tile)


def forward_behind_kernel(
    flags, q_ref, k1_ref, v1_ref, v0_ref, far_ref, acc_in, top_in, total_in,
    after, out_ref, turned_ref, log_ref, acc, top, total,
):
    acc[...] = acc_in[...]
    top[...] = top_in[0]
    total[...] = total_in[0]
    for qb, o, index in BEHIND_TILES:
        rows = block_rows(qb)
        line = slice(qb, qb + 1)

        @pl.when(flags[qb * WIN + o] == 1)
        def _(rows=rows, line=line, index=index):
            keys, vals = key_value(index, k1_ref, v1_ref, v0_ref, far_ref)
            top[line, :], total[line, :] = absorb(
                keys, vals, q_ref[rows, :], top[line, :], total[line, :], acc, rows
            )

    for qb in range(2):
        rows = block_rows(qb)
        result = acc[:, rows] * (1.0 / total[qb : qb + 1, :])
        turned_ref[:, rows] = result.astype(bf16)
        out_ref[rows, :] = result.T.astype(bf16)
    log_ref[0] = top[...] * SCALE2 + jnp.log2(total[...])


def tile_grads(keys, vals, query, grad, log_sum, delta, diagonal):
    p = jnp.exp2(dot(keys, query, NT) * SCALE2 - log_sum)
    if diagonal:
        p = jnp.where(causal(), p, 0.0)
    value_part = dot(p.astype(bf16), grad, NN)
    dp = dot(vals, grad, NT)
    ds = (p * (dp - delta)).astype(bf16)
    return dot(ds, query, NN), value_part, dot(keys.T, ds, NN)


def backward_behind_kernel(
    flags, q_ref, k1_ref, v1_ref, v0_ref, far_ref, out_ref, grad_ref, log_ref,
    after, near_back, far_back, dq, delta_ref, dk, dv,
):
    dk[...] = jnp.zeros_like(dk)
    dv[...] = jnp.zeros_like(dv)
    dq[...] = jnp.zeros_like(dq)
    product = grad_ref[...].astype(f32) * out_ref[...].astype(f32)
    delta = jnp.sum(product.T, axis=0, keepdims=True)
    for qb in range(2):
        delta_ref[0, qb : qb + 1, :] = delta[:, qb * BLK : (qb + 1) * BLK]
    for qb, o, index in BEHIND_TILES:
        rows = block_rows(qb)
        line = slice(qb, qb + 1)

        @pl.when(flags[qb * WIN + o] == 1)
        def _(rows=rows, line=line, index=index):
            keys, vals = key_value(index, k1_ref, v1_ref, v0_ref, far_ref)
            key_part, value_part, query_part = tile_grads(
                keys, vals, q_ref[rows, :], grad_ref[rows, :],
                log_ref[0, line, :], delta_ref[0, line, :], False,
            )
            dk[block_rows(index), :] += key_part
            dv[block_rows(index), :] += value_part
            dq[:, rows] += query_part

    far_back[0] = (dk[block_rows(0), :] * SCALE).astype(bf16)
    far_back[1] = dv[block_rows(0), :].astype(bf16)
    near_back[0] = (dk[pl.ds(BLK, 2 * BLK), :] * SCALE).astype(bf16)
    near_back[1] = dv[pl.ds(BLK, 2 * BLK), :].astype(bf16)


def backward_own_kernel(
    flags, q_ref, k_ref, v_ref, grad_ref, log_ref, dq_in, delta_ref, after,
    dq_ref, own_ref, dk, dv, dq,
):
    dk[...] = jnp.zeros_like(dk)
    dv[...] = jnp.zeros_like(dv)
    dq[...] = dq_in[...]
    for qb, o, index in OWN_TILES:
        rows = block_rows(qb)
        line = slice(qb, qb + 1)

        @pl.when(flags[qb * WIN + o] == 1)
        def _(rows=rows, line=line, index=index, o=o):
            held = block_rows(index)
            key_part, value_part, query_part = tile_grads(
                k_ref[held, :], v_ref[held, :], q_ref[rows, :], grad_ref[rows, :],
                log_ref[0, line, :], delta_ref[0, line, :], o == 0,
            )
            dk[held, :] += key_part
            dv[held, :] += value_part
            dq[:, rows] += query_part

    own_ref[0] = dk[...] * SCALE
    own_ref[1] = dv[...]
    dq_ref[...] = (dq[...] * SCALE).T.astype(bf16)


def finish_kernel(place, own_ref, near_ref, far_ref, after, key_ref, value_ref):
    for part, result in enumerate((key_ref, value_ref)):
        for block in range(2):
            rows = block_rows(block)
            total = own_ref[part, rows, :] + near_ref[part, rows, :].astype(f32)
            if block == 1:
                total += far_ref[part].astype(f32)
            result[rows, :] = total.astype(bf16)


def head(rows):
    return pl.BlockSpec((rows, HDIM), lambda h, *_: (0, h))


def head_pair(rows):
    return pl.BlockSpec((2, rows, HDIM), lambda h, *_: (0, 0, h))


HEAD_LINES = pl.BlockSpec((1, 2, BLK), lambda h, *_: (h, 0, 0))
ANY = pl.BlockSpec(memory_space=pl.ANY)
HEAD_TURNED = pl.BlockSpec((HDIM, 1024), lambda h, *_: (h, 0))


def shape(dims, dtype):
    return jax.ShapeDtypeStruct(dims, dtype)


WIDTH = 512
HEADS = WIDTH // HDIM
LINES = shape((HEADS, 2, BLK), f32)
TURNED = shape((WIDTH, 1024), f32)


def call(kernel, name, grid, ins, outs, out_shape, scratch, args):
    return pl.pallas_call(
        kernel,
        grid_spec=pltpu.PrefetchScalarGridSpec(
            num_scalar_prefetch=1,
            grid=grid,
            in_specs=ins,
            out_specs=outs,
            scratch_shapes=scratch,
        ),
        out_shape=out_shape,
        compiler_params=pltpu.CompilerParams(vmem_limit_bytes=64 << 20),
        cost_estimate=pl.CostEstimate(flops=1, bytes_accessed=1, transcendentals=0),
        name=name,
    )(*args)


def forward_own(flags, q, k, v, after):
    return call(
        forward_own_kernel, "forward_own", (HEADS,),
        [head(1024)] * 3 + [ANY],
        [HEAD_TURNED, HEAD_LINES, HEAD_LINES],
        [TURNED, LINES, LINES],
        [], (flags, q, k, v, after),
    )


def forward_behind(flags, q, near_k, near_v, edge_v, far, state, after):
    lines = pltpu.VMEM((2, BLK), f32)
    return call(
        forward_behind_kernel, "forward_behind", (HEADS,),
        [head(1024)] * 4 + [head_pair(512)]
        + [HEAD_TURNED, HEAD_LINES, HEAD_LINES, ANY],
        [head(1024), HEAD_TURNED, HEAD_LINES],
        [shape((1024, WIDTH), bf16), shape((WIDTH, 1024), bf16), LINES],
        [pltpu.VMEM((HDIM, 1024), f32), lines, lines],
        (flags, q, near_k, near_v, edge_v, far, *state, after),
    )


def backward_behind(
    flags, q, near_k, near_v, edge_v, far, out, grad, log_sum, after
):
    held = pltpu.VMEM((3 * BLK, HDIM), f32)
    return call(
        backward_behind_kernel, "backward_behind", (HEADS,),
        [head(1024)] * 4 + [head_pair(512)]
        + [head(1024), head(1024), HEAD_LINES, ANY],
        [head_pair(1024), head_pair(512), HEAD_TURNED, HEAD_LINES],
        [shape((2, 1024, WIDTH), bf16), shape((2, 512, WIDTH), bf16), TURNED, LINES],
        [held, held], (flags, q, near_k, near_v, edge_v, far, out, grad, log_sum, after),
    )


def backward_own(flags, q, k, v, grad, log_sum, dq, delta, after):
    held = pltpu.VMEM((2 * BLK, HDIM), f32)
    return call(
        backward_own_kernel, "backward_own", (HEADS,),
        [head(1024)] * 4 + [HEAD_LINES, HEAD_TURNED, HEAD_LINES, ANY],
        [head(1024), head_pair(1024)],
        [shape((1024, WIDTH), bf16), shape((2, 1024, WIDTH), f32)],
        [held, held, pltpu.VMEM((HDIM, 1024), f32)],
        (flags, q, k, v, grad, log_sum, dq, delta, after),
    )


def finish(place, own, near, far, after):
    return call(
        finish_kernel, "key_value_sum", (HEADS,),
        [head_pair(1024)] * 2 + [head_pair(512), ANY],
        [head(1024), head(1024)],
        [shape((1024, WIDTH), bf16)] * 2,
        [], (place, own, near, far, after),
    )


def pack_kernel(place, k_ref, v_ref, second_ref):
    second_ref[0] = k_ref[...]
    second_ref[1] = v_ref[...]


def pack(place, k, v):
    second = pl.BlockSpec((BLK, WIDTH), lambda i, place: (1, 0))
    return call(
        pack_kernel, "second_blocks", (1,), [second, second],
        pl.BlockSpec((2, BLK, WIDTH), lambda i, place: (0, 0, 0)),
        shape((2, BLK, WIDTH), bf16), [], (place, k, v),
    )


def nothing_kernel(*refs):
    pass


def together(values, after=()):
    return pl.pallas_call(
        nothing_kernel,
        in_specs=[ANY] * (len(values) + len(after)),
        out_specs=[ANY] * len(values),
        out_shape=[shape(value.shape, value.dtype) for value in values],
        input_output_aliases={index: index for index in range(len(values))},
        compiler_params=pltpu.CompilerParams(vmem_limit_bytes=64 << 20),
        name="order",
    )(*values, *after)


def grad_kernel(place, a_ref, b_ref, wa_ref, wb_ref, *rest):
    total = dot(a_ref[...], wa_ref[...], NT) + dot(b_ref[...], wb_ref[...], NT)
    if len(rest) == 3:
        total += rest[0][...]
    rest[-1][...] = total.astype(rest[-1].dtype)


def grad_terms(place, first, a, b, weight, before, after):
    tile = 512
    row = pl.BlockSpec((tile, 1024), lambda i, place: (i, 0))
    result = pl.BlockSpec((tile, 512), lambda i, place: (i, 0))

    def columns(flip):
        return pl.BlockSpec((512, 1024), lambda i, place: (0, place[0] ^ flip))

    more = [] if before is None else [before]
    return call(
        grad_kernel, "projection_backward", (1024 // tile,),
        [row, row, columns(first), columns(first + 1)] + [result] * len(more) + [ANY], result,
        shape((1024, 512), bf16 if more else f32), [], (place, a, b, weight, weight, *more, after),
    )


def weight_kernel(place, turned_ref, g0, g1, g2, g3, *outs):
    owner = place[0] ^ pl.program_id(0)
    y = owner % 2 * 2 + pl.program_id(1)
    for part, ref in enumerate((g0, g1, g2, g3)):
        for slot, out_ref in enumerate(outs):

            @pl.when((pl.program_id(0) == part) & ((y - place[1] + 3) % 4 == slot))
            def _(ref=ref, out_ref=out_ref, part=part):
                out_ref[part // 2] = dot(turned_ref[...], ref[...], NN).astype(bf16)


def weight_terms(place, turned, cotangents):
    def piece(part):
        return pl.BlockSpec(
            (1024, 512),
            lambda i, half, place: (
                0, jnp.where(i == part, half, jnp.where(i < part, 0, 1)),
            ),
        )

    return call(
        weight_kernel, "weight_gradient", (4, 2),
        [pl.BlockSpec((512, 1024), lambda i, half, place: (0, 0))] + [piece(p) for p in range(4)],
        [pl.BlockSpec((2, 512, 512), lambda i, half, place: (0, 0, 0))] * 4,
        [shape((2, 512, 512), bf16)] * 4, [], (place, turned, *cotangents),
    )


def over_y(parts):
    return [to_y(parts[s], s + 1) for s in (0, 2, 1)]


def pieces_kernel(place, a, b, c, d, after, *outs):
    for slot, out_ref in enumerate(outs):

        @pl.when(pl.program_id(0) == slot)
        def _(out_ref=out_ref):
            out_ref[...] = sum(ref[...].astype(f32) for ref in (a, b, c, d)).astype(bf16)


def pieces_by_z(place, terms, after):
    piece = pl.BlockSpec((2, 512, 128), lambda i, place: (0, 0, (place[2] + i + 1) % 4))
    return call(
        pieces_kernel, "weight_by_z", (4,), [piece] * 4 + [ANY],
        [pl.BlockSpec((2, 512, 128), lambda i, place: (0, 0, 0))] * 4,
        [shape((2, 512, 128), bf16)] * 4, [], (place, *terms, after),
    )


def weight_z_kernel(place, a_ref, b_ref, c_ref, d_ref, after, kept_ref, sent_ref):
    def total(index):
        return sum(ref[index].astype(f32) for ref in (a_ref, b_ref, c_ref, d_ref))

    kept = place[3] ^ (place[0] // 2)
    kept_ref[...] = total(kept)
    sent_ref[...] = total(1 - kept).astype(bf16)


def weight_z_sum(place, terms, after):
    whole = pl.BlockSpec((2, 512, 128), lambda i, place: (0, 0, 0))
    result = pl.BlockSpec((512, 128), lambda i, place: (0, 0))
    return call(
        weight_z_kernel, "weight_z_sum", (1,), [whole] * 4 + [ANY], [result] * 2,
        [shape((512, 128), f32), shape((512, 128), bf16)], [], (place, *terms, after),
    )


def copy_kernel(place, in_ref, *refs):
    refs[-1][...] = in_ref[...]


def far_columns(place, weight, after):
    return call(
        copy_kernel, "projection_far", (2,),
        [pl.BlockSpec((256, 2048), lambda i, place: (i, 1 - place[0] // 2)), ANY],
        pl.BlockSpec((256, 2048), lambda i, place: (i, 0)),
        shape((512, 2048), bf16), [], (place, weight, after),
    )


def core_kernel(place, own_ref, far_ref, far_rows, own_rows, after, out_ref):
    out_ref[0] = own_ref[...]
    out_ref[1] = far_ref[...]
    for part, rows in ((2, far_rows), (3, own_rows)):
        for half in range(2):
            out_ref[part, :, block_rows(half)] = rows[block_rows(half), :]


def for_core(place, weight, far_weight, far_attention, attention, after):
    rows = pl.BlockSpec((1024, 512), lambda i, place: (0, 0))
    return call(
        core_kernel, "for_core", (1,),
        [
            pl.BlockSpec((512, 1024), lambda i, place: (0, place[0] ^ 1)),
            pl.BlockSpec((512, 1024), lambda i, place: (0, 1 - place[0] % 2)),
            rows, rows, ANY,
        ],
        pl.BlockSpec((4, 512, 1024), lambda i, place: (0, 0, 0)),
        shape((4, 512, 1024), bf16), [],
        (place, weight, far_weight, far_attention, attention, after),
    )


def mix_kernel(place, own, core, far, far_core, w_own, w_far, w_core, after, out_ref):
    total = dot(own[...], w_own[...], NN) + dot(core[0], w_core[0], NN)
    total += dot(far[...], w_far[...], NN) + dot(far_core[0], w_core[1], NN)
    out_ref[...] = total.astype(bf16)


def mix(place, attention, far_attention, weight, far_weight, from_core, after):
    rows = pl.BlockSpec((512, 512), lambda i, place: (i, 0))
    return call(
        mix_kernel, "projection", (2,),
        [
            rows,
            pl.BlockSpec((1, 512, 512), lambda i, place: (3, 0, i)),
            rows,
            pl.BlockSpec((1, 512, 512), lambda i, place: (2, 0, i)),
            pl.BlockSpec((512, 1024), lambda i, place: (0, place[0])),
            pl.BlockSpec((512, 1024), lambda i, place: (0, place[0] % 2)),
            pl.BlockSpec((2, 512, 1024), lambda i, place: (0, 0, 0)),
            ANY,
        ],
        pl.BlockSpec((512, 1024), lambda i, place: (i, 0)),
        shape((1024, 1024), bf16), [],
        (place, attention, from_core, far_attention, from_core, weight, far_weight, from_core, after),
    )


def per_device(queries, keys, values, out_weight, out_grad, spans, pairs):
    ctx = lax.axis_index("ctx")
    tp = lax.axis_index("tp")
    place = jnp.stack([tp, ctx // 4 % 4, ctx % 4, ctx // 16]).astype(jnp.int32)

    far_grad = to_x_hi(out_grad)
    near_keys = along_ctx(keys, 1)
    near_pairs = [(s, s + 1) for s in range(31) if s != EDGE]
    near_values = lax.ppermute(values, "ctx", near_pairs + [(EDGE, 0)])
    core_grad = to_core(out_grad)
    far_moved = first_hop(pack(place, keys, values), 1)

    query_block = ctx * 2 + jnp.arange(2, dtype=jnp.int32)[:, None] + jnp.zeros((1, WIN), jnp.int32)
    key_block = query_block - jnp.arange(WIN, dtype=jnp.int32)[None, :]
    flags = block_rule(spans, pairs, query_block, key_block).astype(jnp.int32).reshape(-1)
    own_state = forward_own(flags, queries, keys, values, keys)
    terms = grad_terms(place, 0, out_grad, core_grad, out_weight, None, own_state[1])

    [far_moved] = together([far_moved], [terms])
    far = second_hop(far_moved, 1)
    [near_values] = together([near_values], [far_moved])
    edge_values = lax.ppermute(near_values, "ctx", [(0, EDGE + 1)])
    near_keys, far, far_grad, edge_values = together(
        [near_keys, far, far_grad, edge_values], [far_moved]
    )

    far_core_grad = to_core(far_grad)
    far_weight = to_x_hi(far_columns(place, out_weight, near_keys))
    behind = (flags, queries, near_keys, near_values, edge_values, far)
    attention, turned, log_sum = forward_behind(*behind, own_state, far)
    [far_core_grad] = together([far_core_grad], [log_sum])
    far_attention = to_x_hi(attention)
    weight_parts = weight_terms(place, turned, (out_grad, core_grad, far_grad, far_core_grad))
    weight_moved = over_y(weight_parts)
    attn_grad = grad_terms(place, 2, far_grad, far_core_grad, out_weight, terms, weight_parts[3])
    near_back, far_back, dq, delta = backward_behind(
        *behind, attention, attn_grad, log_sum, weight_parts[3]
    )
    query_grad, own = backward_own(
        flags, queries, keys, values, attn_grad, log_sum, dq, delta, delta
    )

    *weight_moved, near_back, far_back, far_attention, far_weight = together(
        [*weight_moved, near_back, far_back, far_attention, far_weight], [own]
    )
    near_back = along_ctx(near_back, -1)
    back_moved = first_hop(far_back, -1)
    from_core = to_core(
        for_core(place, out_weight, far_weight, far_attention, attention, weight_moved[0])
    )
    weight_pieces = pieces_by_z(place, [weight_parts[3], *weight_moved], weight_moved[0])
    back_moved, from_core = together([back_moved, from_core], [weight_pieces[3]])
    far_back = second_hop(back_moved, -1)
    weight_moved = [to_z(weight_pieces[s], s + 1) for s in (0, 2, 1)]
    mixed = mix(place, attention, far_attention, out_weight, far_weight, from_core, back_moved)
    near_back, far_back, *weight_moved = together([near_back, far_back, *weight_moved], [mixed])
    kept, sent = weight_z_sum(place, [weight_pieces[3], *weight_moved], near_back)
    weight_grad = kept + to_x_lo(sent).astype(f32)
    key_grad, value_grad = finish(place, own, near_back, far_back, kept)
    return (mixed, query_grad, key_grad, value_grad, weight_grad)


def solution(mesh):
    placed = (
        P("ctx", "tp"),
        P("ctx", "tp"),
        P("ctx", "tp"),
        P("tp", None),
        P("ctx", "tp"),
        P(),
        P(),
    )
    return jax.shard_map(
        per_device,
        mesh=mesh,
        in_specs=placed,
        out_specs=(P("ctx", "tp"), P("ctx", "tp"), P("ctx", "tp"), P("ctx", "tp"), P("tp", "ctx")),
        check_vma=False,
    )
```

```python
import functools
import math

import jax
import jax.numpy as jnp
from jax import lax
from jax.experimental import pallas as pl
from jax.experimental.pallas import tpu as pltpu
from jax.sharding import PartitionSpec as P

HDIM = 128
BLK = 512
WIN = 4
SCALE = 1.0 / math.sqrt(HDIM)
SCALE2 = SCALE * math.log2(math.e)
AXES = ("ctx", "tp")
NT = (((1,), (1,)), ((), ()))
NN = (((1,), (0,)), ((), ()))
f32 = jnp.float32
bf16 = jnp.bfloat16


def places():
    for x_lo in range(2):
        for y in range(4):
            for z in range(4):
                for x_hi in range(2):
                    for core in range(2):
                        yield x_lo, y, z, x_hi, core


def number(x_lo, y, z, x_hi, core):
    return ((x_lo * 4 + y) * 4 + z) * 4 + x_hi * 2 + core


def move(value, target):
    pairs = [(number(*place), number(*target(*place))) for place in places()]
    return lax.ppermute(value, AXES, pairs)


def to_core(value):
    return move(value, lambda x_lo, y, z, x_hi, core: (x_lo, y, z, x_hi, 1 - core))


def to_x_hi(value):
    return move(value, lambda x_lo, y, z, x_hi, core: (x_lo, y, z, 1 - x_hi, core))


def to_x_lo(value):
    return move(value, lambda x_lo, y, z, x_hi, core: (1 - x_lo, y, z, x_hi, core))


def to_y(value, steps):
    return move(value, lambda x_lo, y, z, x_hi, core: (x_lo, (y + steps) % 4, z, x_hi, core))


def to_z(value, steps):
    return move(value, lambda x_lo, y, z, x_hi, core: (x_lo, y, (z + steps) % 4, x_hi, core))


EDGE = 15


def along_ctx(value, steps):
    pairs = [(s, s + steps) for s in range(32) if 0 <= s + steps < 32]
    return lax.ppermute(value, "ctx", pairs)


def middle(source, sign):
    return source // 4 * 4 + (source % 4 - sign) % 4


def two_pairs(sign):
    sources = [s for s in range(32) if 0 <= s + 2 * sign < 32]
    return [(s, middle(s, sign), s + 2 * sign) for s in sources]


def first_hop(value, sign):
    return lax.ppermute(value, "ctx", [(s, m) for s, m, _ in two_pairs(sign)])


def second_hop(value, sign):
    return lax.ppermute(value, "ctx", [(m, t) for _, m, t in two_pairs(sign)])


def block_rule(spans, pairs, query_block, key_block):
    listed = jnp.any(
        (pairs[:, 0] == query_block[..., None]) & (pairs[:, 1] == key_block[..., None]), axis=-1
    )
    span_lower = spans[:, 0]
    span_upper = spans[:, 0] + spans[:, 1]
    query_inside = (span_lower <= query_block[..., None]) & (query_block[..., None] < span_upper)
    key_inside = (span_lower <= key_block[..., None]) & (key_block[..., None] < span_upper)
    same = jnp.any(query_inside & key_inside, axis=-1)
    reach = (query_block - key_block >= 0) & (query_block - key_block < WIN)
    return listed & same & reach


def dot(a, b, dims):
    return lax.dot_general(a, b, dims, preferred_element_type=f32)


def causal():
    key_row = lax.broadcasted_iota(jnp.int32, (BLK, BLK), 0)
    query_column = lax.broadcasted_iota(jnp.int32, (BLK, BLK), 1)
    return key_row <= query_column


def block_rows(index):
    return pl.ds(index * BLK, BLK)


OWN_TILES = ((0, 0, 0), (1, 0, 1), (1, 1, 0))
BEHIND_TILES = ((0, 3, 0), (0, 2, 1), (0, 1, 2), (1, 3, 1), (1, 2, 2))


def key_value(index, near_k, near_v, edge_v, far):
    if index == 0:
        return far[0], far[1]
    rows = block_rows(index - 1)
    return near_k[rows, :], near_v[rows, :] + edge_v[rows, :]


def absorb(keys, vals, query, top, total, acc, rows):
    s = dot(keys, query, NT)
    old = top
    m = jnp.maximum(old, jnp.max(s, axis=0, keepdims=True))
    p = jnp.exp2(s * SCALE2 - m * SCALE2)
    fix = jnp.exp2((old - m) * SCALE2)
    part = dot(vals.T, p.astype(bf16), NN)
    acc[:, rows] = acc[:, rows] * fix + part
    return m, total * fix + jnp.sum(p, axis=0, keepdims=True)


def forward_own_kernel(flags, q_ref, k_ref, v_ref, after, acc, top, total):
    for qb, o, index in OWN_TILES:
        rows = block_rows(qb)
        line = slice(qb, qb + 1)

        def diagonal(rows=rows, line=line):
            s = jnp.where(causal(), dot(k_ref[rows, :], q_ref[rows, :], NT), -jnp.inf)
            m = jnp.max(s, axis=0, keepdims=True)
            p = jnp.exp2(s * SCALE2 - m * SCALE2)
            acc[:, rows] = dot(v_ref[rows, :].T, p.astype(bf16), NN)
            top[0, line, :] = m
            total[0, line, :] = jnp.sum(p, axis=0, keepdims=True)

        def nothing(rows=rows, line=line):
            acc[:, rows] = jnp.zeros((HDIM, BLK), f32)
            top[0, line, :] = jnp.zeros((1, BLK), f32)
            total[0, line, :] = jnp.ones((1, BLK), f32)

        def tile(rows=rows, line=line, index=index):
            held = block_rows(index)
            top[0, line, :], total[0, line, :] = absorb(
                k_ref[held, :], v_ref[held, :], q_ref[rows, :],
                top[0, line, :], total[0, line, :], acc, rows,
            )

        listed = flags[qb * WIN + o] == 1
        if o == 0:
            pl.when(listed)(diagonal)
            pl.when(jnp.logical_not(listed))(nothing)
        else:
            pl.when(listed)(tile)


def forward_behind_kernel(
    flags, q_ref, k1_ref, v1_ref, v0_ref, far_ref, acc_in, top_in, total_in,
    after, out_ref, turned_ref, log_ref, acc, top, total,
):
    acc[...] = acc_in[...]
    top[...] = top_in[0]
    total[...] = total_in[0]
    for qb, o, index in BEHIND_TILES:
        rows = block_rows(qb)
        line = slice(qb, qb + 1)

        @pl.when(flags[qb * WIN + o] == 1)
        def _(rows=rows, line=line, index=index):
            keys, vals = key_value(index, k1_ref, v1_ref, v0_ref, far_ref)
            top[line, :], total[line, :] = absorb(
                keys, vals, q_ref[rows, :], top[line, :], total[line, :], acc, rows
            )

    for qb in range(2):
        rows = block_rows(qb)
        result = acc[:, rows] * (1.0 / total[qb : qb + 1, :])
        turned_ref[:, rows] = result.astype(bf16)
        out_ref[rows, :] = result.T.astype(bf16)
    log_ref[0] = top[...] * SCALE2 + jnp.log2(total[...])


def tile_grads(keys, vals, query, grad, log_sum, delta, diagonal):
    p = jnp.exp2(dot(keys, query, NT) * SCALE2 - log_sum)
    if diagonal:
        p = jnp.where(causal(), p, 0.0)
    value_part = dot(p.astype(bf16), grad, NN)
    dp = dot(vals, grad, NT)
    ds = (p * (dp - delta)).astype(bf16)
    return dot(ds, query, NN), value_part, dot(keys.T, ds, NN)


def backward_behind_kernel(
    flags, q_ref, k1_ref, v1_ref, v0_ref, far_ref, out_ref, grad_ref, log_ref,
    after, near_back, far_back, dq, delta_ref, dk, dv,
):
    dk[...] = jnp.zeros_like(dk)
    dv[...] = jnp.zeros_like(dv)
    dq[...] = jnp.zeros_like(dq)
    product = grad_ref[...].astype(f32) * out_ref[...].astype(f32)
    delta = jnp.sum(product.T, axis=0, keepdims=True)
    for qb in range(2):
        delta_ref[0, qb : qb + 1, :] = delta[:, qb * BLK : (qb + 1) * BLK]
    for qb, o, index in BEHIND_TILES:
        rows = block_rows(qb)
        line = slice(qb, qb + 1)

        @pl.when(flags[qb * WIN + o] == 1)
        def _(rows=rows, line=line, index=index):
            keys, vals = key_value(index, k1_ref, v1_ref, v0_ref, far_ref)
            key_part, value_part, query_part = tile_grads(
                keys, vals, q_ref[rows, :], grad_ref[rows, :],
                log_ref[0, line, :], delta_ref[0, line, :], False,
            )
            dk[block_rows(index), :] += key_part
            dv[block_rows(index), :] += value_part
            dq[:, rows] += query_part

    far_back[0] = (dk[block_rows(0), :] * SCALE).astype(bf16)
    far_back[1] = dv[block_rows(0), :].astype(bf16)
    near_back[0] = (dk[pl.ds(BLK, 2 * BLK), :] * SCALE).astype(bf16)
    near_back[1] = dv[pl.ds(BLK, 2 * BLK), :].astype(bf16)


def backward_own_kernel(
    flags, q_ref, k_ref, v_ref, grad_ref, log_ref, dq_in, delta_ref, after,
    dq_ref, own_ref, dk, dv, dq,
):
    dk[...] = jnp.zeros_like(dk)
    dv[...] = jnp.zeros_like(dv)
    dq[...] = dq_in[...]
    for qb, o, index in OWN_TILES:
        rows = block_rows(qb)
        line = slice(qb, qb + 1)

        @pl.when(flags[qb * WIN + o] == 1)
        def _(rows=rows, line=line, index=index, o=o):
            held = block_rows(index)
            key_part, value_part, query_part = tile_grads(
                k_ref[held, :], v_ref[held, :], q_ref[rows, :], grad_ref[rows, :],
                log_ref[0, line, :], delta_ref[0, line, :], o == 0,
            )
            dk[held, :] += key_part
            dv[held, :] += value_part
            dq[:, rows] += query_part

    own_ref[0] = (dk[...] * SCALE).astype(bf16)
    own_ref[1] = dv[...].astype(bf16)
    dq_ref[...] = (dq[...] * SCALE).T.astype(bf16)


def finish_kernel(place, own_ref, near_ref, far_ref, after, key_ref, value_ref):
    for part, result in enumerate((key_ref, value_ref)):
        for block in range(2):
            rows = block_rows(block)
            total = own_ref[part, rows, :].astype(f32) + near_ref[part, rows, :].astype(f32)
            if block == 1:
                total += far_ref[part].astype(f32)
            result[rows, :] = total.astype(bf16)


def head(rows):
    return pl.BlockSpec((rows, HDIM), lambda h, *_: (0, h))


def head_pair(rows):
    return pl.BlockSpec((2, rows, HDIM), lambda h, *_: (0, 0, h))


HEAD_LINES = pl.BlockSpec((1, 2, BLK), lambda h, *_: (h, 0, 0))
ANY = pl.BlockSpec(memory_space=pl.ANY)
HEAD_TURNED = pl.BlockSpec((HDIM, 1024), lambda h, *_: (h, 0))


def shape(dims, dtype):
    return jax.ShapeDtypeStruct(dims, dtype)


WIDTH = 512
HEADS = WIDTH // HDIM
LINES = shape((HEADS, 2, BLK), f32)
TURNED = shape((WIDTH, 1024), f32)


def call(kernel, name, grid, ins, outs, out_shape, scratch, args):
    return pl.pallas_call(
        kernel,
        grid_spec=pltpu.PrefetchScalarGridSpec(
            num_scalar_prefetch=1,
            grid=grid,
            in_specs=ins,
            out_specs=outs,
            scratch_shapes=scratch,
        ),
        out_shape=out_shape,
        compiler_params=pltpu.CompilerParams(vmem_limit_bytes=64 << 20),
        cost_estimate=pl.CostEstimate(flops=1, bytes_accessed=1, transcendentals=0),
        name=name,
    )(*args)


def forward_own(flags, q, k, v, after):
    return call(
        forward_own_kernel, "forward_own", (HEADS,),
        [head(1024)] * 3 + [ANY],
        [HEAD_TURNED, HEAD_LINES, HEAD_LINES],
        [TURNED, LINES, LINES],
        [], (flags, q, k, v, after),
    )


def forward_behind(flags, q, near_k, near_v, edge_v, far, state, after):
    lines = pltpu.VMEM((2, BLK), f32)
    return call(
        forward_behind_kernel, "forward_behind", (HEADS,),
        [head(1024)] * 4 + [head_pair(512)]
        + [HEAD_TURNED, HEAD_LINES, HEAD_LINES, ANY],
        [head(1024), HEAD_TURNED, HEAD_LINES],
        [shape((1024, WIDTH), bf16), shape((WIDTH, 1024), bf16), LINES],
        [pltpu.VMEM((HDIM, 1024), f32), lines, lines],
        (flags, q, near_k, near_v, edge_v, far, *state, after),
    )


def backward_behind(
    flags, q, near_k, near_v, edge_v, far, out, grad, log_sum, after
):
    held = pltpu.VMEM((3 * BLK, HDIM), f32)
    return call(
        backward_behind_kernel, "backward_behind", (HEADS,),
        [head(1024)] * 4 + [head_pair(512)]
        + [head(1024), head(1024), HEAD_LINES, ANY],
        [head_pair(1024), head_pair(512), HEAD_TURNED, HEAD_LINES],
        [shape((2, 1024, WIDTH), bf16), shape((2, 512, WIDTH), bf16), TURNED, LINES],
        [held, held], (flags, q, near_k, near_v, edge_v, far, out, grad, log_sum, after),
    )


def backward_own(flags, q, k, v, grad, log_sum, dq, delta, after):
    held = pltpu.VMEM((2 * BLK, HDIM), f32)
    return call(
        backward_own_kernel, "backward_own", (HEADS,),
        [head(1024)] * 4 + [HEAD_LINES, HEAD_TURNED, HEAD_LINES, ANY],
        [head(1024), head_pair(1024)],
        [shape((1024, WIDTH), bf16), shape((2, 1024, WIDTH), bf16)],
        [held, held, pltpu.VMEM((HDIM, 1024), f32)],
        (flags, q, k, v, grad, log_sum, dq, delta, after),
    )


def finish(place, own, near, far, after):
    return call(
        finish_kernel, "key_value_sum", (HEADS,),
        [head_pair(1024)] * 2 + [head_pair(512), ANY],
        [head(1024), head(1024)],
        [shape((1024, WIDTH), bf16)] * 2,
        [], (place, own, near, far, after),
    )


def pack_kernel(place, k_ref, v_ref, second_ref):
    second_ref[0] = k_ref[...]
    second_ref[1] = v_ref[...]


def pack(place, k, v):
    second = pl.BlockSpec((BLK, WIDTH), lambda i, place: (1, 0))
    return call(
        pack_kernel, "second_blocks", (1,), [second, second],
        pl.BlockSpec((2, BLK, WIDTH), lambda i, place: (0, 0, 0)),
        shape((2, BLK, WIDTH), bf16), [], (place, k, v),
    )


def nothing_kernel(*refs):
    pass


def together(values, after=()):
    return pl.pallas_call(
        nothing_kernel,
        in_specs=[ANY] * (len(values) + len(after)),
        out_specs=[ANY] * len(values),
        out_shape=[shape(value.shape, value.dtype) for value in values],
        input_output_aliases={index: index for index in range(len(values))},
        compiler_params=pltpu.CompilerParams(vmem_limit_bytes=64 << 20),
        name="order",
    )(*values, *after)


def grad_kernel(place, a_ref, b_ref, wa_ref, wb_ref, *rest):
    total = dot(a_ref[...], wa_ref[...], NT) + dot(b_ref[...], wb_ref[...], NT)
    if len(rest) == 3:
        total += rest[0][...]
    rest[-1][...] = total.astype(rest[-1].dtype)


def grad_terms(place, first, a, b, weight, before, after):
    tile = 512
    row = pl.BlockSpec((tile, 1024), lambda i, place: (i, 0))
    result = pl.BlockSpec((tile, 512), lambda i, place: (i, 0))

    def columns(flip):
        return pl.BlockSpec((512, 1024), lambda i, place: (0, place[0] ^ flip))

    more = [] if before is None else [before]
    return call(
        grad_kernel, "projection_backward", (1024 // tile,),
        [row, row, columns(first), columns(first + 1)] + [result] * len(more) + [ANY], result,
        shape((1024, 512), bf16 if more else f32), [], (place, a, b, weight, weight, *more, after),
    )


def weight_kernel(place, turned_ref, g0, g1, g2, g3, *outs):
    owner = place[0] ^ pl.program_id(0)
    y = owner % 2 * 2 + pl.program_id(1)
    for part, ref in enumerate((g0, g1, g2, g3)):
        for slot, out_ref in enumerate(outs):

            @pl.when((pl.program_id(0) == part) & ((y - place[1] + 3) % 4 == slot))
            def _(ref=ref, out_ref=out_ref, part=part):
                out_ref[part // 2] = dot(turned_ref[...], ref[...], NN).astype(bf16)


def weight_terms(place, turned, cotangents):
    def piece(part):
        return pl.BlockSpec(
            (1024, 512),
            lambda i, half, place: (
                0, jnp.where(i == part, half, jnp.where(i < part, 0, 1)),
            ),
        )

    return call(
        weight_kernel, "weight_gradient", (4, 2),
        [pl.BlockSpec((512, 1024), lambda i, half, place: (0, 0))] + [piece(p) for p in range(4)],
        [pl.BlockSpec((2, 512, 512), lambda i, half, place: (0, 0, 0))] * 4,
        [shape((2, 512, 512), bf16)] * 4, [], (place, turned, *cotangents),
    )


def over_y(parts):
    return [to_y(parts[s], s + 1) for s in (0, 2, 1)]


def pieces_kernel(place, a, b, c, d, after, *outs):
    for slot, out_ref in enumerate(outs):

        @pl.when(pl.program_id(0) == slot)
        def _(out_ref=out_ref):
            out_ref[...] = sum(ref[...].astype(f32) for ref in (a, b, c, d)).astype(bf16)


def pieces_by_z(place, terms, after):
    piece = pl.BlockSpec((2, 512, 128), lambda i, place: (0, 0, (place[2] + i + 1) % 4))
    return call(
        pieces_kernel, "weight_by_z", (4,), [piece] * 4 + [ANY],
        [pl.BlockSpec((2, 512, 128), lambda i, place: (0, 0, 0))] * 4,
        [shape((2, 512, 128), bf16)] * 4, [], (place, *terms, after),
    )


def weight_z_kernel(place, a_ref, b_ref, c_ref, d_ref, after, kept_ref, sent_ref):
    def total(index):
        return sum(ref[index].astype(f32) for ref in (a_ref, b_ref, c_ref, d_ref))

    kept = place[3] ^ (place[0] // 2)
    kept_ref[...] = total(kept)
    sent_ref[...] = total(1 - kept).astype(bf16)


def weight_z_sum(place, terms, after):
    whole = pl.BlockSpec((2, 512, 128), lambda i, place: (0, 0, 0))
    result = pl.BlockSpec((512, 128), lambda i, place: (0, 0))
    return call(
        weight_z_kernel, "weight_z_sum", (1,), [whole] * 4 + [ANY], [result] * 2,
        [shape((512, 128), f32), shape((512, 128), bf16)], [], (place, *terms, after),
    )


def copy_kernel(place, in_ref, *refs):
    refs[-1][...] = in_ref[...]


def far_columns(place, weight, after):
    return call(
        copy_kernel, "projection_far", (2,),
        [pl.BlockSpec((256, 2048), lambda i, place: (i, 1 - place[0] // 2)), ANY],
        pl.BlockSpec((256, 2048), lambda i, place: (i, 0)),
        shape((512, 2048), bf16), [], (place, weight, after),
    )


def core_kernel(place, own_ref, far_ref, far_rows, own_rows, after, out_ref):
    out_ref[0] = own_ref[...]
    out_ref[1] = far_ref[...]
    for part, rows in ((2, far_rows), (3, own_rows)):
        for half in range(2):
            out_ref[part, :, block_rows(half)] = rows[block_rows(half), :]


def for_core(place, weight, far_weight, far_attention, attention, after):
    rows = pl.BlockSpec((1024, 512), lambda i, place: (0, 0))
    return call(
        core_kernel, "for_core", (1,),
        [
            pl.BlockSpec((512, 1024), lambda i, place: (0, place[0] ^ 1)),
            pl.BlockSpec((512, 1024), lambda i, place: (0, 1 - place[0] % 2)),
            rows, rows, ANY,
        ],
        pl.BlockSpec((4, 512, 1024), lambda i, place: (0, 0, 0)),
        shape((4, 512, 1024), bf16), [],
        (place, weight, far_weight, far_attention, attention, after),
    )


def mix_kernel(place, own, core, far, far_core, w_own, w_far, w_core, after, out_ref):
    total = dot(own[...], w_own[...], NN) + dot(core[0], w_core[0], NN)
    total += dot(far[...], w_far[...], NN) + dot(far_core[0], w_core[1], NN)
    out_ref[...] = total.astype(bf16)


def mix(place, attention, far_attention, weight, far_weight, from_core, after):
    rows = pl.BlockSpec((512, 512), lambda i, place: (i, 0))
    return call(
        mix_kernel, "projection", (2,),
        [
            rows,
            pl.BlockSpec((1, 512, 512), lambda i, place: (3, 0, i)),
            rows,
            pl.BlockSpec((1, 512, 512), lambda i, place: (2, 0, i)),
            pl.BlockSpec((512, 1024), lambda i, place: (0, place[0])),
            pl.BlockSpec((512, 1024), lambda i, place: (0, place[0] % 2)),
            pl.BlockSpec((2, 512, 1024), lambda i, place: (0, 0, 0)),
            ANY,
        ],
        pl.BlockSpec((512, 1024), lambda i, place: (i, 0)),
        shape((1024, 1024), bf16), [],
        (place, attention, from_core, far_attention, from_core, weight, far_weight, from_core, after),
    )


def per_device(queries, keys, values, out_weight, out_grad, spans, pairs):
    ctx = lax.axis_index("ctx")
    tp = lax.axis_index("tp")
    place = jnp.stack([tp, ctx // 4 % 4, ctx % 4, ctx // 16]).astype(jnp.int32)

    far_grad = to_x_hi(out_grad)
    near_keys = along_ctx(keys, 1)
    near_pairs = [(s, s + 1) for s in range(31) if s != EDGE]
    near_values = lax.ppermute(values, "ctx", near_pairs + [(EDGE, 0)])
    core_grad = to_core(out_grad)
    far_moved = first_hop(pack(place, keys, values), 1)

    query_block = ctx * 2 + jnp.arange(2, dtype=jnp.int32)[:, None] + jnp.zeros((1, WIN), jnp.int32)
    key_block = query_block - jnp.arange(WIN, dtype=jnp.int32)[None, :]
    flags = block_rule(spans, pairs, query_block, key_block).astype(jnp.int32).reshape(-1)
    own_state = forward_own(flags, queries, keys, values, keys)
    far_weight = far_columns(place, out_weight, own_state[1])
    terms = grad_terms(place, 0, out_grad, core_grad, out_weight, None, far_weight)

    [far_moved] = together([far_moved], [terms])
    far = second_hop(far_moved, 1)
    [near_values] = together([near_values], [far_moved])
    edge_values = lax.ppermute(near_values, "ctx", [(0, EDGE + 1)])
    near_keys, far, far_grad, edge_values, far_weight = together(
        [near_keys, far, far_grad, edge_values, far_weight], [far_moved]
    )

    far_core_grad = to_core(far_grad)
    far_weight = to_x_hi(far_weight)
    behind = (flags, queries, near_keys, near_values, edge_values, far)
    attention, turned, log_sum = forward_behind(*behind, own_state, far)
    [far_core_grad] = together([far_core_grad], [log_sum])
    far_attention = to_x_hi(attention)
    weight_parts = weight_terms(place, turned, (out_grad, core_grad, far_grad, far_core_grad))
    weight_moved = over_y(weight_parts)
    attn_grad = grad_terms(place, 2, far_grad, far_core_grad, out_weight, terms, weight_parts[3])
    near_back, far_back, dq, delta = backward_behind(
        *behind, attention, attn_grad, log_sum, weight_parts[3]
    )
    query_grad, own = backward_own(
        flags, queries, keys, values, attn_grad, log_sum, dq, delta, delta
    )

    far_attention, far_weight = together([far_attention, far_weight], [own])
    from_core = for_core(place, out_weight, far_weight, far_attention, attention, own)

    *weight_moved, near_back, far_back, from_core = together(
        [*weight_moved, near_back, far_back, from_core]
    )
    near_back = along_ctx(near_back, -1)
    back_moved = first_hop(far_back, -1)
    from_core = to_core(from_core)
    weight_pieces = pieces_by_z(place, [weight_parts[3], *weight_moved], weight_moved[0])
    weight_moved = [to_z(weight_pieces[s], s + 1) for s in (0, 2, 1)]
    mixed = mix(
        place, attention, far_attention, out_weight, far_weight, from_core, weight_pieces[3]
    )
    [back_moved] = together([back_moved], [mixed])
    far_back = second_hop(back_moved, -1)
    kept, sent = weight_z_sum(place, [weight_pieces[3], *weight_moved], back_moved)
    weight_grad = kept + to_x_lo(sent).astype(f32)
    key_grad, value_grad = finish(place, own, near_back, far_back, kept)
    return (mixed, query_grad, key_grad, value_grad, weight_grad)


def solution(mesh):
    placed = (
        P("ctx", "tp"),
        P("ctx", "tp"),
        P("ctx", "tp"),
        P("tp", None),
        P("ctx", "tp"),
        P(),
        P(),
    )
    return jax.shard_map(
        per_device,
        mesh=mesh,
        in_specs=placed,
        out_specs=(P("ctx", "tp"), P("ctx", "tp"), P("ctx", "tp"), P("ctx", "tp"), P("tp", "ctx")),
        check_vma=False,
    )
```

```python
import functools
import math

import jax
import jax.numpy as jnp
from jax import lax
from jax.experimental import pallas as pl
from jax.experimental.pallas import tpu as pltpu
from jax.sharding import PartitionSpec as P

HDIM = 128
BLK = 512
WIN = 4
SCALE = 1.0 / math.sqrt(HDIM)
SCALE2 = SCALE * math.log2(math.e)
AXES = ("ctx", "tp")
NT = (((1,), (1,)), ((), ()))
NN = (((1,), (0,)), ((), ()))
f32 = jnp.float32
bf16 = jnp.bfloat16


def places():
    for x_lo in range(2):
        for y in range(4):
            for z in range(4):
                for x_hi in range(2):
                    for core in range(2):
                        yield x_lo, y, z, x_hi, core


def number(x_lo, y, z, x_hi, core):
    return ((x_lo * 4 + y) * 4 + z) * 4 + x_hi * 2 + core


def move(value, target):
    pairs = [(number(*place), number(*target(*place))) for place in places()]
    return lax.ppermute(value, AXES, pairs)


def to_core(value):
    return move(value, lambda x_lo, y, z, x_hi, core: (x_lo, y, z, x_hi, 1 - core))


def to_x_hi(value):
    return move(value, lambda x_lo, y, z, x_hi, core: (x_lo, y, z, 1 - x_hi, core))


def to_x_lo(value):
    return move(value, lambda x_lo, y, z, x_hi, core: (1 - x_lo, y, z, x_hi, core))


def to_y(value, steps):
    return move(value, lambda x_lo, y, z, x_hi, core: (x_lo, (y + steps) % 4, z, x_hi, core))


def to_z(value, steps):
    return move(value, lambda x_lo, y, z, x_hi, core: (x_lo, y, (z + steps) % 4, x_hi, core))


EDGE = 15


def along_ctx(value, steps):
    pairs = [(s, s + steps) for s in range(32) if 0 <= s + steps < 32]
    return lax.ppermute(value, "ctx", pairs)


def middle(source, sign):
    return source // 4 * 4 + (source % 4 - sign) % 4


def two_pairs(sign):
    sources = [s for s in range(32) if 0 <= s + 2 * sign < 32]
    return [(s, middle(s, sign), s + 2 * sign) for s in sources]


def first_hop(value, sign):
    return lax.ppermute(value, "ctx", [(s, m) for s, m, _ in two_pairs(sign)])


def second_hop(value, sign):
    return lax.ppermute(value, "ctx", [(m, t) for _, m, t in two_pairs(sign)])


def block_rule(spans, pairs, query_block, key_block):
    listed = jnp.any(
        (pairs[:, 0] == query_block[..., None]) & (pairs[:, 1] == key_block[..., None]), axis=-1
    )
    span_lower = spans[:, 0]
    span_upper = spans[:, 0] + spans[:, 1]
    query_inside = (span_lower <= query_block[..., None]) & (query_block[..., None] < span_upper)
    key_inside = (span_lower <= key_block[..., None]) & (key_block[..., None] < span_upper)
    same = jnp.any(query_inside & key_inside, axis=-1)
    reach = (query_block - key_block >= 0) & (query_block - key_block < WIN)
    return listed & same & reach


def dot(a, b, dims):
    return lax.dot_general(a, b, dims, preferred_element_type=f32)


def causal():
    key_row = lax.broadcasted_iota(jnp.int32, (BLK, BLK), 0)
    query_column = lax.broadcasted_iota(jnp.int32, (BLK, BLK), 1)
    return key_row <= query_column


def block_rows(index):
    return pl.ds(index * BLK, BLK)


OWN_TILES = ((0, 0, 0), (1, 0, 1), (1, 1, 0))
BEHIND_TILES = ((0, 3, 0), (0, 2, 1), (0, 1, 2), (1, 3, 1), (1, 2, 2))


def key_value(index, near_k, near_v, edge_v, far):
    if index == 0:
        return far[0], far[1]
    rows = block_rows(index - 1)
    return near_k[rows, :], near_v[rows, :] + edge_v[rows, :]


def absorb(keys, vals, query, top, total, acc, rows):
    s = dot(keys, query, NT)
    old = top
    m = jnp.maximum(old, jnp.max(s, axis=0, keepdims=True))
    p = jnp.exp2(s * SCALE2 - m * SCALE2)
    fix = jnp.exp2((old - m) * SCALE2)
    part = dot(vals.T, p.astype(bf16), NN)
    acc[:, rows] = acc[:, rows] * fix + part
    return m, total * fix + jnp.sum(p, axis=0, keepdims=True)


def forward_own_kernel(flags, q_ref, k_ref, v_ref, after, acc, top, total):
    for qb, o, index in OWN_TILES:
        rows = block_rows(qb)
        line = slice(qb, qb + 1)

        def diagonal(rows=rows, line=line):
            s = jnp.where(causal(), dot(k_ref[rows, :], q_ref[rows, :], NT), -jnp.inf)
            m = jnp.max(s, axis=0, keepdims=True)
            p = jnp.exp2(s * SCALE2 - m * SCALE2)
            acc[:, rows] = dot(v_ref[rows, :].T, p.astype(bf16), NN)
            top[0, line, :] = m
            total[0, line, :] = jnp.sum(p, axis=0, keepdims=True)

        def nothing(rows=rows, line=line):
            acc[:, rows] = jnp.zeros((HDIM, BLK), f32)
            top[0, line, :] = jnp.zeros((1, BLK), f32)
            total[0, line, :] = jnp.ones((1, BLK), f32)

        def tile(rows=rows, line=line, index=index):
            held = block_rows(index)
            top[0, line, :], total[0, line, :] = absorb(
                k_ref[held, :], v_ref[held, :], q_ref[rows, :],
                top[0, line, :], total[0, line, :], acc, rows,
            )

        listed = flags[qb * WIN + o] == 1
        if o == 0:
            pl.when(listed)(diagonal)
            pl.when(jnp.logical_not(listed))(nothing)
        else:
            pl.when(listed)(tile)


def forward_behind_kernel(
    flags, q_ref, k1_ref, v1_ref, v0_ref, far_ref, acc_in, top_in, total_in,
    after, out_ref, turned_ref, log_ref, acc, top, total,
):
    acc[...] = acc_in[...]
    top[...] = top_in[0]
    total[...] = total_in[0]
    for qb, o, index in BEHIND_TILES:
        rows = block_rows(qb)
        line = slice(qb, qb + 1)

        @pl.when(flags[qb * WIN + o] == 1)
        def _(rows=rows, line=line, index=index):
            keys, vals = key_value(index, k1_ref, v1_ref, v0_ref, far_ref)
            top[line, :], total[line, :] = absorb(
                keys, vals, q_ref[rows, :], top[line, :], total[line, :], acc, rows
            )

    for qb in range(2):
        rows = block_rows(qb)
        result = acc[:, rows] * (1.0 / total[qb : qb + 1, :])
        turned_ref[:, rows] = result.astype(bf16)
        out_ref[rows, :] = result.T.astype(bf16)
    log_ref[0] = top[...] * SCALE2 + jnp.log2(total[...])


def tile_grads(keys, vals, query, grad, log_sum, delta, diagonal):
    p = jnp.exp2(dot(keys, query, NT) * SCALE2 - log_sum)
    if diagonal:
        p = jnp.where(causal(), p, 0.0)
    value_part = dot(p.astype(bf16), grad, NN)
    dp = dot(vals, grad, NT)
    ds = (p * (dp - delta)).astype(bf16)
    return dot(ds, query, NN), value_part, dot(keys.T, ds, NN)


def backward_behind_kernel(
    flags, q_ref, k1_ref, v1_ref, v0_ref, far_ref, out_ref, grad_ref, log_ref,
    after, near_back, far_back, dq, delta_ref, dk, dv,
):
    dk[...] = jnp.zeros_like(dk)
    dv[...] = jnp.zeros_like(dv)
    dq[...] = jnp.zeros_like(dq)
    product = grad_ref[...].astype(f32) * out_ref[...].astype(f32)
    delta = jnp.sum(product.T, axis=0, keepdims=True)
    for qb in range(2):
        delta_ref[0, qb : qb + 1, :] = delta[:, qb * BLK : (qb + 1) * BLK]
    for qb, o, index in BEHIND_TILES:
        rows = block_rows(qb)
        line = slice(qb, qb + 1)

        @pl.when(flags[qb * WIN + o] == 1)
        def _(rows=rows, line=line, index=index):
            keys, vals = key_value(index, k1_ref, v1_ref, v0_ref, far_ref)
            key_part, value_part, query_part = tile_grads(
                keys, vals, q_ref[rows, :], grad_ref[rows, :],
                log_ref[0, line, :], delta_ref[0, line, :], False,
            )
            dk[block_rows(index), :] += key_part
            dv[block_rows(index), :] += value_part
            dq[:, rows] += query_part

    far_back[0] = (dk[block_rows(0), :] * SCALE).astype(bf16)
    far_back[1] = dv[block_rows(0), :].astype(bf16)
    near_back[0] = (dk[pl.ds(BLK, 2 * BLK), :] * SCALE).astype(bf16)
    near_back[1] = dv[pl.ds(BLK, 2 * BLK), :].astype(bf16)


def backward_own_kernel(
    flags, q_ref, k_ref, v_ref, grad_ref, log_ref, dq_in, delta_ref, after,
    dq_ref, own_ref, dk, dv, dq,
):
    dk[...] = jnp.zeros_like(dk)
    dv[...] = jnp.zeros_like(dv)
    dq[...] = dq_in[...]
    for qb, o, index in OWN_TILES:
        rows = block_rows(qb)
        line = slice(qb, qb + 1)

        @pl.when(flags[qb * WIN + o] == 1)
        def _(rows=rows, line=line, index=index, o=o):
            held = block_rows(index)
            key_part, value_part, query_part = tile_grads(
                k_ref[held, :], v_ref[held, :], q_ref[rows, :], grad_ref[rows, :],
                log_ref[0, line, :], delta_ref[0, line, :], o == 0,
            )
            dk[held, :] += key_part
            dv[held, :] += value_part
            dq[:, rows] += query_part

    own_ref[0] = (dk[...] * SCALE).astype(bf16)
    own_ref[1] = dv[...].astype(bf16)
    dq_ref[...] = (dq[...] * SCALE).T.astype(bf16)


def finish_kernel(place, own_ref, near_ref, far_ref, after, key_ref, value_ref):
    for part, result in enumerate((key_ref, value_ref)):
        for block in range(2):
            rows = block_rows(block)
            total = own_ref[part, rows, :].astype(f32) + near_ref[part, rows, :].astype(f32)
            if block == 1:
                total += far_ref[part].astype(f32)
            result[rows, :] = total.astype(bf16)


def head(rows):
    return pl.BlockSpec((rows, HDIM), lambda h, *_: (0, h))


def head_pair(rows):
    return pl.BlockSpec((2, rows, HDIM), lambda h, *_: (0, 0, h))


HEAD_LINES = pl.BlockSpec((1, 2, BLK), lambda h, *_: (h, 0, 0))
ANY = pl.BlockSpec(memory_space=pl.ANY)
HEAD_TURNED = pl.BlockSpec((HDIM, 1024), lambda h, *_: (h, 0))


def shape(dims, dtype):
    return jax.ShapeDtypeStruct(dims, dtype)


WIDTH = 512
HEADS = WIDTH // HDIM
LINES = shape((HEADS, 2, BLK), f32)
TURNED = shape((WIDTH, 1024), f32)


def call(kernel, name, grid, ins, outs, out_shape, scratch, args):
    return pl.pallas_call(
        kernel,
        grid_spec=pltpu.PrefetchScalarGridSpec(
            num_scalar_prefetch=1,
            grid=grid,
            in_specs=ins,
            out_specs=outs,
            scratch_shapes=scratch,
        ),
        out_shape=out_shape,
        compiler_params=pltpu.CompilerParams(vmem_limit_bytes=64 << 20),
        cost_estimate=pl.CostEstimate(flops=1, bytes_accessed=1, transcendentals=0),
        name=name,
    )(*args)


def forward_own(flags, q, k, v, after):
    return call(
        forward_own_kernel, "forward_own", (HEADS,),
        [head(1024)] * 3 + [ANY],
        [HEAD_TURNED, HEAD_LINES, HEAD_LINES],
        [TURNED, LINES, LINES],
        [], (flags, q, k, v, after),
    )


def forward_behind(flags, q, near_k, near_v, edge_v, far, state, after):
    lines = pltpu.VMEM((2, BLK), f32)
    return call(
        forward_behind_kernel, "forward_behind", (HEADS,),
        [head(1024)] * 4 + [head_pair(512)]
        + [HEAD_TURNED, HEAD_LINES, HEAD_LINES, ANY],
        [head(1024), HEAD_TURNED, HEAD_LINES],
        [shape((1024, WIDTH), bf16), shape((WIDTH, 1024), bf16), LINES],
        [pltpu.VMEM((HDIM, 1024), f32), lines, lines],
        (flags, q, near_k, near_v, edge_v, far, *state, after),
    )


def backward_behind(
    flags, q, near_k, near_v, edge_v, far, out, grad, log_sum, after
):
    held = pltpu.VMEM((3 * BLK, HDIM), f32)
    return call(
        backward_behind_kernel, "backward_behind", (HEADS,),
        [head(1024)] * 4 + [head_pair(512)]
        + [head(1024), head(1024), HEAD_LINES, ANY],
        [head_pair(1024), head_pair(512), HEAD_TURNED, HEAD_LINES],
        [shape((2, 1024, WIDTH), bf16), shape((2, 512, WIDTH), bf16), TURNED, LINES],
        [held, held], (flags, q, near_k, near_v, edge_v, far, out, grad, log_sum, after),
    )


def backward_own(flags, q, k, v, grad, log_sum, dq, delta, after):
    held = pltpu.VMEM((2 * BLK, HDIM), f32)
    return call(
        backward_own_kernel, "backward_own", (HEADS,),
        [head(1024)] * 4 + [HEAD_LINES, HEAD_TURNED, HEAD_LINES, ANY],
        [head(1024), head_pair(1024)],
        [shape((1024, WIDTH), bf16), shape((2, 1024, WIDTH), bf16)],
        [held, held, pltpu.VMEM((HDIM, 1024), f32)],
        (flags, q, k, v, grad, log_sum, dq, delta, after),
    )


def finish(place, own, near, far, after):
    return call(
        finish_kernel, "key_value_sum", (HEADS,),
        [head_pair(1024)] * 2 + [head_pair(512), ANY],
        [head(1024), head(1024)],
        [shape((1024, WIDTH), bf16)] * 2,
        [], (place, own, near, far, after),
    )


def pack_kernel(place, k_ref, v_ref, second_ref, held_ref):
    held_ref[...] = k_ref[...]

    @pl.when(pl.program_id(0) == 1)
    def _():
        second_ref[0] = k_ref[...]
        second_ref[1] = v_ref[...]


def pack(place, k, v):
    block = pl.BlockSpec((BLK, WIDTH), lambda i, place: (i, 0))
    return call(
        pack_kernel, "second_blocks", (2,),
        [block, pl.BlockSpec((BLK, WIDTH), lambda i, place: (1, 0))],
        [pl.BlockSpec((2, BLK, WIDTH), lambda i, place: (0, 0, 0)), block],
        [shape((2, BLK, WIDTH), bf16), shape(k.shape, bf16)], [], (place, k, v),
    )


def nothing_kernel(*refs):
    pass


def together(values, after=()):
    return pl.pallas_call(
        nothing_kernel,
        in_specs=[ANY] * (len(values) + len(after)),
        out_specs=[ANY] * len(values),
        out_shape=[shape(value.shape, value.dtype) for value in values],
        input_output_aliases={index: index for index in range(len(values))},
        compiler_params=pltpu.CompilerParams(vmem_limit_bytes=64 << 20),
        name="order",
    )(*values, *after)


def grad_kernel(place, a_ref, b_ref, wa_ref, wb_ref, *rest):
    total = dot(a_ref[...], wa_ref[...], NT) + dot(b_ref[...], wb_ref[...], NT)
    if len(rest) == 3:
        total += rest[0][...]
    rest[-1][...] = total.astype(rest[-1].dtype)


def grad_terms(place, first, a, b, weight, before, after):
    tile = 512
    row = pl.BlockSpec((tile, 1024), lambda i, place: (i, 0))
    result = pl.BlockSpec((tile, 512), lambda i, place: (i, 0))

    def columns(flip):
        return pl.BlockSpec((512, 1024), lambda i, place: (0, place[0] ^ flip))

    more = [] if before is None else [before]
    return call(
        grad_kernel, "projection_backward", (1024 // tile,),
        [row, row, columns(first), columns(first + 1)] + [result] * len(more) + [ANY], result,
        shape((1024, 512), bf16 if more else f32), [], (place, a, b, weight, weight, *more, after),
    )


def weight_kernel(place, turned_ref, g0, g1, g2, g3, after, *outs):
    owner = place[0] ^ pl.program_id(0)
    y = owner % 2 * 2 + pl.program_id(1)
    for part, ref in enumerate((g0, g1, g2, g3)):
        for slot, out_ref in enumerate(outs):

            @pl.when((pl.program_id(0) == part) & ((y - place[1] + 3) % 4 == slot))
            def _(ref=ref, out_ref=out_ref, part=part):
                out_ref[part // 2] = dot(turned_ref[...], ref[...], NN).astype(bf16)


def weight_terms(place, turned, cotangents, after):
    def piece(part):
        return pl.BlockSpec(
            (1024, 512),
            lambda i, half, place: (
                0, jnp.where(i == part, half, jnp.where(i < part, 0, 1)),
            ),
        )

    return call(
        weight_kernel, "weight_gradient", (4, 2),
        [pl.BlockSpec((512, 1024), lambda i, half, place: (0, 0))] + [piece(p) for p in range(4)]
        + [ANY],
        [pl.BlockSpec((2, 512, 512), lambda i, half, place: (0, 0, 0))] * 4,
        [shape((2, 512, 512), bf16)] * 4, [], (place, turned, *cotangents, after),
    )


def over_y(parts):
    return [to_y(parts[s], s + 1) for s in (0, 2, 1)]


def pieces_kernel(place, a, b, c, d, after, *outs):
    for slot, out_ref in enumerate(outs):

        @pl.when(pl.program_id(0) == slot)
        def _(out_ref=out_ref):
            out_ref[...] = sum(ref[...].astype(f32) for ref in (a, b, c, d)).astype(bf16)


def pieces_by_z(place, terms, after):
    piece = pl.BlockSpec((2, 512, 128), lambda i, place: (0, 0, (place[2] + i + 1) % 4))
    return call(
        pieces_kernel, "weight_by_z", (4,), [piece] * 4 + [ANY],
        [pl.BlockSpec((2, 512, 128), lambda i, place: (0, 0, 0))] * 4,
        [shape((2, 512, 128), bf16)] * 4, [], (place, *terms, after),
    )


def weight_z_kernel(place, a_ref, b_ref, c_ref, d_ref, after, kept_ref, sent_ref):
    def total(index):
        return sum(ref[index].astype(f32) for ref in (a_ref, b_ref, c_ref, d_ref))

    kept = place[3] ^ (place[0] // 2)
    kept_ref[...] = total(kept)
    sent_ref[...] = total(1 - kept).astype(bf16)


def weight_z_sum(place, terms, after):
    whole = pl.BlockSpec((2, 512, 128), lambda i, place: (0, 0, 0))
    result = pl.BlockSpec((512, 128), lambda i, place: (0, 0))
    return call(
        weight_z_kernel, "weight_z_sum", (1,), [whole] * 4 + [ANY], [result] * 2,
        [shape((512, 128), f32), shape((512, 128), bf16)], [], (place, *terms, after),
    )


def copy_kernel(place, in_ref, *refs):
    refs[-1][...] = in_ref[...]


def far_columns(place, weight, after):
    return call(
        copy_kernel, "projection_far", (1,),
        [pl.BlockSpec((128, 2048), lambda i, place: (place[2], 1 - place[0] // 2)), ANY],
        pl.BlockSpec((128, 2048), lambda i, place: (0, 0)),
        shape((128, 2048), bf16), [], (place, weight, after),
    )


def along_z():
    return [[line * 4 + z for z in range(4)] for line in range(8)]


def core_kernel(place, own_ref, far_ref, far_rows, own_rows, after, out_ref):
    out_ref[0] = own_ref[...]
    out_ref[1] = far_ref[...]
    for part, rows in ((2, far_rows), (3, own_rows)):
        for half in range(2):
            out_ref[part, :, block_rows(half)] = rows[block_rows(half), :]


def for_core(place, weight, far_weight, far_attention, attention, after):
    rows = pl.BlockSpec((1024, 512), lambda i, place: (0, 0))
    return call(
        core_kernel, "for_core", (1,),
        [
            pl.BlockSpec((512, 1024), lambda i, place: (0, place[0] ^ 1)),
            pl.BlockSpec((512, 1024), lambda i, place: (0, 1 - place[0] % 2)),
            rows, rows, ANY,
        ],
        pl.BlockSpec((4, 512, 1024), lambda i, place: (0, 0, 0)),
        shape((4, 512, 1024), bf16), [],
        (place, weight, far_weight, far_attention, attention, after),
    )


def mix_kernel(place, own, core, far, far_core, w_own, w_far, w_core, after, out_ref):
    total = dot(own[...], w_own[...], NN) + dot(core[0], w_core[0], NN)
    total += dot(far[...], w_far[...], NN) + dot(far_core[0], w_core[1], NN)
    out_ref[...] = total.astype(bf16)


def mix(place, attention, far_attention, weight, far_weight, from_core, after):
    rows = pl.BlockSpec((512, 512), lambda i, place: (i, 0))
    return call(
        mix_kernel, "projection", (2,),
        [
            rows,
            pl.BlockSpec((1, 512, 512), lambda i, place: (3, 0, i)),
            rows,
            pl.BlockSpec((1, 512, 512), lambda i, place: (2, 0, i)),
            pl.BlockSpec((512, 1024), lambda i, place: (0, place[0])),
            pl.BlockSpec((512, 1024), lambda i, place: (0, place[0] % 2)),
            pl.BlockSpec((2, 512, 1024), lambda i, place: (0, 0, 0)),
            ANY,
        ],
        pl.BlockSpec((512, 1024), lambda i, place: (i, 0)),
        shape((1024, 1024), bf16), [],
        (place, attention, from_core, far_attention, from_core, weight, far_weight, from_core, after),
    )


def per_device(queries, keys, values, out_weight, out_grad, spans, pairs):
    ctx = lax.axis_index("ctx")
    tp = lax.axis_index("tp")
    place = jnp.stack([tp, ctx // 4 % 4, ctx % 4, ctx // 16]).astype(jnp.int32)

    far_grad = to_x_hi(out_grad)
    near_pairs = [(s, s + 1) for s in range(31) if s != EDGE]
    near_values = lax.ppermute(values, "ctx", near_pairs + [(EDGE, 0)])
    core_grad = to_core(out_grad)
    second, held_keys = pack(place, keys, values)
    far_moved = first_hop(second, 1)

    query_block = ctx * 2 + jnp.arange(2, dtype=jnp.int32)[:, None] + jnp.zeros((1, WIN), jnp.int32)
    key_block = query_block - jnp.arange(WIN, dtype=jnp.int32)[None, :]
    flags = block_rule(spans, pairs, query_block, key_block).astype(jnp.int32).reshape(-1)
    own_state = forward_own(flags, queries, keys, values, keys)
    far_weight = far_columns(place, out_weight, own_state[1])
    terms = grad_terms(place, 0, out_grad, core_grad, out_weight, None, far_weight)

    [far_moved] = together([far_moved], [terms])
    far = second_hop(far_moved, 1)
    near_values, held_keys = together([near_values, held_keys], [far_moved])
    near_keys = along_ctx(held_keys, 1)
    edge_values = lax.ppermute(near_values, "ctx", [(0, EDGE + 1)])
    near_keys, far, far_grad, edge_values, far_weight = together(
        [near_keys, far, far_grad, edge_values, far_weight], [far_moved]
    )

    far_core_grad = to_core(far_grad)
    far_weight = to_x_hi(far_weight)
    behind = (flags, queries, near_keys, near_values, edge_values, far)
    attention, turned, log_sum = forward_behind(*behind, own_state, far)
    far_core_grad, far_weight = together([far_core_grad, far_weight], [log_sum])
    far_weight = lax.all_gather(
        far_weight, "ctx", axis=0, tiled=True, axis_index_groups=along_z()
    )
    far_attention = to_x_hi(attention)
    attn_grad = grad_terms(place, 2, far_grad, far_core_grad, out_weight, terms, far_core_grad)
    cotangents = (out_grad, core_grad, far_grad, far_core_grad)
    weight_parts = weight_terms(place, turned, cotangents, attn_grad)
    weight_moved = over_y(weight_parts)
    near_back, far_back, dq, delta = backward_behind(
        *behind, attention, attn_grad, log_sum, weight_parts[3]
    )
    query_grad, own = backward_own(
        flags, queries, keys, values, attn_grad, log_sum, dq, delta, delta
    )

    back_moved = first_hop(far_back, -1)
    far_attention, far_weight = together([far_attention, far_weight], [own])
    from_core = for_core(place, out_weight, far_weight, far_attention, attention, own)

    *weight_moved, near_back, back_moved, from_core = together(
        [*weight_moved, near_back, back_moved, from_core]
    )
    near_back = along_ctx(near_back, -1)
    far_back = second_hop(back_moved, -1)
    from_core = to_core(from_core)
    weight_pieces = pieces_by_z(place, [weight_parts[3], *weight_moved], weight_moved[0])
    weight_moved = [to_z(weight_pieces[s], s + 1) for s in (0, 2, 1)]
    mixed = mix(
        place, attention, far_attention, out_weight, far_weight, from_core, weight_pieces[3]
    )
    kept, sent = weight_z_sum(place, [weight_pieces[3], *weight_moved], mixed)
    key_grad, value_grad = finish(place, own, near_back, far_back, kept)
    [sent] = together([to_x_lo(sent)], [key_grad])
    weight_grad = kept + sent.astype(f32)
    return (mixed, query_grad, key_grad, value_grad, weight_grad)


def solution(mesh):
    placed = (
        P("ctx", "tp"),
        P("ctx", "tp"),
        P("ctx", "tp"),
        P("tp", None),
        P("ctx", "tp"),
        P(),
        P(),
    )
    return jax.shard_map(
        per_device,
        mesh=mesh,
        in_specs=placed,
        out_specs=(P("ctx", "tp"), P("ctx", "tp"), P("ctx", "tp"), P("ctx", "tp"), P("tp", "ctx")),
        check_vma=False,
    )
```

```python
import functools
import math

import jax
import jax.numpy as jnp
from jax import lax
from jax.experimental import pallas as pl
from jax.experimental.pallas import tpu as pltpu
from jax.sharding import PartitionSpec as P

HDIM = 128
BLK = 512
WIN = 4
SCALE = 1.0 / math.sqrt(HDIM)
SCALE2 = SCALE * math.log2(math.e)
AXES = ("ctx", "tp")
NT = (((1,), (1,)), ((), ()))
NN = (((1,), (0,)), ((), ()))
f32 = jnp.float32
bf16 = jnp.bfloat16


def places():
    for x_lo in range(2):
        for y in range(4):
            for z in range(4):
                for x_hi in range(2):
                    for core in range(2):
                        yield x_lo, y, z, x_hi, core


def number(x_lo, y, z, x_hi, core):
    return ((x_lo * 4 + y) * 4 + z) * 4 + x_hi * 2 + core


def move(value, target):
    pairs = [(number(*place), number(*target(*place))) for place in places()]
    return lax.ppermute(value, AXES, pairs)


def to_core(value):
    return move(value, lambda x_lo, y, z, x_hi, core: (x_lo, y, z, x_hi, 1 - core))


def to_x_hi(value):
    return move(value, lambda x_lo, y, z, x_hi, core: (x_lo, y, z, 1 - x_hi, core))


def to_x_lo(value):
    return move(value, lambda x_lo, y, z, x_hi, core: (1 - x_lo, y, z, x_hi, core))


def to_y(value, steps):
    return move(value, lambda x_lo, y, z, x_hi, core: (x_lo, (y + steps) % 4, z, x_hi, core))


def to_z(value, steps):
    return move(value, lambda x_lo, y, z, x_hi, core: (x_lo, y, (z + steps) % 4, x_hi, core))


EDGE = 15


def along_ctx(value, steps):
    pairs = [(s, s + steps) for s in range(32) if 0 <= s + steps < 32]
    return lax.ppermute(value, "ctx", pairs)


def middle(source, sign):
    return source // 4 * 4 + (source % 4 - sign) % 4


def two_pairs(sign):
    sources = [s for s in range(32) if 0 <= s + 2 * sign < 32]
    return [(s, middle(s, sign), s + 2 * sign) for s in sources]


def first_hop(value, sign):
    return lax.ppermute(value, "ctx", [(s, m) for s, m, _ in two_pairs(sign)])


def second_hop(value, sign):
    return lax.ppermute(value, "ctx", [(m, t) for _, m, t in two_pairs(sign)])


def block_rule(spans, pairs, query_block, key_block):
    listed = jnp.any(
        (pairs[:, 0] == query_block[..., None]) & (pairs[:, 1] == key_block[..., None]), axis=-1
    )
    span_lower = spans[:, 0]
    span_upper = spans[:, 0] + spans[:, 1]
    query_inside = (span_lower <= query_block[..., None]) & (query_block[..., None] < span_upper)
    key_inside = (span_lower <= key_block[..., None]) & (key_block[..., None] < span_upper)
    same = jnp.any(query_inside & key_inside, axis=-1)
    reach = (query_block - key_block >= 0) & (query_block - key_block < WIN)
    return listed & same & reach


def dot(a, b, dims):
    return lax.dot_general(a, b, dims, preferred_element_type=f32)


def causal():
    key_row = lax.broadcasted_iota(jnp.int32, (BLK, BLK), 0)
    query_column = lax.broadcasted_iota(jnp.int32, (BLK, BLK), 1)
    return key_row <= query_column


def block_rows(index):
    return pl.ds(index * BLK, BLK)


OWN_TILES = ((0, 0, 0), (1, 0, 1), (1, 1, 0))
BEHIND_TILES = ((0, 3, 0), (0, 2, 1), (0, 1, 2), (1, 3, 1), (1, 2, 2))


def key_value(index, near_k, near_v, edge_v, far):
    if index == 0:
        return far[0], far[1]
    rows = block_rows(index - 1)
    return near_k[rows, :], near_v[rows, :] + edge_v[rows, :]


def absorb(keys, vals, query, top, total, acc, rows):
    s = dot(keys, query, NT)
    old = top
    m = jnp.maximum(old, jnp.max(s, axis=0, keepdims=True))
    p = jnp.exp2(s * SCALE2 - m * SCALE2)
    fix = jnp.exp2((old - m) * SCALE2)
    part = dot(vals.T, p.astype(bf16), NN)
    acc[:, rows] = acc[:, rows] * fix + part
    return m, total * fix + jnp.sum(p, axis=0, keepdims=True)


def forward_own_kernel(flags, q_ref, k_ref, v_ref, after, acc, top, total):
    for qb, o, index in OWN_TILES:
        rows = block_rows(qb)
        line = slice(qb, qb + 1)

        def diagonal(rows=rows, line=line):
            s = jnp.where(causal(), dot(k_ref[rows, :], q_ref[rows, :], NT), -jnp.inf)
            m = jnp.max(s, axis=0, keepdims=True)
            p = jnp.exp2(s * SCALE2 - m * SCALE2)
            acc[:, rows] = dot(v_ref[rows, :].T, p.astype(bf16), NN)
            top[0, line, :] = m
            total[0, line, :] = jnp.sum(p, axis=0, keepdims=True)

        def nothing(rows=rows, line=line):
            acc[:, rows] = jnp.zeros((HDIM, BLK), f32)
            top[0, line, :] = jnp.zeros((1, BLK), f32)
            total[0, line, :] = jnp.ones((1, BLK), f32)

        def tile(rows=rows, line=line, index=index):
            held = block_rows(index)
            top[0, line, :], total[0, line, :] = absorb(
                k_ref[held, :], v_ref[held, :], q_ref[rows, :],
                top[0, line, :], total[0, line, :], acc, rows,
            )

        listed = flags[qb * WIN + o] == 1
        if o == 0:
            pl.when(listed)(diagonal)
            pl.when(jnp.logical_not(listed))(nothing)
        else:
            pl.when(listed)(tile)


def forward_behind_kernel(
    flags, q_ref, k1_ref, v1_ref, v0_ref, far_ref, acc_in, top_in, total_in,
    after, out_ref, turned_ref, log_ref, acc, top, total,
):
    acc[...] = acc_in[...]
    top[...] = top_in[0]
    total[...] = total_in[0]
    for qb, o, index in BEHIND_TILES:
        rows = block_rows(qb)
        line = slice(qb, qb + 1)

        @pl.when(flags[qb * WIN + o] == 1)
        def _(rows=rows, line=line, index=index):
            keys, vals = key_value(index, k1_ref, v1_ref, v0_ref, far_ref)
            top[line, :], total[line, :] = absorb(
                keys, vals, q_ref[rows, :], top[line, :], total[line, :], acc, rows
            )

    for qb in range(2):
        rows = block_rows(qb)
        result = acc[:, rows] * (1.0 / total[qb : qb + 1, :])
        turned_ref[:, rows] = result.astype(bf16)
        out_ref[rows, :] = result.T.astype(bf16)
    log_ref[0] = top[...] * SCALE2 + jnp.log2(total[...])


def tile_grads(keys, vals, query, grad, log_sum, delta, diagonal):
    p = jnp.exp2(dot(keys, query, NT) * SCALE2 - log_sum)
    if diagonal:
        p = jnp.where(causal(), p, 0.0)
    value_part = dot(p.astype(bf16), grad, NN)
    dp = dot(vals, grad, NT)
    ds = (p * (dp - delta)).astype(bf16)
    return dot(ds, query, NN), value_part, dot(keys.T, ds, NN)


def backward_behind_kernel(
    flags, q_ref, k1_ref, v1_ref, v0_ref, far_ref, out_ref, grad_ref, log_ref,
    after, near_back, far_back, dq, delta_ref, dk, dv,
):
    dk[...] = jnp.zeros_like(dk)
    dv[...] = jnp.zeros_like(dv)
    dq[...] = jnp.zeros_like(dq)
    product = grad_ref[...].astype(f32) * out_ref[...].astype(f32)
    delta = jnp.sum(product.T, axis=0, keepdims=True)
    for qb in range(2):
        delta_ref[0, qb : qb + 1, :] = delta[:, qb * BLK : (qb + 1) * BLK]
    for qb, o, index in BEHIND_TILES:
        rows = block_rows(qb)
        line = slice(qb, qb + 1)

        @pl.when(flags[qb * WIN + o] == 1)
        def _(rows=rows, line=line, index=index):
            keys, vals = key_value(index, k1_ref, v1_ref, v0_ref, far_ref)
            key_part, value_part, query_part = tile_grads(
                keys, vals, q_ref[rows, :], grad_ref[rows, :],
                log_ref[0, line, :], delta_ref[0, line, :], False,
            )
            dk[block_rows(index), :] += key_part
            dv[block_rows(index), :] += value_part
            dq[:, rows] += query_part

    far_back[0] = (dk[block_rows(0), :] * SCALE).astype(bf16)
    far_back[1] = dv[block_rows(0), :].astype(bf16)
    near_back[0] = (dk[pl.ds(BLK, 2 * BLK), :] * SCALE).astype(bf16)
    near_back[1] = dv[pl.ds(BLK, 2 * BLK), :].astype(bf16)


def backward_own_kernel(
    flags, q_ref, k_ref, v_ref, grad_ref, log_ref, dq_in, delta_ref, after,
    dq_ref, own_ref, dk, dv, dq,
):
    dk[...] = jnp.zeros_like(dk)
    dv[...] = jnp.zeros_like(dv)
    dq[...] = dq_in[...]
    for qb, o, index in OWN_TILES:
        rows = block_rows(qb)
        line = slice(qb, qb + 1)

        @pl.when(flags[qb * WIN + o] == 1)
        def _(rows=rows, line=line, index=index, o=o):
            held = block_rows(index)
            key_part, value_part, query_part = tile_grads(
                k_ref[held, :], v_ref[held, :], q_ref[rows, :], grad_ref[rows, :],
                log_ref[0, line, :], delta_ref[0, line, :], o == 0,
            )
            dk[held, :] += key_part
            dv[held, :] += value_part
            dq[:, rows] += query_part

    own_ref[0] = (dk[...] * SCALE).astype(bf16)
    own_ref[1] = dv[...].astype(bf16)
    dq_ref[...] = (dq[...] * SCALE).T.astype(bf16)


def finish_kernel(place, own_ref, near_ref, far_ref, after, key_ref, value_ref):
    for part, result in enumerate((key_ref, value_ref)):
        for block in range(2):
            rows = block_rows(block)
            total = own_ref[part, rows, :].astype(f32) + near_ref[part, rows, :].astype(f32)
            if block == 1:
                total += far_ref[part].astype(f32)
            result[rows, :] = total.astype(bf16)


def head(rows):
    return pl.BlockSpec((rows, HDIM), lambda h, *_: (0, h))


def head_pair(rows):
    return pl.BlockSpec((2, rows, HDIM), lambda h, *_: (0, 0, h))


HEAD_LINES = pl.BlockSpec((1, 2, BLK), lambda h, *_: (h, 0, 0))
ANY = pl.BlockSpec(memory_space=pl.ANY)
HEAD_TURNED = pl.BlockSpec((HDIM, 1024), lambda h, *_: (h, 0))


def shape(dims, dtype):
    return jax.ShapeDtypeStruct(dims, dtype)


WIDTH = 512
HEADS = WIDTH // HDIM
LINES = shape((HEADS, 2, BLK), f32)
TURNED = shape((WIDTH, 1024), f32)


def call(kernel, name, grid, ins, outs, out_shape, scratch, args):
    return pl.pallas_call(
        kernel,
        grid_spec=pltpu.PrefetchScalarGridSpec(
            num_scalar_prefetch=1,
            grid=grid,
            in_specs=ins,
            out_specs=outs,
            scratch_shapes=scratch,
        ),
        out_shape=out_shape,
        compiler_params=pltpu.CompilerParams(vmem_limit_bytes=64 << 20),
        cost_estimate=pl.CostEstimate(flops=1, bytes_accessed=1, transcendentals=0),
        name=name,
    )(*args)


def forward_own(flags, q, k, v, after):
    return call(
        forward_own_kernel, "forward_own", (HEADS,),
        [head(1024)] * 3 + [ANY],
        [HEAD_TURNED, HEAD_LINES, HEAD_LINES],
        [TURNED, LINES, LINES],
        [], (flags, q, k, v, after),
    )


def forward_behind(flags, q, near_k, near_v, edge_v, far, state, after):
    lines = pltpu.VMEM((2, BLK), f32)
    return call(
        forward_behind_kernel, "forward_behind", (HEADS,),
        [head(1024)] * 4 + [head_pair(512)]
        + [HEAD_TURNED, HEAD_LINES, HEAD_LINES, ANY],
        [head(1024), HEAD_TURNED, HEAD_LINES],
        [shape((1024, WIDTH), bf16), shape((WIDTH, 1024), bf16), LINES],
        [pltpu.VMEM((HDIM, 1024), f32), lines, lines],
        (flags, q, near_k, near_v, edge_v, far, *state, after),
    )


def backward_behind(
    flags, q, near_k, near_v, edge_v, far, out, grad, log_sum, after
):
    held = pltpu.VMEM((3 * BLK, HDIM), f32)
    return call(
        backward_behind_kernel, "backward_behind", (HEADS,),
        [head(1024)] * 4 + [head_pair(512)]
        + [head(1024), head(1024), HEAD_LINES, ANY],
        [head_pair(1024), head_pair(512), HEAD_TURNED, HEAD_LINES],
        [shape((2, 1024, WIDTH), bf16), shape((2, 512, WIDTH), bf16), TURNED, LINES],
        [held, held], (flags, q, near_k, near_v, edge_v, far, out, grad, log_sum, after),
    )


def backward_own(flags, q, k, v, grad, log_sum, dq, delta, after):
    held = pltpu.VMEM((2 * BLK, HDIM), f32)
    return call(
        backward_own_kernel, "backward_own", (HEADS,),
        [head(1024)] * 4 + [HEAD_LINES, HEAD_TURNED, HEAD_LINES, ANY],
        [head(1024), head_pair(1024)],
        [shape((1024, WIDTH), bf16), shape((2, 1024, WIDTH), bf16)],
        [held, held, pltpu.VMEM((HDIM, 1024), f32)],
        (flags, q, k, v, grad, log_sum, dq, delta, after),
    )


def finish(place, own, near, far, after):
    return call(
        finish_kernel, "key_value_sum", (HEADS,),
        [head_pair(1024)] * 2 + [head_pair(512), ANY],
        [head(1024), head(1024)],
        [shape((1024, WIDTH), bf16)] * 2,
        [], (place, own, near, far, after),
    )


def pack_kernel(place, k_ref, v_ref, second_ref, held_ref):
    held_ref[...] = k_ref[...]

    @pl.when(pl.program_id(0) == 1)
    def _():
        second_ref[0] = k_ref[...]
        second_ref[1] = v_ref[...]


def pack(place, k, v):
    block = pl.BlockSpec((BLK, WIDTH), lambda i, place: (i, 0))
    return call(
        pack_kernel, "second_blocks", (2,),
        [block, pl.BlockSpec((BLK, WIDTH), lambda i, place: (1, 0))],
        [pl.BlockSpec((2, BLK, WIDTH), lambda i, place: (0, 0, 0)), block],
        [shape((2, BLK, WIDTH), bf16), shape(k.shape, bf16)], [], (place, k, v),
    )


def nothing_kernel(*refs):
    pass


def together(values, after=()):
    return pl.pallas_call(
        nothing_kernel,
        in_specs=[ANY] * (len(values) + len(after)),
        out_specs=[ANY] * len(values),
        out_shape=[shape(value.shape, value.dtype) for value in values],
        input_output_aliases={index: index for index in range(len(values))},
        compiler_params=pltpu.CompilerParams(vmem_limit_bytes=64 << 20),
        name="order",
    )(*values, *after)


def grad_kernel(place, a_ref, b_ref, wa_ref, wb_ref, *rest):
    total = dot(a_ref[...], wa_ref[...], NT) + dot(b_ref[...], wb_ref[...], NT)
    if len(rest) == 3:
        total += rest[0][...]
    rest[-1][...] = total.astype(rest[-1].dtype)


def grad_terms(place, first, a, b, weight, before, after):
    tile = 512
    row = pl.BlockSpec((tile, 1024), lambda i, place: (i, 0))
    result = pl.BlockSpec((tile, 512), lambda i, place: (i, 0))

    def columns(flip):
        return pl.BlockSpec((512, 1024), lambda i, place: (0, place[0] ^ flip))

    more = [] if before is None else [before]
    return call(
        grad_kernel, "projection_backward", (1024 // tile,),
        [row, row, columns(first), columns(first + 1)] + [result] * len(more) + [ANY], result,
        shape((1024, 512), bf16 if more else f32), [], (place, a, b, weight, weight, *more, after),
    )


def weight_kernel(place, turned_ref, g0, g1, g2, g3, after, *outs):
    owner = place[0] ^ pl.program_id(0)
    y = owner % 2 * 2 + pl.program_id(1)
    for part, ref in enumerate((g0, g1, g2, g3)):
        for slot, out_ref in enumerate(outs):

            @pl.when((pl.program_id(0) == part) & ((y - place[1] + 3) % 4 == slot))
            def _(ref=ref, out_ref=out_ref, part=part):
                out_ref[part // 2] = dot(turned_ref[...], ref[...], NN).astype(bf16)


def weight_terms(place, turned, cotangents, after):
    def piece(part):
        return pl.BlockSpec(
            (1024, 512),
            lambda i, half, place: (
                0, jnp.where(i == part, half, jnp.where(i < part, 0, 1)),
            ),
        )

    return call(
        weight_kernel, "weight_gradient", (4, 2),
        [pl.BlockSpec((512, 1024), lambda i, half, place: (0, 0))] + [piece(p) for p in range(4)]
        + [ANY],
        [pl.BlockSpec((2, 512, 512), lambda i, half, place: (0, 0, 0))] * 4,
        [shape((2, 512, 512), bf16)] * 4, [], (place, turned, *cotangents, after),
    )


def over_y(parts):
    return [to_y(parts[s], s + 1) for s in (0, 2, 1)]


def pieces_kernel(place, a, b, c, d, after, *outs):
    for slot, out_ref in enumerate(outs):

        @pl.when(pl.program_id(0) == slot)
        def _(out_ref=out_ref):
            out_ref[...] = sum(ref[...].astype(f32) for ref in (a, b, c, d)).astype(bf16)


def pieces_by_z(place, terms, after):
    piece = pl.BlockSpec((2, 512, 128), lambda i, place: (0, 0, (place[2] + i + 1) % 4))
    return call(
        pieces_kernel, "weight_by_z", (4,), [piece] * 4 + [ANY],
        [pl.BlockSpec((2, 512, 128), lambda i, place: (0, 0, 0))] * 4,
        [shape((2, 512, 128), bf16)] * 4, [], (place, *terms, after),
    )


def weight_z_kernel(place, a_ref, b_ref, c_ref, d_ref, after, kept_ref, sent_ref):
    def total(index):
        return sum(ref[index].astype(f32) for ref in (a_ref, b_ref, c_ref, d_ref))

    kept = place[3] ^ (place[0] // 2)
    kept_ref[...] = total(kept)
    sent_ref[...] = total(1 - kept).astype(bf16)


def weight_z_sum(place, terms, after):
    whole = pl.BlockSpec((2, 512, 128), lambda i, place: (0, 0, 0))
    result = pl.BlockSpec((512, 128), lambda i, place: (0, 0))
    return call(
        weight_z_kernel, "weight_z_sum", (1,), [whole] * 4 + [ANY], [result] * 2,
        [shape((512, 128), f32), shape((512, 128), bf16)], [], (place, *terms, after),
    )


def copy_kernel(place, in_ref, *refs):
    refs[-1][...] = in_ref[...]


def far_columns(place, weight, after):
    return call(
        copy_kernel, "projection_far", (2,),
        [pl.BlockSpec((256, 2048), lambda i, place: (i, 1 - place[0] // 2)), ANY],
        pl.BlockSpec((256, 2048), lambda i, place: (i, 0)),
        shape((512, 2048), bf16), [], (place, weight, after),
    )


def core_kernel(place, own_ref, far_ref, far_rows, own_rows, after, out_ref):
    out_ref[0] = own_ref[...]
    out_ref[1] = far_ref[...]
    for part, rows in ((2, far_rows), (3, own_rows)):
        for half in range(2):
            out_ref[part, :, block_rows(half)] = rows[block_rows(half), :]


def for_core(place, weight, far_weight, far_attention, attention, after):
    rows = pl.BlockSpec((1024, 512), lambda i, place: (0, 0))
    return call(
        core_kernel, "for_core", (1,),
        [
            pl.BlockSpec((512, 1024), lambda i, place: (0, place[0] ^ 1)),
            pl.BlockSpec((512, 1024), lambda i, place: (0, 1 - place[0] % 2)),
            rows, rows, ANY,
        ],
        pl.BlockSpec((4, 512, 1024), lambda i, place: (0, 0, 0)),
        shape((4, 512, 1024), bf16), [],
        (place, weight, far_weight, far_attention, attention, after),
    )


def mix_kernel(place, own, core, far, far_core, w_own, w_far, w_core, after, out_ref):
    total = dot(own[...], w_own[...], NN) + dot(core[0], w_core[0], NN)
    total += dot(far[...], w_far[...], NN) + dot(far_core[0], w_core[1], NN)
    out_ref[...] = total.astype(bf16)


def mix(place, attention, far_attention, weight, far_weight, from_core, after):
    rows = pl.BlockSpec((512, 512), lambda i, place: (i, 0))
    return call(
        mix_kernel, "projection", (2,),
        [
            rows,
            pl.BlockSpec((1, 512, 512), lambda i, place: (3, 0, i)),
            rows,
            pl.BlockSpec((1, 512, 512), lambda i, place: (2, 0, i)),
            pl.BlockSpec((512, 1024), lambda i, place: (0, place[0])),
            pl.BlockSpec((512, 1024), lambda i, place: (0, place[0] % 2)),
            pl.BlockSpec((2, 512, 1024), lambda i, place: (0, 0, 0)),
            ANY,
        ],
        pl.BlockSpec((512, 1024), lambda i, place: (i, 0)),
        shape((1024, 1024), bf16), [],
        (place, attention, from_core, far_attention, from_core, weight, far_weight, from_core, after),
    )


def per_device(queries, keys, values, out_weight, out_grad, spans, pairs):
    ctx = lax.axis_index("ctx")
    tp = lax.axis_index("tp")
    place = jnp.stack([tp, ctx // 4 % 4, ctx % 4, ctx // 16]).astype(jnp.int32)

    far_grad = to_x_hi(out_grad)
    near_pairs = [(s, s + 1) for s in range(31) if s != EDGE]
    near_values = lax.ppermute(values, "ctx", near_pairs + [(EDGE, 0)])
    core_grad = to_core(out_grad)
    second, held_keys = pack(place, keys, values)
    far_moved = first_hop(second, 1)

    query_block = ctx * 2 + jnp.arange(2, dtype=jnp.int32)[:, None] + jnp.zeros((1, WIN), jnp.int32)
    key_block = query_block - jnp.arange(WIN, dtype=jnp.int32)[None, :]
    flags = block_rule(spans, pairs, query_block, key_block).astype(jnp.int32).reshape(-1)
    own_state = forward_own(flags, queries, keys, values, keys)
    far_weight = far_columns(place, out_weight, own_state[1])
    terms = grad_terms(place, 0, out_grad, core_grad, out_weight, None, far_weight)

    [far_moved] = together([far_moved], [terms])
    far = second_hop(far_moved, 1)
    near_values, held_keys = together([near_values, held_keys], [far_moved])
    near_keys = along_ctx(held_keys, 1)
    edge_values = lax.ppermute(near_values, "ctx", [(0, EDGE + 1)])
    near_keys, far, far_grad, edge_values, far_weight = together(
        [near_keys, far, far_grad, edge_values, far_weight], [far_moved]
    )

    far_core_grad = to_core(far_grad)
    far_weight = to_x_hi(far_weight)
    behind = (flags, queries, near_keys, near_values, edge_values, far)
    attention, turned, log_sum = forward_behind(*behind, own_state, far)
    [far_core_grad] = together([far_core_grad], [log_sum])
    far_attention = to_x_hi(attention)
    attn_grad = grad_terms(place, 2, far_grad, far_core_grad, out_weight, terms, far_core_grad)
    cotangents = (out_grad, core_grad, far_grad, far_core_grad)
    weight_parts = weight_terms(place, turned, cotangents, attn_grad)
    weight_moved = over_y(weight_parts)
    near_back, far_back, dq, delta = backward_behind(
        *behind, attention, attn_grad, log_sum, weight_parts[3]
    )
    far_back, far_weight = together([far_back, far_weight])
    query_grad, own = backward_own(
        flags, queries, keys, values, attn_grad, log_sum, dq, delta, delta
    )

    back_moved = first_hop(far_back, -1)
    [far_attention] = together([far_attention], [own])
    from_core = for_core(place, out_weight, far_weight, far_attention, attention, own)

    *weight_moved, near_back, back_moved, from_core = together(
        [*weight_moved, near_back, back_moved, from_core]
    )
    near_back = along_ctx(near_back, -1)
    far_back = second_hop(back_moved, -1)
    from_core = to_core(from_core)
    weight_pieces = pieces_by_z(place, [weight_parts[3], *weight_moved], weight_moved[0])
    weight_moved = [to_z(weight_pieces[s], s + 1) for s in (0, 2, 1)]
    mixed = mix(
        place, attention, far_attention, out_weight, far_weight, from_core, weight_pieces[3]
    )
    kept, sent = weight_z_sum(place, [weight_pieces[3], *weight_moved], mixed)
    key_grad, value_grad = finish(place, own, near_back, far_back, kept)
    [sent] = together([to_x_lo(sent)], [key_grad])
    weight_grad = kept + sent.astype(f32)
    return (mixed, query_grad, key_grad, value_grad, weight_grad)


def solution(mesh):
    placed = (
        P("ctx", "tp"),
        P("ctx", "tp"),
        P("ctx", "tp"),
        P("tp", None),
        P("ctx", "tp"),
        P(),
        P(),
    )
    return jax.shard_map(
        per_device,
        mesh=mesh,
        in_specs=placed,
        out_specs=(P("ctx", "tp"), P("ctx", "tp"), P("ctx", "tp"), P("ctx", "tp"), P("tp", "ctx")),
        check_vma=False,
    )
```

```python
import functools
import math

import jax
import jax.numpy as jnp
from jax import lax
from jax.experimental import pallas as pl
from jax.experimental.pallas import tpu as pltpu
from jax.sharding import PartitionSpec as P

HDIM = 128
BLK = 512
WIN = 4
SCALE = 1.0 / math.sqrt(HDIM)
SCALE2 = SCALE * math.log2(math.e)
AXES = ("ctx", "tp")
NT = (((1,), (1,)), ((), ()))
NN = (((1,), (0,)), ((), ()))
f32 = jnp.float32
bf16 = jnp.bfloat16


def places():
    for x_lo in range(2):
        for y in range(4):
            for z in range(4):
                for x_hi in range(2):
                    for core in range(2):
                        yield x_lo, y, z, x_hi, core


def number(x_lo, y, z, x_hi, core):
    return ((x_lo * 4 + y) * 4 + z) * 4 + x_hi * 2 + core


def move(value, target):
    pairs = [(number(*place), number(*target(*place))) for place in places()]
    return lax.ppermute(value, AXES, pairs)


def to_core(value):
    return move(value, lambda x_lo, y, z, x_hi, core: (x_lo, y, z, x_hi, 1 - core))


def to_x_hi(value):
    return move(value, lambda x_lo, y, z, x_hi, core: (x_lo, y, z, 1 - x_hi, core))


def to_x_lo(value):
    return move(value, lambda x_lo, y, z, x_hi, core: (1 - x_lo, y, z, x_hi, core))


def to_y(value, steps):
    return move(value, lambda x_lo, y, z, x_hi, core: (x_lo, (y + steps) % 4, z, x_hi, core))


def to_z(value, steps):
    return move(value, lambda x_lo, y, z, x_hi, core: (x_lo, y, (z + steps) % 4, x_hi, core))


EDGE = 15


def along_ctx(value, steps):
    pairs = [(s, s + steps) for s in range(32) if 0 <= s + steps < 32]
    return lax.ppermute(value, "ctx", pairs)


def middle(source, sign):
    return source // 4 * 4 + (source % 4 - sign) % 4


def two_pairs(sign):
    sources = [s for s in range(32) if 0 <= s + 2 * sign < 32]
    return [(s, middle(s, sign), s + 2 * sign) for s in sources]


def first_hop(value, sign):
    return lax.ppermute(value, "ctx", [(s, m) for s, m, _ in two_pairs(sign)])


def second_hop(value, sign):
    return lax.ppermute(value, "ctx", [(m, t) for _, m, t in two_pairs(sign)])


def block_rule(spans, pairs, query_block, key_block):
    listed = jnp.any(
        (pairs[:, 0] == query_block[..., None]) & (pairs[:, 1] == key_block[..., None]), axis=-1
    )
    span_lower = spans[:, 0]
    span_upper = spans[:, 0] + spans[:, 1]
    query_inside = (span_lower <= query_block[..., None]) & (query_block[..., None] < span_upper)
    key_inside = (span_lower <= key_block[..., None]) & (key_block[..., None] < span_upper)
    same = jnp.any(query_inside & key_inside, axis=-1)
    reach = (query_block - key_block >= 0) & (query_block - key_block < WIN)
    return listed & same & reach


def dot(a, b, dims):
    return lax.dot_general(a, b, dims, preferred_element_type=f32)


def causal():
    key_row = lax.broadcasted_iota(jnp.int32, (BLK, BLK), 0)
    query_column = lax.broadcasted_iota(jnp.int32, (BLK, BLK), 1)
    return key_row <= query_column


def block_rows(index):
    return pl.ds(index * BLK, BLK)


OWN_TILES = ((0, 0, 0), (1, 0, 1), (1, 1, 0))
BEHIND_TILES = ((0, 3, 0), (0, 2, 1), (0, 1, 2), (1, 3, 1), (1, 2, 2))


def key_value(index, near_k, near_v, edge_v, far):
    if index == 0:
        return far[0], far[1]
    rows = block_rows(index - 1)
    return near_k[rows, :], near_v[rows, :] + edge_v[rows, :]


def absorb(keys, vals, query, top, total, acc, rows):
    s = dot(keys, query, NT)
    old = top
    m = jnp.maximum(old, jnp.max(s, axis=0, keepdims=True))
    p = jnp.exp2(s * SCALE2 - m * SCALE2)
    fix = jnp.exp2((old - m) * SCALE2)
    part = dot(vals.T, p.astype(bf16), NN)
    acc[:, rows] = acc[:, rows] * fix + part
    return m, total * fix + jnp.sum(p, axis=0, keepdims=True)


def forward_own_kernel(flags, q_ref, k_ref, v_ref, after, acc, top, total):
    for qb, o, index in OWN_TILES:
        rows = block_rows(qb)
        line = slice(qb, qb + 1)

        def diagonal(rows=rows, line=line):
            s = jnp.where(causal(), dot(k_ref[rows, :], q_ref[rows, :], NT), -jnp.inf)
            m = jnp.max(s, axis=0, keepdims=True)
            p = jnp.exp2(s * SCALE2 - m * SCALE2)
            acc[:, rows] = dot(v_ref[rows, :].T, p.astype(bf16), NN)
            top[0, line, :] = m
            total[0, line, :] = jnp.sum(p, axis=0, keepdims=True)

        def nothing(rows=rows, line=line):
            acc[:, rows] = jnp.zeros((HDIM, BLK), f32)
            top[0, line, :] = jnp.zeros((1, BLK), f32)
            total[0, line, :] = jnp.ones((1, BLK), f32)

        def tile(rows=rows, line=line, index=index):
            held = block_rows(index)
            top[0, line, :], total[0, line, :] = absorb(
                k_ref[held, :], v_ref[held, :], q_ref[rows, :],
                top[0, line, :], total[0, line, :], acc, rows,
            )

        listed = flags[qb * WIN + o] == 1
        if o == 0:
            pl.when(listed)(diagonal)
            pl.when(jnp.logical_not(listed))(nothing)
        else:
            pl.when(listed)(tile)


def forward_behind_kernel(
    flags, q_ref, k1_ref, v1_ref, v0_ref, far_ref, acc_in, top_in, total_in,
    after, out_ref, turned_ref, log_ref, acc, top, total,
):
    acc[...] = acc_in[...]
    top[...] = top_in[0]
    total[...] = total_in[0]
    for qb, o, index in BEHIND_TILES:
        rows = block_rows(qb)
        line = slice(qb, qb + 1)

        @pl.when(flags[qb * WIN + o] == 1)
        def _(rows=rows, line=line, index=index):
            keys, vals = key_value(index, k1_ref, v1_ref, v0_ref, far_ref)
            top[line, :], total[line, :] = absorb(
                keys, vals, q_ref[rows, :], top[line, :], total[line, :], acc, rows
            )

    for qb in range(2):
        rows = block_rows(qb)
        result = acc[:, rows] * (1.0 / total[qb : qb + 1, :])
        turned_ref[:, rows] = result.astype(bf16)
        out_ref[rows, :] = result.T.astype(bf16)
    log_ref[0] = top[...] * SCALE2 + jnp.log2(total[...])


def tile_grads(keys, vals, query, grad, log_sum, delta, diagonal):
    p = jnp.exp2(dot(keys, query, NT) * SCALE2 - log_sum)
    if diagonal:
        p = jnp.where(causal(), p, 0.0)
    value_part = dot(p.astype(bf16), grad, NN)
    dp = dot(vals, grad, NT)
    ds = (p * (dp - delta)).astype(bf16)
    return dot(ds, query, NN), value_part, dot(keys.T, ds, NN)


def backward_behind_kernel(
    flags, q_ref, k1_ref, v1_ref, v0_ref, far_ref, out_ref, grad_ref, log_ref,
    after, near_back, far_back, dq, delta_ref, dk, dv,
):
    dk[...] = jnp.zeros_like(dk)
    dv[...] = jnp.zeros_like(dv)
    dq[...] = jnp.zeros_like(dq)
    product = grad_ref[...].astype(f32) * out_ref[...].astype(f32)
    delta = jnp.sum(product.T, axis=0, keepdims=True)
    for qb in range(2):
        delta_ref[0, qb : qb + 1, :] = delta[:, qb * BLK : (qb + 1) * BLK]
    for qb, o, index in BEHIND_TILES:
        rows = block_rows(qb)
        line = slice(qb, qb + 1)

        @pl.when(flags[qb * WIN + o] == 1)
        def _(rows=rows, line=line, index=index):
            keys, vals = key_value(index, k1_ref, v1_ref, v0_ref, far_ref)
            key_part, value_part, query_part = tile_grads(
                keys, vals, q_ref[rows, :], grad_ref[rows, :],
                log_ref[0, line, :], delta_ref[0, line, :], False,
            )
            dk[block_rows(index), :] += key_part
            dv[block_rows(index), :] += value_part
            dq[:, rows] += query_part

    far_back[0] = (dk[block_rows(0), :] * SCALE).astype(bf16)
    far_back[1] = dv[block_rows(0), :].astype(bf16)
    near_back[0] = (dk[pl.ds(BLK, 2 * BLK), :] * SCALE).astype(bf16)
    near_back[1] = dv[pl.ds(BLK, 2 * BLK), :].astype(bf16)


def backward_own_kernel(
    flags, q_ref, k_ref, v_ref, grad_ref, log_ref, dq_in, delta_ref, after,
    dq_ref, own_ref, dk, dv, dq,
):
    dk[...] = jnp.zeros_like(dk)
    dv[...] = jnp.zeros_like(dv)
    dq[...] = dq_in[...]
    for qb, o, index in OWN_TILES:
        rows = block_rows(qb)
        line = slice(qb, qb + 1)

        @pl.when(flags[qb * WIN + o] == 1)
        def _(rows=rows, line=line, index=index, o=o):
            held = block_rows(index)
            key_part, value_part, query_part = tile_grads(
                k_ref[held, :], v_ref[held, :], q_ref[rows, :], grad_ref[rows, :],
                log_ref[0, line, :], delta_ref[0, line, :], o == 0,
            )
            dk[held, :] += key_part
            dv[held, :] += value_part
            dq[:, rows] += query_part

    own_ref[0] = (dk[...] * SCALE).astype(bf16)
    own_ref[1] = dv[...].astype(bf16)
    dq_ref[...] = (dq[...] * SCALE).T.astype(bf16)


def finish_kernel(place, own_ref, near_ref, far_ref, after, key_ref, value_ref):
    for part, result in enumerate((key_ref, value_ref)):
        for block in range(2):
            rows = block_rows(block)
            total = own_ref[part, rows, :].astype(f32) + near_ref[part, rows, :].astype(f32)
            if block == 1:
                total += far_ref[part].astype(f32)
            result[rows, :] = total.astype(bf16)


def head(rows):
    return pl.BlockSpec((rows, HDIM), lambda h, *_: (0, h))


def head_pair(rows):
    return pl.BlockSpec((2, rows, HDIM), lambda h, *_: (0, 0, h))


HEAD_LINES = pl.BlockSpec((1, 2, BLK), lambda h, *_: (h, 0, 0))
ANY = pl.BlockSpec(memory_space=pl.ANY)
HEAD_TURNED = pl.BlockSpec((HDIM, 1024), lambda h, *_: (h, 0))


def shape(dims, dtype):
    return jax.ShapeDtypeStruct(dims, dtype)


WIDTH = 512
HEADS = WIDTH // HDIM
LINES = shape((HEADS, 2, BLK), f32)
TURNED = shape((WIDTH, 1024), f32)


def call(kernel, name, grid, ins, outs, out_shape, scratch, args):
    return pl.pallas_call(
        kernel,
        grid_spec=pltpu.PrefetchScalarGridSpec(
            num_scalar_prefetch=1,
            grid=grid,
            in_specs=ins,
            out_specs=outs,
            scratch_shapes=scratch,
        ),
        out_shape=out_shape,
        compiler_params=pltpu.CompilerParams(vmem_limit_bytes=64 << 20),
        cost_estimate=pl.CostEstimate(flops=1, bytes_accessed=1, transcendentals=0),
        name=name,
    )(*args)


def forward_own(flags, q, k, v, after):
    return call(
        forward_own_kernel, "forward_own", (HEADS,),
        [head(1024)] * 3 + [ANY],
        [HEAD_TURNED, HEAD_LINES, HEAD_LINES],
        [TURNED, LINES, LINES],
        [], (flags, q, k, v, after),
    )


def forward_behind(flags, q, near_k, near_v, edge_v, far, state, after):
    lines = pltpu.VMEM((2, BLK), f32)
    return call(
        forward_behind_kernel, "forward_behind", (HEADS,),
        [head(1024)] * 4 + [head_pair(512)]
        + [HEAD_TURNED, HEAD_LINES, HEAD_LINES, ANY],
        [head(1024), HEAD_TURNED, HEAD_LINES],
        [shape((1024, WIDTH), bf16), shape((WIDTH, 1024), bf16), LINES],
        [pltpu.VMEM((HDIM, 1024), f32), lines, lines],
        (flags, q, near_k, near_v, edge_v, far, *state, after),
    )


def backward_behind(
    flags, q, near_k, near_v, edge_v, far, out, grad, log_sum, after
):
    held = pltpu.VMEM((3 * BLK, HDIM), f32)
    return call(
        backward_behind_kernel, "backward_behind", (HEADS,),
        [head(1024)] * 4 + [head_pair(512)]
        + [head(1024), head(1024), HEAD_LINES, ANY],
        [head_pair(1024), head_pair(512), HEAD_TURNED, HEAD_LINES],
        [shape((2, 1024, WIDTH), bf16), shape((2, 512, WIDTH), bf16), TURNED, LINES],
        [held, held], (flags, q, near_k, near_v, edge_v, far, out, grad, log_sum, after),
    )


def backward_own(flags, q, k, v, grad, log_sum, dq, delta, after):
    held = pltpu.VMEM((2 * BLK, HDIM), f32)
    return call(
        backward_own_kernel, "backward_own", (HEADS,),
        [head(1024)] * 4 + [HEAD_LINES, HEAD_TURNED, HEAD_LINES, ANY],
        [head(1024), head_pair(1024)],
        [shape((1024, WIDTH), bf16), shape((2, 1024, WIDTH), bf16)],
        [held, held, pltpu.VMEM((HDIM, 1024), f32)],
        (flags, q, k, v, grad, log_sum, dq, delta, after),
    )


def finish(place, own, near, far, after):
    return call(
        finish_kernel, "key_value_sum", (HEADS,),
        [head_pair(1024)] * 2 + [head_pair(512), ANY],
        [head(1024), head(1024)],
        [shape((1024, WIDTH), bf16)] * 2,
        [], (place, own, near, far, after),
    )


def pack_kernel(place, k_ref, v_ref, second_ref, held_ref):
    held_ref[...] = k_ref[...]

    @pl.when(pl.program_id(0) == 1)
    def _():
        second_ref[0] = k_ref[...]
        second_ref[1] = v_ref[...]


def pack(place, k, v):
    block = pl.BlockSpec((BLK, WIDTH), lambda i, place: (i, 0))
    return call(
        pack_kernel, "second_blocks", (2,),
        [block, pl.BlockSpec((BLK, WIDTH), lambda i, place: (1, 0))],
        [pl.BlockSpec((2, BLK, WIDTH), lambda i, place: (0, 0, 0)), block],
        [shape((2, BLK, WIDTH), bf16), shape(k.shape, bf16)], [], (place, k, v),
    )


def nothing_kernel(*refs):
    pass


def together(values, after=()):
    return pl.pallas_call(
        nothing_kernel,
        in_specs=[ANY] * (len(values) + len(after)),
        out_specs=[ANY] * len(values),
        out_shape=[shape(value.shape, value.dtype) for value in values],
        input_output_aliases={index: index for index in range(len(values))},
        compiler_params=pltpu.CompilerParams(vmem_limit_bytes=64 << 20),
        name="order",
    )(*values, *after)


def grad_kernel(place, a_ref, b_ref, wa_ref, wb_ref, *rest):
    total = dot(a_ref[...], wa_ref[...], NT) + dot(b_ref[...], wb_ref[...], NT)
    if len(rest) == 3:
        total += rest[0][...]
    rest[-1][...] = total.astype(rest[-1].dtype)


def grad_terms(place, first, a, b, weight, before, after):
    tile = 512
    row = pl.BlockSpec((tile, 1024), lambda i, place: (i, 0))
    result = pl.BlockSpec((tile, 512), lambda i, place: (i, 0))

    def columns(flip):
        return pl.BlockSpec((512, 1024), lambda i, place: (0, place[0] ^ flip))

    more = [] if before is None else [before]
    return call(
        grad_kernel, "projection_backward", (1024 // tile,),
        [row, row, columns(first), columns(first + 1)] + [result] * len(more) + [ANY], result,
        shape((1024, 512), bf16 if more else f32), [], (place, a, b, weight, weight, *more, after),
    )


def weight_kernel(place, turned_ref, g0, g1, g2, g3, after, *outs):
    owner = place[0] ^ pl.program_id(0)
    y = owner % 2 * 2 + pl.program_id(1)
    for part, ref in enumerate((g0, g1, g2, g3)):
        for slot, out_ref in enumerate(outs):

            @pl.when((pl.program_id(0) == part) & ((y - place[1] + 3) % 4 == slot))
            def _(ref=ref, out_ref=out_ref, part=part):
                out_ref[part // 2] = dot(turned_ref[...], ref[...], NN).astype(bf16)


def weight_terms(place, turned, cotangents, after):
    def piece(part):
        return pl.BlockSpec(
            (1024, 512),
            lambda i, half, place: (
                0, jnp.where(i == part, half, jnp.where(i < part, 0, 1)),
            ),
        )

    return call(
        weight_kernel, "weight_gradient", (4, 2),
        [pl.BlockSpec((512, 1024), lambda i, half, place: (0, 0))] + [piece(p) for p in range(4)]
        + [ANY],
        [pl.BlockSpec((2, 512, 512), lambda i, half, place: (0, 0, 0))] * 4,
        [shape((2, 512, 512), bf16)] * 4, [], (place, turned, *cotangents, after),
    )


def over_y(parts):
    return [to_y(parts[s], s + 1) for s in (0, 2, 1)]


def y_sum_kernel(place, a, b, c, d, after, kept_ref, sent_ref):
    def total(index):
        return sum(ref[index].astype(f32) for ref in (a, b, c, d)).astype(bf16)

    kept = place[3] ^ (place[0] // 2)
    kept_ref[...] = total(kept)
    sent_ref[...] = total(1 - kept)


def weight_y_sum(place, terms, after):
    result = pl.BlockSpec((256, 512), lambda i, place: (i, 0))
    return call(
        y_sum_kernel, "weight_y_sum", (2,),
        [pl.BlockSpec((2, 256, 512), lambda i, place: (0, i, 0))] * 4 + [ANY],
        [result] * 2, [shape((512, 512), bf16)] * 2, [], (place, *terms, after),
    )


def pieces_kernel(place, a, b, after, *outs):
    for slot, out_ref in enumerate(outs):

        @pl.when(pl.program_id(0) == slot)
        def _(out_ref=out_ref):
            out_ref[...] = (a[...].astype(f32) + b[...].astype(f32)).astype(bf16)


def pieces_by_z(place, a, b, after):
    piece = pl.BlockSpec((512, 128), lambda i, place: (0, (place[2] + i + 1) % 4))
    return call(
        pieces_kernel, "weight_by_z", (4,), [piece] * 2 + [ANY],
        [pl.BlockSpec((512, 128), lambda i, place: (0, 0))] * 4,
        [shape((512, 128), bf16)] * 4, [], (place, a, b, after),
    )


def copy_kernel(place, in_ref, *refs):
    refs[-1][...] = in_ref[...]


def far_columns(place, weight, after):
    return call(
        copy_kernel, "projection_far", (2,),
        [pl.BlockSpec((256, 2048), lambda i, place: (i, 1 - place[0] // 2)), ANY],
        pl.BlockSpec((256, 2048), lambda i, place: (i, 0)),
        shape((512, 2048), bf16), [], (place, weight, after),
    )


def core_kernel(place, own_ref, far_ref, far_rows, own_rows, after, out_ref):
    out_ref[0] = own_ref[...]
    out_ref[1] = far_ref[...]
    for part, rows in ((2, far_rows), (3, own_rows)):
        for half in range(2):
            out_ref[part, :, block_rows(half)] = rows[block_rows(half), :]


def for_core(place, weight, far_weight, far_attention, attention, after):
    rows = pl.BlockSpec((1024, 512), lambda i, place: (0, 0))
    return call(
        core_kernel, "for_core", (1,),
        [
            pl.BlockSpec((512, 1024), lambda i, place: (0, place[0] ^ 1)),
            pl.BlockSpec((512, 1024), lambda i, place: (0, 1 - place[0] % 2)),
            rows, rows, ANY,
        ],
        pl.BlockSpec((4, 512, 1024), lambda i, place: (0, 0, 0)),
        shape((4, 512, 1024), bf16), [],
        (place, weight, far_weight, far_attention, attention, after),
    )


def mix_kernel(place, own, core, far, far_core, w_own, w_far, w_core, after, out_ref):
    total = dot(own[...], w_own[...], NN) + dot(core[0], w_core[0], NN)
    total += dot(far[...], w_far[...], NN) + dot(far_core[0], w_core[1], NN)
    out_ref[...] = total.astype(bf16)


def mix(place, attention, far_attention, weight, far_weight, from_core, after):
    rows = pl.BlockSpec((512, 512), lambda i, place: (i, 0))
    return call(
        mix_kernel, "projection", (2,),
        [
            rows,
            pl.BlockSpec((1, 512, 512), lambda i, place: (3, 0, i)),
            rows,
            pl.BlockSpec((1, 512, 512), lambda i, place: (2, 0, i)),
            pl.BlockSpec((512, 1024), lambda i, place: (0, place[0])),
            pl.BlockSpec((512, 1024), lambda i, place: (0, place[0] % 2)),
            pl.BlockSpec((2, 512, 1024), lambda i, place: (0, 0, 0)),
            ANY,
        ],
        pl.BlockSpec((512, 1024), lambda i, place: (i, 0)),
        shape((1024, 1024), bf16), [],
        (place, attention, from_core, far_attention, from_core, weight, far_weight, from_core, after),
    )


def per_device(queries, keys, values, out_weight, out_grad, spans, pairs):
    ctx = lax.axis_index("ctx")
    tp = lax.axis_index("tp")
    place = jnp.stack([tp, ctx // 4 % 4, ctx % 4, ctx // 16]).astype(jnp.int32)

    far_grad = to_x_hi(out_grad)
    near_pairs = [(s, s + 1) for s in range(31) if s != EDGE]
    near_values = lax.ppermute(values, "ctx", near_pairs + [(EDGE, 0)])
    core_grad = to_core(out_grad)
    second, held_keys = pack(place, keys, values)
    far_moved = first_hop(second, 1)

    query_block = ctx * 2 + jnp.arange(2, dtype=jnp.int32)[:, None] + jnp.zeros((1, WIN), jnp.int32)
    key_block = query_block - jnp.arange(WIN, dtype=jnp.int32)[None, :]
    flags = block_rule(spans, pairs, query_block, key_block).astype(jnp.int32).reshape(-1)
    own_state = forward_own(flags, queries, keys, values, keys)
    far_weight = far_columns(place, out_weight, own_state[1])
    terms = grad_terms(place, 0, out_grad, core_grad, out_weight, None, far_weight)

    [far_moved] = together([far_moved], [terms])
    far = second_hop(far_moved, 1)
    near_values, held_keys = together([near_values, held_keys], [far_moved])
    near_keys = along_ctx(held_keys, 1)
    edge_values = lax.ppermute(near_values, "ctx", [(0, EDGE + 1)])
    near_keys, far, far_grad, edge_values, far_weight = together(
        [near_keys, far, far_grad, edge_values, far_weight], [far_moved]
    )

    far_core_grad = to_core(far_grad)
    far_weight = to_x_hi(far_weight)
    behind = (flags, queries, near_keys, near_values, edge_values, far)
    attention, turned, log_sum = forward_behind(*behind, own_state, far)
    [far_core_grad] = together([far_core_grad], [log_sum])
    far_attention = to_x_hi(attention)
    attn_grad = grad_terms(place, 2, far_grad, far_core_grad, out_weight, terms, far_core_grad)
    cotangents = (out_grad, core_grad, far_grad, far_core_grad)
    weight_parts = weight_terms(place, turned, cotangents, attn_grad)
    weight_moved = over_y(weight_parts)
    near_back, far_back, dq, delta = backward_behind(
        *behind, attention, attn_grad, log_sum, weight_parts[3]
    )
    far_back, far_weight = together([far_back, far_weight])
    query_grad, own = backward_own(
        flags, queries, keys, values, attn_grad, log_sum, dq, delta, delta
    )

    back_moved = first_hop(far_back, -1)
    [far_attention] = together([far_attention], [own])
    from_core = for_core(place, out_weight, far_weight, far_attention, attention, own)

    *weight_moved, near_back, back_moved, from_core = together(
        [*weight_moved, near_back, back_moved, from_core]
    )
    near_back = along_ctx(near_back, -1)
    far_back = second_hop(back_moved, -1)
    from_core = to_core(from_core)
    kept, sent = weight_y_sum(place, [weight_parts[3], *weight_moved], weight_moved[0])
    sent = to_x_lo(sent)
    mixed = mix(place, attention, far_attention, out_weight, far_weight, from_core, kept)
    weight_pieces = pieces_by_z(place, kept, sent, mixed)
    weight_moved = [to_z(weight_pieces[s], s + 1) for s in (0, 2, 1)]
    key_grad, value_grad = finish(place, own, near_back, far_back, weight_pieces[3])
    weight_moved = together(weight_moved, [key_grad])
    weight_grad = sum(piece.astype(f32) for piece in [weight_pieces[3], *weight_moved])
    return (mixed, query_grad, key_grad, value_grad, weight_grad)


def solution(mesh):
    placed = (
        P("ctx", "tp"),
        P("ctx", "tp"),
        P("ctx", "tp"),
        P("tp", None),
        P("ctx", "tp"),
        P(),
        P(),
    )
    return jax.shard_map(
        per_device,
        mesh=mesh,
        in_specs=placed,
        out_specs=(P("ctx", "tp"), P("ctx", "tp"), P("ctx", "tp"), P("ctx", "tp"), P("tp", "ctx")),
        check_vma=False,
    )
```

```python
import functools
import math

import jax
import jax.numpy as jnp
from jax import lax
from jax.experimental import pallas as pl
from jax.experimental.pallas import tpu as pltpu
from jax.sharding import PartitionSpec as P

HDIM = 128
BLK = 512
WIN = 4
SCALE = 1.0 / math.sqrt(HDIM)
SCALE2 = SCALE * math.log2(math.e)
AXES = ("ctx", "tp")
NT = (((1,), (1,)), ((), ()))
NN = (((1,), (0,)), ((), ()))
f32 = jnp.float32
bf16 = jnp.bfloat16


def places():
    for x_lo in range(2):
        for y in range(4):
            for z in range(4):
                for x_hi in range(2):
                    for core in range(2):
                        yield x_lo, y, z, x_hi, core


def number(x_lo, y, z, x_hi, core):
    return ((x_lo * 4 + y) * 4 + z) * 4 + x_hi * 2 + core


def move(value, target):
    pairs = [(number(*place), number(*target(*place))) for place in places()]
    return lax.ppermute(value, AXES, pairs)


def to_core(value):
    return move(value, lambda x_lo, y, z, x_hi, core: (x_lo, y, z, x_hi, 1 - core))


def to_x_hi(value):
    return move(value, lambda x_lo, y, z, x_hi, core: (x_lo, y, z, 1 - x_hi, core))


def to_x_lo(value):
    return move(value, lambda x_lo, y, z, x_hi, core: (1 - x_lo, y, z, x_hi, core))


def to_y(value, steps):
    return move(value, lambda x_lo, y, z, x_hi, core: (x_lo, (y + steps) % 4, z, x_hi, core))


def to_z(value, steps):
    return move(value, lambda x_lo, y, z, x_hi, core: (x_lo, y, (z + steps) % 4, x_hi, core))


EDGE = 15


def along_ctx(value, steps):
    pairs = [(s, s + steps) for s in range(32) if 0 <= s + steps < 32]
    return lax.ppermute(value, "ctx", pairs)


def middle(source, sign):
    return source // 4 * 4 + (source % 4 - sign) % 4


def two_pairs(sign):
    sources = [s for s in range(32) if 0 <= s + 2 * sign < 32]
    return [(s, middle(s, sign), s + 2 * sign) for s in sources]


def first_hop(value, sign):
    return lax.ppermute(value, "ctx", [(s, m) for s, m, _ in two_pairs(sign)])


def second_hop(value, sign):
    return lax.ppermute(value, "ctx", [(m, t) for _, m, t in two_pairs(sign)])


def block_rule(spans, pairs, query_block, key_block):
    listed = jnp.any(
        (pairs[:, 0] == query_block[..., None]) & (pairs[:, 1] == key_block[..., None]), axis=-1
    )
    span_lower = spans[:, 0]
    span_upper = spans[:, 0] + spans[:, 1]
    query_inside = (span_lower <= query_block[..., None]) & (query_block[..., None] < span_upper)
    key_inside = (span_lower <= key_block[..., None]) & (key_block[..., None] < span_upper)
    same = jnp.any(query_inside & key_inside, axis=-1)
    reach = (query_block - key_block >= 0) & (query_block - key_block < WIN)
    return listed & same & reach


def dot(a, b, dims):
    return lax.dot_general(a, b, dims, preferred_element_type=f32)


def causal():
    key_row = lax.broadcasted_iota(jnp.int32, (BLK, BLK), 0)
    query_column = lax.broadcasted_iota(jnp.int32, (BLK, BLK), 1)
    return key_row <= query_column


def block_rows(index):
    return pl.ds(index * BLK, BLK)


OWN_TILES = ((0, 0, 0), (1, 0, 1), (1, 1, 0))
BEHIND_TILES = ((0, 3, 0), (0, 2, 1), (0, 1, 2), (1, 3, 1), (1, 2, 2))


def key_value(index, near_k, near_v, edge_v, far):
    if index == 0:
        return far[0], far[1]
    rows = block_rows(index - 1)
    return near_k[rows, :], near_v[rows, :] + edge_v[rows, :]


def absorb(keys, vals, query, top, total, acc, rows):
    s = dot(keys, query, NT)
    old = top
    m = jnp.maximum(old, jnp.max(s, axis=0, keepdims=True))
    p = jnp.exp2(s * SCALE2 - m * SCALE2)
    fix = jnp.exp2((old - m) * SCALE2)
    part = dot(vals.T, p.astype(bf16), NN)
    acc[:, rows] = acc[:, rows] * fix + part
    return m, total * fix + jnp.sum(p, axis=0, keepdims=True)


def forward_own_kernel(flags, q_ref, k_ref, v_ref, after, acc, top, total):
    for qb, o, index in OWN_TILES:
        rows = block_rows(qb)
        line = slice(qb, qb + 1)

        def diagonal(rows=rows, line=line):
            s = jnp.where(causal(), dot(k_ref[rows, :], q_ref[rows, :], NT), -jnp.inf)
            m = jnp.max(s, axis=0, keepdims=True)
            p = jnp.exp2(s * SCALE2 - m * SCALE2)
            acc[:, rows] = dot(v_ref[rows, :].T, p.astype(bf16), NN)
            top[0, line, :] = m
            total[0, line, :] = jnp.sum(p, axis=0, keepdims=True)

        def nothing(rows=rows, line=line):
            acc[:, rows] = jnp.zeros((HDIM, BLK), f32)
            top[0, line, :] = jnp.zeros((1, BLK), f32)
            total[0, line, :] = jnp.ones((1, BLK), f32)

        def tile(rows=rows, line=line, index=index):
            held = block_rows(index)
            top[0, line, :], total[0, line, :] = absorb(
                k_ref[held, :], v_ref[held, :], q_ref[rows, :],
                top[0, line, :], total[0, line, :], acc, rows,
            )

        listed = flags[qb * WIN + o] == 1
        if o == 0:
            pl.when(listed)(diagonal)
            pl.when(jnp.logical_not(listed))(nothing)
        else:
            pl.when(listed)(tile)


def forward_behind_kernel(
    flags, q_ref, k1_ref, v1_ref, v0_ref, far_ref, acc_in, top_in, total_in,
    after, out_ref, turned_ref, log_ref, acc, top, total,
):
    acc[...] = acc_in[...]
    top[...] = top_in[0]
    total[...] = total_in[0]
    for qb, o, index in BEHIND_TILES:
        rows = block_rows(qb)
        line = slice(qb, qb + 1)

        @pl.when(flags[qb * WIN + o] == 1)
        def _(rows=rows, line=line, index=index):
            keys, vals = key_value(index, k1_ref, v1_ref, v0_ref, far_ref)
            top[line, :], total[line, :] = absorb(
                keys, vals, q_ref[rows, :], top[line, :], total[line, :], acc, rows
            )

    for qb in range(2):
        rows = block_rows(qb)
        result = acc[:, rows] * (1.0 / total[qb : qb + 1, :])
        turned_ref[:, rows] = result.astype(bf16)
        out_ref[rows, :] = result.T.astype(bf16)
    log_ref[0] = top[...] * SCALE2 + jnp.log2(total[...])


def tile_grads(keys, vals, query, grad, log_sum, delta, diagonal):
    p = jnp.exp2(dot(keys, query, NT) * SCALE2 - log_sum)
    if diagonal:
        p = jnp.where(causal(), p, 0.0)
    value_part = dot(p.astype(bf16), grad, NN)
    dp = dot(vals, grad, NT)
    ds = (p * (dp - delta)).astype(bf16)
    return dot(ds, query, NN), value_part, dot(keys.T, ds, NN)


def backward_behind_kernel(
    flags, q_ref, k1_ref, v1_ref, v0_ref, far_ref, out_ref, grad_ref, log_ref,
    after, near_back, far_back, dq, delta_ref, dk, dv,
):
    dk[...] = jnp.zeros_like(dk)
    dv[...] = jnp.zeros_like(dv)
    dq[...] = jnp.zeros_like(dq)
    product = grad_ref[...].astype(f32) * out_ref[...].astype(f32)
    delta = jnp.sum(product.T, axis=0, keepdims=True)
    for qb in range(2):
        delta_ref[0, qb : qb + 1, :] = delta[:, qb * BLK : (qb + 1) * BLK]
    for qb, o, index in BEHIND_TILES:
        rows = block_rows(qb)
        line = slice(qb, qb + 1)

        @pl.when(flags[qb * WIN + o] == 1)
        def _(rows=rows, line=line, index=index):
            keys, vals = key_value(index, k1_ref, v1_ref, v0_ref, far_ref)
            key_part, value_part, query_part = tile_grads(
                keys, vals, q_ref[rows, :], grad_ref[rows, :],
                log_ref[0, line, :], delta_ref[0, line, :], False,
            )
            dk[block_rows(index), :] += key_part
            dv[block_rows(index), :] += value_part
            dq[:, rows] += query_part

    far_back[0] = (dk[block_rows(0), :] * SCALE).astype(bf16)
    far_back[1] = dv[block_rows(0), :].astype(bf16)
    near_back[0] = (dk[pl.ds(BLK, 2 * BLK), :] * SCALE).astype(bf16)
    near_back[1] = dv[pl.ds(BLK, 2 * BLK), :].astype(bf16)


def backward_own_kernel(
    flags, q_ref, k_ref, v_ref, grad_ref, log_ref, dq_in, delta_ref, after,
    dq_ref, own_ref, dk, dv, dq,
):
    dk[...] = jnp.zeros_like(dk)
    dv[...] = jnp.zeros_like(dv)
    dq[...] = dq_in[...]
    for qb, o, index in OWN_TILES:
        rows = block_rows(qb)
        line = slice(qb, qb + 1)

        @pl.when(flags[qb * WIN + o] == 1)
        def _(rows=rows, line=line, index=index, o=o):
            held = block_rows(index)
            key_part, value_part, query_part = tile_grads(
                k_ref[held, :], v_ref[held, :], q_ref[rows, :], grad_ref[rows, :],
                log_ref[0, line, :], delta_ref[0, line, :], o == 0,
            )
            dk[held, :] += key_part
            dv[held, :] += value_part
            dq[:, rows] += query_part

    own_ref[0] = (dk[...] * SCALE).astype(bf16)
    own_ref[1] = dv[...].astype(bf16)
    dq_ref[...] = (dq[...] * SCALE).T.astype(bf16)


def finish_kernel(place, own_ref, near_ref, far_ref, after, key_ref, value_ref):
    for part, result in enumerate((key_ref, value_ref)):
        for block in range(2):
            rows = block_rows(block)
            total = own_ref[part, rows, :].astype(f32) + near_ref[part, rows, :].astype(f32)
            if block == 1:
                total += far_ref[part].astype(f32)
            result[rows, :] = total.astype(bf16)


def head(rows):
    return pl.BlockSpec((rows, HDIM), lambda h, *_: (0, h))


def head_pair(rows):
    return pl.BlockSpec((2, rows, HDIM), lambda h, *_: (0, 0, h))


HEAD_LINES = pl.BlockSpec((1, 2, BLK), lambda h, *_: (h, 0, 0))
ANY = pl.BlockSpec(memory_space=pl.ANY)
HEAD_TURNED = pl.BlockSpec((HDIM, 1024), lambda h, *_: (h, 0))


def shape(dims, dtype):
    return jax.ShapeDtypeStruct(dims, dtype)


WIDTH = 512
HEADS = WIDTH // HDIM
LINES = shape((HEADS, 2, BLK), f32)
TURNED = shape((WIDTH, 1024), f32)


def call(kernel, name, grid, ins, outs, out_shape, scratch, args):
    return pl.pallas_call(
        kernel,
        grid_spec=pltpu.PrefetchScalarGridSpec(
            num_scalar_prefetch=1,
            grid=grid,
            in_specs=ins,
            out_specs=outs,
            scratch_shapes=scratch,
        ),
        out_shape=out_shape,
        compiler_params=pltpu.CompilerParams(vmem_limit_bytes=64 << 20),
        cost_estimate=pl.CostEstimate(flops=1, bytes_accessed=1, transcendentals=0),
        name=name,
    )(*args)


def forward_own(flags, q, k, v, after):
    return call(
        forward_own_kernel, "forward_own", (HEADS,),
        [head(1024)] * 3 + [ANY],
        [HEAD_TURNED, HEAD_LINES, HEAD_LINES],
        [TURNED, LINES, LINES],
        [], (flags, q, k, v, after),
    )


def forward_behind(flags, q, near_k, near_v, edge_v, far, state, after):
    lines = pltpu.VMEM((2, BLK), f32)
    return call(
        forward_behind_kernel, "forward_behind", (HEADS,),
        [head(1024)] * 4 + [head_pair(512)]
        + [HEAD_TURNED, HEAD_LINES, HEAD_LINES, ANY],
        [head(1024), HEAD_TURNED, HEAD_LINES],
        [shape((1024, WIDTH), bf16), shape((WIDTH, 1024), bf16), LINES],
        [pltpu.VMEM((HDIM, 1024), f32), lines, lines],
        (flags, q, near_k, near_v, edge_v, far, *state, after),
    )


def backward_behind(
    flags, q, near_k, near_v, edge_v, far, out, grad, log_sum, after
):
    held = pltpu.VMEM((3 * BLK, HDIM), f32)
    return call(
        backward_behind_kernel, "backward_behind", (HEADS,),
        [head(1024)] * 4 + [head_pair(512)]
        + [head(1024), head(1024), HEAD_LINES, ANY],
        [head_pair(1024), head_pair(512), HEAD_TURNED, HEAD_LINES],
        [shape((2, 1024, WIDTH), bf16), shape((2, 512, WIDTH), bf16), TURNED, LINES],
        [held, held], (flags, q, near_k, near_v, edge_v, far, out, grad, log_sum, after),
    )


def backward_own(flags, q, k, v, grad, log_sum, dq, delta, after):
    held = pltpu.VMEM((2 * BLK, HDIM), f32)
    return call(
        backward_own_kernel, "backward_own", (HEADS,),
        [head(1024)] * 4 + [HEAD_LINES, HEAD_TURNED, HEAD_LINES, ANY],
        [head(1024), head_pair(1024)],
        [shape((1024, WIDTH), bf16), shape((2, 1024, WIDTH), bf16)],
        [held, held, pltpu.VMEM((HDIM, 1024), f32)],
        (flags, q, k, v, grad, log_sum, dq, delta, after),
    )


def finish(place, own, near, far, after):
    return call(
        finish_kernel, "key_value_sum", (HEADS,),
        [head_pair(1024)] * 2 + [head_pair(512), ANY],
        [head(1024), head(1024)],
        [shape((1024, WIDTH), bf16)] * 2,
        [], (place, own, near, far, after),
    )


def pack_kernel(place, k_ref, v_ref, second_ref, held_ref):
    held_ref[...] = k_ref[...]

    @pl.when(pl.program_id(0) == 1)
    def _():
        second_ref[0] = k_ref[...]
        second_ref[1] = v_ref[...]


def pack(place, k, v):
    block = pl.BlockSpec((BLK, WIDTH), lambda i, place: (i, 0))
    return call(
        pack_kernel, "second_blocks", (2,),
        [block, pl.BlockSpec((BLK, WIDTH), lambda i, place: (1, 0))],
        [pl.BlockSpec((2, BLK, WIDTH), lambda i, place: (0, 0, 0)), block],
        [shape((2, BLK, WIDTH), bf16), shape(k.shape, bf16)], [], (place, k, v),
    )


def nothing_kernel(*refs):
    pass


def together(values, after=()):
    return pl.pallas_call(
        nothing_kernel,
        in_specs=[ANY] * (len(values) + len(after)),
        out_specs=[ANY] * len(values),
        out_shape=[shape(value.shape, value.dtype) for value in values],
        input_output_aliases={index: index for index in range(len(values))},
        compiler_params=pltpu.CompilerParams(vmem_limit_bytes=64 << 20),
        name="order",
    )(*values, *after)


def grad_kernel(place, a_ref, b_ref, wa_ref, wb_ref, *rest):
    total = dot(a_ref[...], wa_ref[...], NT) + dot(b_ref[...], wb_ref[...], NT)
    if len(rest) == 3:
        total += rest[0][...]
    rest[-1][...] = total.astype(rest[-1].dtype)


def grad_terms(place, first, a, b, weight, before, after):
    tile = 512
    row = pl.BlockSpec((tile, 1024), lambda i, place: (i, 0))
    result = pl.BlockSpec((tile, 512), lambda i, place: (i, 0))

    def columns(flip):
        return pl.BlockSpec((512, 1024), lambda i, place: (0, place[0] ^ flip))

    more = [] if before is None else [before]
    return call(
        grad_kernel, "projection_backward", (1024 // tile,),
        [row, row, columns(first), columns(first + 1)] + [result] * len(more) + [ANY], result,
        shape((1024, 512), bf16 if more else f32), [], (place, a, b, weight, weight, *more, after),
    )


def weight_kernel(place, turned_ref, g0, g1, g2, g3, after, *outs):
    owner = place[0] ^ pl.program_id(0)
    y = owner % 2 * 2 + pl.program_id(1)
    for part, ref in enumerate((g0, g1, g2, g3)):
        for slot, out_ref in enumerate(outs):

            @pl.when((pl.program_id(0) == part) & ((y - place[1] + 3) % 4 == slot))
            def _(ref=ref, out_ref=out_ref, part=part):
                out_ref[part // 2] = dot(turned_ref[...], ref[...], NN).astype(bf16)


def weight_terms(place, turned, cotangents, after):
    def piece(part):
        return pl.BlockSpec(
            (1024, 512),
            lambda i, half, place: (
                0, jnp.where(i == part, half, jnp.where(i < part, 0, 1)),
            ),
        )

    return call(
        weight_kernel, "weight_gradient", (4, 2),
        [pl.BlockSpec((512, 1024), lambda i, half, place: (0, 0))] + [piece(p) for p in range(4)]
        + [ANY],
        [pl.BlockSpec((2, 512, 512), lambda i, half, place: (0, 0, 0))] * 4,
        [shape((2, 512, 512), bf16)] * 4, [], (place, turned, *cotangents, after),
    )


def over_y(parts):
    return [to_y(parts[s], s + 1) for s in (1, 0, 2)]


def pieces_kernel(place, a, b, c, d, after, *outs):
    for slot, out_ref in enumerate(outs):

        @pl.when(pl.program_id(0) == slot)
        def _(out_ref=out_ref):
            out_ref[...] = sum(ref[...].astype(f32) for ref in (a, b, c, d)).astype(bf16)


def pieces_by_z(place, terms, after):
    piece = pl.BlockSpec((2, 512, 128), lambda i, place: (0, 0, (place[2] + i + 1) % 4))
    return call(
        pieces_kernel, "weight_by_z", (4,), [piece] * 4 + [ANY],
        [pl.BlockSpec((2, 512, 128), lambda i, place: (0, 0, 0))] * 4,
        [shape((2, 512, 128), bf16)] * 4, [], (place, *terms, after),
    )


def weight_z_kernel(place, a_ref, b_ref, c_ref, d_ref, after, kept_ref, sent_ref):
    def total(index):
        return sum(ref[index].astype(f32) for ref in (a_ref, b_ref, c_ref, d_ref))

    kept = place[3] ^ (place[0] // 2)
    kept_ref[...] = total(kept)
    sent_ref[...] = total(1 - kept).astype(bf16)


def weight_z_sum(place, terms, after):
    whole = pl.BlockSpec((2, 512, 128), lambda i, place: (0, 0, 0))
    result = pl.BlockSpec((512, 128), lambda i, place: (0, 0))
    return call(
        weight_z_kernel, "weight_z_sum", (1,), [whole] * 4 + [ANY], [result] * 2,
        [shape((512, 128), f32), shape((512, 128), bf16)], [], (place, *terms, after),
    )


def copy_kernel(place, in_ref, *refs):
    refs[-1][...] = in_ref[...]


def far_columns(place, weight, after):
    return call(
        copy_kernel, "projection_far", (2,),
        [pl.BlockSpec((256, 2048), lambda i, place: (i, 1 - place[0] // 2)), ANY],
        pl.BlockSpec((256, 2048), lambda i, place: (i, 0)),
        shape((512, 2048), bf16), [], (place, weight, after),
    )


def core_kernel(place, own_ref, far_ref, far_rows, own_rows, after, out_ref):
    out_ref[0] = own_ref[...]
    out_ref[1] = far_ref[...]
    for part, rows in ((2, far_rows), (3, own_rows)):
        for half in range(2):
            out_ref[part, :, block_rows(half)] = rows[block_rows(half), :]


def for_core(place, weight, far_weight, far_attention, attention, after):
    rows = pl.BlockSpec((1024, 512), lambda i, place: (0, 0))
    return call(
        core_kernel, "for_core", (1,),
        [
            pl.BlockSpec((512, 1024), lambda i, place: (0, place[0] ^ 1)),
            pl.BlockSpec((512, 1024), lambda i, place: (0, 1 - place[0] % 2)),
            rows, rows, ANY,
        ],
        pl.BlockSpec((4, 512, 1024), lambda i, place: (0, 0, 0)),
        shape((4, 512, 1024), bf16), [],
        (place, weight, far_weight, far_attention, attention, after),
    )


def mix_kernel(place, own, core, far, far_core, w_own, w_far, w_core, after, out_ref):
    total = dot(own[...], w_own[...], NN) + dot(core[0], w_core[0], NN)
    total += dot(far[...], w_far[...], NN) + dot(far_core[0], w_core[1], NN)
    out_ref[...] = total.astype(bf16)


def mix(place, attention, far_attention, weight, far_weight, from_core, after):
    rows = pl.BlockSpec((512, 512), lambda i, place: (i, 0))
    return call(
        mix_kernel, "projection", (2,),
        [
            rows,
            pl.BlockSpec((1, 512, 512), lambda i, place: (3, 0, i)),
            rows,
            pl.BlockSpec((1, 512, 512), lambda i, place: (2, 0, i)),
            pl.BlockSpec((512, 1024), lambda i, place: (0, place[0])),
            pl.BlockSpec((512, 1024), lambda i, place: (0, place[0] % 2)),
            pl.BlockSpec((2, 512, 1024), lambda i, place: (0, 0, 0)),
            ANY,
        ],
        pl.BlockSpec((512, 1024), lambda i, place: (i, 0)),
        shape((1024, 1024), bf16), [],
        (place, attention, from_core, far_attention, from_core, weight, far_weight, from_core, after),
    )


def per_device(queries, keys, values, out_weight, out_grad, spans, pairs):
    ctx = lax.axis_index("ctx")
    tp = lax.axis_index("tp")
    place = jnp.stack([tp, ctx // 4 % 4, ctx % 4, ctx // 16]).astype(jnp.int32)

    far_grad = to_x_hi(out_grad)
    near_pairs = [(s, s + 1) for s in range(31) if s != EDGE]
    near_values = lax.ppermute(values, "ctx", near_pairs + [(EDGE, 0)])
    core_grad = to_core(out_grad)
    second, held_keys = pack(place, keys, values)
    far_moved = first_hop(second, 1)

    query_block = ctx * 2 + jnp.arange(2, dtype=jnp.int32)[:, None] + jnp.zeros((1, WIN), jnp.int32)
    key_block = query_block - jnp.arange(WIN, dtype=jnp.int32)[None, :]
    flags = block_rule(spans, pairs, query_block, key_block).astype(jnp.int32).reshape(-1)
    own_state = forward_own(flags, queries, keys, values, keys)
    far_weight = far_columns(place, out_weight, own_state[1])
    terms = grad_terms(place, 0, out_grad, core_grad, out_weight, None, far_weight)

    [far_moved] = together([far_moved], [terms])
    far = second_hop(far_moved, 1)
    near_values, held_keys = together([near_values, held_keys], [far_moved])
    near_keys = along_ctx(held_keys, 1)
    edge_values = lax.ppermute(near_values, "ctx", [(0, EDGE + 1)])
    near_keys, far, far_grad, edge_values, far_weight = together(
        [near_keys, far, far_grad, edge_values, far_weight], [far_moved]
    )

    far_core_grad = to_core(far_grad)
    far_weight = to_x_hi(far_weight)
    behind = (flags, queries, near_keys, near_values, edge_values, far)
    attention, turned, log_sum = forward_behind(*behind, own_state, far)
    [far_core_grad] = together([far_core_grad], [log_sum])
    far_attention = to_x_hi(attention)
    attn_grad = grad_terms(place, 2, far_grad, far_core_grad, out_weight, terms, far_core_grad)
    cotangents = (out_grad, core_grad, far_grad, far_core_grad)
    weight_parts = weight_terms(place, turned, cotangents, attn_grad)
    weight_moved = over_y(weight_parts)
    near_back, far_back, dq, delta = backward_behind(
        *behind, attention, attn_grad, log_sum, weight_parts[3]
    )
    far_back, far_weight = together([far_back, far_weight])
    query_grad, own = backward_own(
        flags, queries, keys, values, attn_grad, log_sum, dq, delta, delta
    )

    back_moved = first_hop(far_back, -1)
    [far_attention] = together([far_attention], [own])
    from_core = for_core(place, out_weight, far_weight, far_attention, attention, own)

    *weight_moved, near_back, back_moved, from_core = together(
        [*weight_moved, near_back, back_moved, from_core]
    )
    far_back = second_hop(back_moved, -1)
    near_back = along_ctx(near_back, -1)
    from_core = to_core(from_core)
    weight_pieces = pieces_by_z(place, [weight_parts[3], *weight_moved], weight_moved[0])
    weight_moved = [to_z(weight_pieces[s], s + 1) for s in (1, 0, 2)]
    mixed = mix(
        place, attention, far_attention, out_weight, far_weight, from_core, weight_pieces[3]
    )
    kept, sent = weight_z_sum(place, [weight_pieces[3], *weight_moved], mixed)
    key_grad, value_grad = finish(place, own, near_back, far_back, kept)
    [sent] = together([to_x_lo(sent)], [key_grad])
    weight_grad = kept + sent.astype(f32)
    return (mixed, query_grad, key_grad, value_grad, weight_grad)


def solution(mesh):
    placed = (
        P("ctx", "tp"),
        P("ctx", "tp"),
        P("ctx", "tp"),
        P("tp", None),
        P("ctx", "tp"),
        P(),
        P(),
    )
    return jax.shard_map(
        per_device,
        mesh=mesh,
        in_specs=placed,
        out_specs=(P("ctx", "tp"), P("ctx", "tp"), P("ctx", "tp"), P("ctx", "tp"), P("tp", "ctx")),
        check_vma=False,
    )
```
